32 devices in a mesh: batch: 16 (over z, y, x), mp: 2 (over core).
Axes of the slice: x: 2, y: 2, z: 4, core: 2. Of those that a mesh axis runs over, the one named last changes fastest.
Arguments:
- image_patches: bfloat16 [128, 50, 768], P('batch'), may hold values from -6 to 6
- text_rows: bfloat16 [128, 16, 768], P('batch'), may hold values from -6 to 6
- text_mask: int32 [128, 16], P('batch'), may hold values from 0 to 1, as said below
- image_qkv: bfloat16 [768, 3, 768], P(None, None, 'mp'), may hold values from -0.21875 to 0.21875
- image_out: bfloat16 [768, 768], P('mp'), may hold values from -0.875 to 0.875
- image_up: bfloat16 [768, 3072], P(None, 'mp'), may hold values from -0.21875 to 0.21875
- image_down: bfloat16 [3072, 768], P('mp'), may hold values from -0.109375 to 0.109375
- text_gain_one: float32 [768], replicated, may hold values from 0.5 to 1.5
- text_gain_two: float32 [768], replicated, may hold values from 0.5 to 1.5
- text_qkv: bfloat16 [768, 3, 768], P(None, None, 'mp'), may hold values from -0.21875 to 0.21875
- text_out: bfloat16 [768, 768], P('mp'), may hold values from -0.625 to 0.625
- text_up: bfloat16 [768, 3072], P(None, 'mp'), may hold values from -0.21875 to 0.21875
- text_down: bfloat16 [3072, 768], P('mp'), may hold values from -0.109375 to 0.109375
- text_proj: bfloat16 [768, 768], P(None, 'mp'), may hold values from -0.21875 to 0.21875
- log_temp: float32 [], replicated, may hold values from 3.5 to 4.2
Outputs:
- loss: float32 [], replicated
- grad_text_rows: float32 [128, 16, 768], P('batch')
- grad_gain_one: float32 [768], P('mp')
- grad_gain_two: float32 [768], P('mp')
- grad_qkv: float32 [768, 3, 768], P(None, None, 'mp')
- grad_out: float32 [768, 768], P('mp')
- grad_up: float32 [768, 3072], P(None, 'mp')
- grad_down: float32 [3072, 768], P('mp')
- grad_proj: float32 [768, 768], P(None, 'mp')
- grad_log_temp: float32 [], replicated
The draws below stay inside these ranges and needn't reach their ends.
Inputs may be any that keep to these rules, and one draw needn't show every extreme that they name: `text_mask`: each row holds ones on a prefix of 4 to 16 positions and zeros after it.
All inputs are finite; a program needn't handle non-finite values.
Results may differ from the reference program's by a relative error of at most 0.01.
Values sent between devices are 32-bit elements; how exact they have to be, the bound alone decides.
A program may use at most 128 MiB of HBM per device.

```python
import jax
import jax.numpy as jnp
from jax import lax

D = 768
FF = 3072
HEAD = 64
PATCHES = 50
LENGTH = 16
PAIRS_DEV = 8
PAIRS = 128


def draw_text_mask(key, part):
    key = jax.random.fold_in(key, 7)
    lengths = jax.random.randint(key, (PAIRS,), LENGTH // 4, LENGTH + 1)
    lengths = lengths.at[0].set(LENGTH)
    positions = jnp.arange(LENGTH, dtype=jnp.int32)
    return (positions[None, :] < lengths[:, None]).astype(jnp.int32)


def shard_levels(own_key, extent, pieces, low, largest):
    factor_of = 1.0
    for dim, parts in pieces:
        steps = jax.random.uniform(jax.random.fold_in(jax.random.fold_in(own_key, 6), dim), (parts,), jnp.float32, low / len(pieces), largest / len(pieces))
        factor_of = factor_of * jnp.repeat(jnp.exp(steps), extent[dim] // parts).reshape((-1,) + (1,) * (len(extent) - 1 - dim))
    return factor_of


def gaussian(key, extent, width, bound, pieces=(), kind=jnp.bfloat16):
    drawn = width * jax.random.normal(key, extent, jnp.float32)
    if pieces:
        drawn = drawn * shard_levels(key, extent, pieces, -0.22, 0.18)
    return jnp.clip(drawn, -bound, bound).astype(kind)


def setup_inputs(seed: int = 0) -> dict:
    streams_of = jax.random.split(jax.random.key(seed), 16)
    image_patches = gaussian(streams_of[0], (PAIRS, PATCHES, D), 1.0, 6.0, ((0, 16),))
    text_rows = gaussian(streams_of[1], (PAIRS, LENGTH, D), 1.0, 6.0, ((0, 16),))
    text_mask = draw_text_mask(jax.random.fold_in(streams_of[15], 71), 0)
    image_qkv = gaussian(streams_of[3], (D, 3, D), D ** -0.5, 0.21875, ((2, 2),))
    image_out = gaussian(streams_of[4], (D, D), (D // 16) ** -0.5, 0.875, ((0, 2),))
    image_up = gaussian(streams_of[5], (D, FF), D ** -0.5, 0.21875, ((1, 2),))
    image_down = gaussian(streams_of[6], (FF, D), FF ** -0.5, 0.109375, ((0, 2),))
    text_gain_one = jnp.clip(1.0 + 0.1 * jax.random.normal(streams_of[7], (D,), jnp.float32), 0.5, 1.5)
    text_gain_two = jnp.clip(1.0 + 0.1 * jax.random.normal(streams_of[8], (D,), jnp.float32), 0.5, 1.5)
    text_qkv = gaussian(streams_of[9], (D, 3, D), D ** -0.5, 0.21875, ((2, 2),))
    text_out = gaussian(streams_of[10], (D, D), (D // 8) ** -0.5, 0.625, ((0, 2),))
    text_up = gaussian(streams_of[11], (D, FF), D ** -0.5, 0.21875, ((1, 2),))
    text_down = gaussian(streams_of[12], (FF, D), FF ** -0.5, 0.109375, ((0, 2),))
    text_proj = gaussian(streams_of[13], (D, D), D ** -0.5, 0.21875, ((1, 2),))
    log_temp = jnp.clip(jax.random.uniform(streams_of[14], (), jnp.float32, 3.5, 4.2), 3.5, 4.2)
    return {"image_patches": image_patches, "text_rows": text_rows, "text_mask": text_mask, "image_qkv": image_qkv, "image_out": image_out, "image_up": image_up, "image_down": image_down, "text_gain_one": text_gain_one, "text_gain_two": text_gain_two, "text_qkv": text_qkv, "text_out": text_out, "text_up": text_up, "text_down": text_down, "text_proj": text_proj, "log_temp": log_temp}


@jax.custom_vjp
def low(v):
    return lax.optimization_barrier(v.astype(jnp.bfloat16)).astype(jnp.float32)

@jax.custom_vjp
def low_back(v):
    return v

def low_keep(v):
    return (low(v), None)

def low_pass(kept, grad):
    return (grad,)

def back_keep(v):
    return (v, None)

def back_low(kept, grad):
    return (low(grad),)
low.defvjp(low_keep, low_pass)
low_back.defvjp(back_keep, back_low)
LN_EPS = 1e-06
NORM_EPS = 1e-06

def product(form, left, right):
    return jnp.einsum(form, left, right, precision=lax.Precision.HIGHEST)

def layer_norm(rows):
    center = rows - lax.optimization_barrier(jnp.mean(rows, -1, keepdims=True))
    spread = lax.optimization_barrier(jnp.mean(center * center, -1, keepdims=True))
    return center * lax.rsqrt(spread + LN_EPS)

def unit_rows(rows):
    return rows * lax.rsqrt(lax.optimization_barrier(jnp.sum(rows * rows, -1, keepdims=True)) + NORM_EPS)

def block_forward(hidden, key_mask, gain_first, gain_second, w_qkv, w_out, w_up, w_down):
    pair_count, length, model_width = hidden.shape
    head_count = model_width // HEAD
    normed = low(layer_norm(hidden) * gain_first)
    packed = product('nsd,dcf->nscf', normed, w_qkv)
    queries = low_back(low(packed[:, :, 0])).reshape(pair_count, length, head_count, HEAD)
    key_rows = low_back(low(packed[:, :, 1])).reshape(pair_count, length, head_count, HEAD)
    value_rows = low_back(low(packed[:, :, 2])).reshape(pair_count, length, head_count, HEAD)
    scores = low_back(product('nqhe,nkhe->nhqk', queries, key_rows) * HEAD ** (-0.5))
    scores = jnp.where(key_mask[:, None, None, :], scores, -1000000000.0)
    row_top = lax.optimization_barrier(jnp.max(scores, -1, keepdims=True))
    raised = jnp.exp(scores - row_top)
    softmax_rows = low(raised / lax.optimization_barrier(jnp.sum(raised, -1, keepdims=True)))
    mixed_rows = low_back(low(product('nhqk,nkhe->nqhe', softmax_rows, value_rows)))
    mixed_rows = mixed_rows.reshape(pair_count, length, model_width)
    attended = low_back(product('nsf,fd->nsd', mixed_rows, w_out))
    first_sum = hidden + attended
    normed_two = low(layer_norm(first_sum) * gain_second)
    upward = low_back(product('nsd,df->nsf', normed_two, w_up))
    activated = low(jax.nn.gelu(upward, approximate=False))
    downward = low_back(product('nsf,fd->nsd', activated, w_down))
    return first_sum + downward

def row_lse(block, others, scale):
    logits = scale * product('pd,qd->pq', block, others)
    row_top = lax.optimization_barrier(jnp.max(logits, -1, keepdims=True))
    return (row_top + jnp.log(lax.optimization_barrier(jnp.sum(jnp.exp(logits - row_top), -1, keepdims=True))))[:, 0]

def reference(image_patches, text_rows, text_mask, image_qkv, image_out, image_up, image_down, text_gain_one, text_gain_two, text_qkv, text_out, text_up, text_down, text_proj, log_temp):
    image_weights = tuple((weight_item.astype(jnp.float32) for weight_item in (image_qkv, image_out, image_up, image_down)))
    patch_blocks = image_patches.astype(jnp.float32).reshape(-1, PAIRS_DEV, PATCHES, D)

    def image_block(patch_block):
        gains = jnp.ones((D,), patch_block.dtype)
        every_patch = jnp.ones(patch_block.shape[:2], dtype=bool)
        out_rows = block_forward(patch_block, every_patch, gains, gains, *image_weights)
        return unit_rows(lax.optimization_barrier(jnp.mean(out_rows, 1)))
    image_norm = lax.map(image_block, patch_blocks).reshape(-1, D)

    def text_loss(rows, gain_first, gain_second, w_qkv, w_out, w_up, w_down, w_proj, temp_log):
        row_blocks = rows.reshape(-1, PAIRS_DEV, LENGTH, D)
        mask_blocks = text_mask.reshape(-1, PAIRS_DEV, LENGTH)

        def text_block(paired):
            block_rows, block_mask = paired
            out_rows = block_forward(block_rows, block_mask > 0, gain_first, gain_second, w_qkv, w_out, w_up, w_down)
            mask_float = block_mask.astype(out_rows.dtype)
            pooled = lax.optimization_barrier(jnp.sum(out_rows * mask_float[:, :, None], 1)) / lax.optimization_barrier(jnp.sum(mask_float, 1, keepdims=True))
            return low_back(product('pd,df->pf', low(pooled), w_proj))
        embeds = lax.map(jax.checkpoint(text_block), (row_blocks, mask_blocks)).reshape(-1, D)
        text_norm = unit_rows(embeds)
        scale = jnp.exp(temp_log)

        def text_side(block):
            return row_lse(block, image_norm, scale)

        def image_side(block):
            return row_lse(block, text_norm, scale)
        text_lse = lax.map(jax.checkpoint(text_side), text_norm.reshape(-1, PAIRS_DEV, D)).reshape(-1)
        image_lse = lax.map(jax.checkpoint(image_side), image_norm.reshape(-1, PAIRS_DEV, D)).reshape(-1)
        diagonal = scale * jnp.sum(text_norm * image_norm)
        return (jnp.sum(text_lse) + jnp.sum(image_lse) - 2.0 * diagonal) / (2.0 * PAIRS)
    primals = (text_rows.astype(jnp.float32), text_gain_one.astype(jnp.float32), text_gain_two.astype(jnp.float32), text_qkv.astype(jnp.float32), text_out.astype(jnp.float32), text_up.astype(jnp.float32), text_down.astype(jnp.float32), text_proj.astype(jnp.float32), log_temp.astype(jnp.float32))
    loss, pullback = jax.vjp(text_loss, *primals)
    grads = pullback(jnp.ones_like(loss))
    return (loss, grads[0], grads[1], grads[2], grads[3], grads[4], grads[5], grads[6], grads[7], grads[8])
```

```python
import functools
import jax
import jax.numpy as jnp
from jax import lax
from jax.experimental import pallas as pl
from jax.experimental.pallas import tpu as pltpu
from jax.sharding import PartitionSpec as P

HEAD = 64
LN_EPS = 1e-06
NORM_EPS = 1e-06
HIGHEST = lax.Precision.HIGHEST
BF = jnp.bfloat16
F32 = jnp.float32
MIB = 2**20


def nn(a, b):
    return lax.dot_general(a, b, (((1,), (0,)), ((), ())), preferred_element_type=F32)


def nt(a, b):
    return lax.dot_general(a, b, (((1,), (1,)), ((), ())), preferred_element_type=F32)


def tn(a, b):
    return lax.dot_general(a, b, (((0,), (0,)), ((), ())), preferred_element_type=F32)


def normalize(rows):
    center = rows - jnp.mean(rows, -1, keepdims=True)
    inv = lax.rsqrt(jnp.mean(center * center, -1, keepdims=True) + LN_EPS)
    return center * inv, inv


def normalize_pull(grad, xhat, inv):
    return inv * (
        grad - jnp.mean(grad, -1, keepdims=True) - xhat * jnp.mean(grad * xhat, -1, keepdims=True)
    )


def two_heads(tile):
    first = lax.broadcasted_iota(jnp.int32, tile.shape, 1) < HEAD
    zero = jnp.zeros_like(tile)
    return jnp.concatenate([jnp.where(first, tile, zero), jnp.where(first, zero, tile)], 0)


def stack_heads(pair):
    half = pair.shape[1] // 2
    return jnp.concatenate([pair[:, :half], pair[:, half:]], 0)


def halves(values):
    high = values.astype(BF)
    return high, (values - high.astype(F32)).astype(BF)


SENTINEL = 1e30
SUB = 128
INSIDE = 128
CHUNK = 256


def text_kernel(
    x_ref, g1_ref, g2_ref, dmw_ref, dh_ref, qkv_h, out_h, up_h, oqkv_h, oout_h, oup_h,
    a1_ref, dqkv_ref, o_ref, dattn_ref, a2_ref, du_ref, gsum_ref, gain2_ref, rows_ref,
    qkv_s, p_s, h1_s, do_s, wqkv_ref, wout_ref, wup_ref, load_sem,
):
    step = pl.program_id(0)
    width = x_ref.shape[1]
    hidden = wup_ref.shape[1]
    pairs = gsum_ref.shape[0]
    g1 = g1_ref[...]
    g2 = g2_ref[...]
    half = width // 2
    tiles = half // 128
    length = SUB // 8

    def loads():
        pieces = []
        for g, h in enumerate((qkv_h, oqkv_h)):
            for k in range(3):
                at = (3 * g + k) * half
                pieces.append((h.at[k], wqkv_ref.at[:, at:at + half]))
        pieces += [(out_h, wout_ref.at[:half]), (oout_h, wout_ref.at[half:])]
        pieces += [(up_h, wup_ref.at[:, :hidden // 2]), (oup_h, wup_ref.at[:, hidden // 2:])]
        return [pltpu.make_async_copy(h, v, load_sem.at[i]) for i, (h, v) in enumerate(pieces)]

    @pl.when(step == 0)
    def _():
        for c in loads():
            c.start()

    x = x_ref[...]
    lane = lax.broadcasted_iota(jnp.int32, (CHUNK, 128), 0) + step * CHUNK
    idcol = jnp.where(x[:, :128] < 0.5 * SENTINEL, (lane // length).astype(F32), -1.0)
    x = jnp.where(x < 0.5 * SENTINEL, x, 0.0)
    xhat, _ = normalize(x)
    a1_ref[...] = (xhat * g1).astype(BF)

    @pl.when(step == 0)
    def _():
        for c in loads():
            c.wait()

    qkv_s[...] = nn(a1_ref[...], wqkv_ref[...]).astype(BF)
    masks = []
    for s in range(CHUNK // SUB):
        ids = idcol[s * SUB:(s + 1) * SUB, :]
        m = ids == ids.T
        masks.append((ids, ids.T, jnp.concatenate([m, m], 1)))

    def columns(group, kind, t):
        start = group * (3 * width // 2) + kind * (width // 2) + t * 128
        return slice(start, start + 128)

    for s in range(CHUNK // SUB):
        rows = slice(s * SUB, (s + 1) * SUB)
        for g in range(2):
            for t in range(tiles):
                q2 = qkv_s[rows, columns(g, 0, t)]
                k2 = qkv_s[rows, columns(g, 1, t)]
                v2 = qkv_s[rows, columns(g, 2, t)]
                st = nt(k2, two_heads(q2)) * HEAD ** (-0.5)
                st = jnp.where(masks[s][2], st, -1000000000.0)
                e = jnp.exp(st - jnp.max(st, 0, keepdims=True))
                p = e * (1.0 / jnp.sum(e, 0, keepdims=True))
                p_s[(s * 2 + g) * tiles + t] = p
                o = tn(stack_heads(p.astype(BF)), two_heads(v2))
                at = g * (width // 2) + t * 128
                o_ref[rows, at:at + 128] = o.astype(BF)
    h1 = x + nn(o_ref[...], wout_ref[...])
    h1_s[...] = h1
    xhat2, inv2 = normalize(h1)
    a2_ref[...] = (xhat2 * g2).astype(BF)

    lanes = lax.broadcasted_iota(jnp.int32, (CHUNK, 2 * pairs), 1)
    lanes = jnp.where(lanes < pairs, lanes, lanes - pairs).astype(F32)
    spread = (jnp.broadcast_to(idcol[:, :1], lanes.shape) == lanes).astype(BF)
    idrow = jnp.concatenate([m[1][:1] for m in masks], 1)
    subl = lax.broadcasted_iota(jnp.int32, (pairs, CHUNK), 0).astype(F32)
    gather = (jnp.broadcast_to(idrow, subl.shape) == subl).astype(BF)

    @pl.when(step == 0)
    def _():
        gsum_ref[...] = jnp.zeros_like(gsum_ref)
        gain2_ref[...] = jnp.zeros_like(gain2_ref)

    piece = 512
    da2 = None
    for j in range(hidden // piece):
        cols = slice(j * piece, (j + 1) * piece)
        u = nn(a2_ref[...], wup_ref[:, cols])
        cdf = 0.5 + 0.5 * lax.erf(u * 0.5 ** 0.5)
        g = (u * cdf).astype(BF)
        slope = cdf + u * (jnp.exp(-0.5 * u * u) * 0.3989422804014327)
        gsum_ref[:, cols] += nn(gather, g)
        du = (nn(spread, dmw_ref[:, cols]) * slope).astype(BF)
        du_ref[:, cols] = du
        part = nt(du, wup_ref[:, cols])
        da2 = part if da2 is None else da2 + part
    xhat2, inv2 = normalize(h1_s[...])
    gain2_ref[...] += jnp.sum(da2 * xhat2, 0, keepdims=True)
    dh1 = nn(spread, dh_ref[...]) + normalize_pull(da2 * g2, xhat2, inv2)
    dattn_ref[...] = dh1.astype(BF)
    do_s[...] = nt(dattn_ref[...], wout_ref[...]).astype(BF)

    for s in range(CHUNK // SUB):
        rows = slice(s * SUB, (s + 1) * SUB)
        for g in range(2):
            for t in range(tiles):
                q2 = qkv_s[rows, columns(g, 0, t)]
                k2 = qkv_s[rows, columns(g, 1, t)]
                v2 = qkv_s[rows, columns(g, 2, t)]
                at = g * (width // 2) + t * 128
                do2 = two_heads(do_s[rows, at:at + 128])
                dp = nt(v2, do2)
                p = p_s[(s * 2 + g) * tiles + t]
                ds = (p * (dp - jnp.sum(dp * p, 0, keepdims=True))).astype(BF)
                dqkv_ref[rows, columns(g, 2, t)] = nn(p.astype(BF), do2).astype(BF)
                dqkv_ref[rows, columns(g, 1, t)] = (
                    nn(ds, two_heads(q2)) * HEAD ** (-0.5)
                ).astype(BF)
                dqkv_ref[rows, columns(g, 0, t)] = (
                    tn(stack_heads(ds), two_heads(k2)) * HEAD ** (-0.5)
                ).astype(BF)

    @pl.when(step == 0)
    def _():
        own = rows_ref.shape[0]
        da1 = nt(dqkv_ref[:own, :], wqkv_ref[...])
        xhat, inv = normalize(x[:own])
        rows_ref[...] = dh1[:own] + normalize_pull(da1 * g1, xhat, inv)


def text_pass(x, group, g1, g2, dmw, dh, weights, own):
    width = x.shape[1]
    pairs = dh.shape[0] // 2
    hidden = dmw.shape[1]
    total = pairs * own[1]
    steps = total // CHUNK
    whole = lambda a: pl.BlockSpec(a.shape, lambda i: (0,) * len(a.shape), pipeline_mode=pl.Buffered(1))
    fixed = lambda *shape: pl.BlockSpec(shape, lambda i: (0,) * len(shape))
    block = lambda cols: pl.BlockSpec((CHUNK, cols), lambda i: (i, 0))
    hbm = pl.BlockSpec(memory_space=pl.ANY)
    tiles = width // 128
    shape = jax.ShapeDtypeStruct
    return pl.pallas_call(
        text_kernel,
        grid=(steps,),
        out_shape=(
            shape((total, width), BF), shape((total, 3 * width), BF), shape((total, width), BF),
            shape((total, width), BF), shape((total, width), BF), shape((total, hidden), BF),
            shape((pairs, hidden), F32), shape((1, width), F32), shape((own[0], width), F32),
        ),
        in_specs=[
            pl.BlockSpec((CHUNK, width), lambda i: (i + group * steps, 0)), whole(g1), whole(g2), whole(dmw), whole(dh),
        ] + [hbm] * 6,
        out_specs=(
            block(width), block(3 * width), block(width), block(width), block(width), block(hidden),
            fixed(pairs, hidden), fixed(1, width), fixed(own[0], width),
        ),
        scratch_shapes=[
            pltpu.VMEM((CHUNK, 3 * width), BF),
            pltpu.VMEM((CHUNK // SUB * tiles, SUB, 2 * SUB), F32),
            pltpu.VMEM((CHUNK, width), F32),
            pltpu.VMEM((CHUNK, width), BF),
            pltpu.VMEM((width, 3 * width), BF),
            pltpu.VMEM((width, width), BF),
            pltpu.VMEM((width, hidden), BF),
            pltpu.SemaphoreType.DMA((10,)),
        ],
        compiler_params=pltpu.CompilerParams(vmem_limit_bytes=56 * MIB),
        name="text_pass",
    )(x, g1, g2, dmw, dh, *weights)


def weight_kernel(a_ref, g_ref, *refs):
    refs[-1][...] = tn(a_ref[...], g_ref[...]) if len(refs) == 1 else refs[0][...] + tn(a_ref[...], g_ref[...])


def weight_grad(a, a_at, a_cols, g, g_at, g_cols, tile, name, init=None):
    total = a.shape[0]
    out_spec = pl.BlockSpec((a_cols, tile), lambda i: (0, i))
    return pl.pallas_call(
        weight_kernel,
        grid=(g_cols // tile,),
        out_shape=jax.ShapeDtypeStruct((a_cols, g_cols), F32),
        in_specs=[
            pl.BlockSpec((total, a_cols), lambda i: (0, a_at // a_cols)),
            pl.BlockSpec((total, tile), lambda i: (0, g_at // tile + i)),
        ] + ([] if init is None else [out_spec]),
        out_specs=out_spec,
        input_output_aliases={} if init is None else {2: 0},
        compiler_params=pltpu.CompilerParams(vmem_limit_bytes=56 * MIB),
        name=name,
    )(a, g, *(() if init is None else (init,)))


MESH = pl.DeviceIdType.MESH


def chip_grid(mesh):
    chips = mesh.devices.reshape(-1, mesh.shape["mp"])[:, 0]
    places = [getattr(d, "coords", None) for d in chips]
    if all(p is not None and len(p) == 3 for p in places):
        grid = tuple(len({p[i] for p in places}) for i in (2, 1, 0))
        if grid[0] * grid[1] * grid[2] == len(chips):
            return grid
    side = 1
    while (2 * side) ** 3 <= len(chips):
        side *= 2
    return (len(chips) // (side * side), side, side)


class Spread:
    def __init__(self, grid, place, core, block, send, recv, first):
        self.grid, self.place, self.core = grid, place, core
        self.block, self.send, self.recv = block, send, recv
        self.first = first
        self.sent = []
        zs, ys, xs = grid
        self.turn = ys == xs
        near = []
        for d in range(1, zs // 2 + 1):
            near += [d] if 2 * d == zs else [d, zs - d]
        self.zorder = near
        self.aorder = list(range(1, ys))
        self.border = list(range(1, xs))
        self.pending = [("z", k) for k in near]
        self.pending += [("a", a, k) for a in self.aorder for k in [0] + near]

    def slot(self, kz, ka, kb):
        zs, ys, xs = self.grid
        plain = (kz * ys + ka) * xs + kb
        if not self.turn:
            return plain
        other = (kz * ys + kb) * xs + ka
        return plain if plain == other else plain + self.core * (other - plain)

    def target(self, dz, da, db):
        zs, ys, xs = self.grid
        z, y, x = self.place
        if self.turn and da != db:
            dy = da + self.core * (db - da)
            dx = db + self.core * (da - db)
        else:
            dy, dx = da, db
        batch = (lax.rem(z + dz, zs) * ys + lax.rem(y + dy, ys)) * xs + lax.rem(x + dx, xs)
        return (batch, self.core)

    def copy(self, source, landing, to):
        index = len(self.sent)
        sent = pltpu.make_async_remote_copy(
            src_ref=source, dst_ref=self.block(landing), send_sem=self.send.at[index],
            recv_sem=self.recv.at[landing], device_id=to, device_id_type=MESH,
        )
        sent.start()
        self.sent.append(sent)

    def along_a(self, source, kz):
        ys = self.grid[1]
        for d in self.aorder:
            self.copy(source, self.slot(kz, ys - d, 0), self.target(0, d, 0))

    def along_b(self, source, kz, ka):
        xs = self.grid[2]
        for d in self.border:
            self.copy(source, self.slot(kz, ka, xs - d), self.target(0, 0, d))

    def start(self):
        zs = self.grid[0]
        self.along_b(self.first, 0, 0)
        self.along_a(self.first, 0)
        for d in self.zorder:
            self.copy(self.first, self.slot(zs - d, 0, 0), self.target(d, 0, 0))

    def arrive(self, slot):
        pltpu.make_async_remote_copy(
            src_ref=self.block(slot), dst_ref=self.block(slot), send_sem=self.send.at[0],
            recv_sem=self.recv.at[slot], device_id=self.target(1, 0, 0), device_id_type=MESH,
        ).wait_recv()

    def serve(self, count=1):
        for _ in range(min(count, len(self.pending))):
            event = self.pending.pop(0)
            if event[0] == "z":
                slot = self.slot(event[1], 0, 0)
                self.arrive(slot)
                self.along_b(self.block(slot), event[1], 0)
                self.along_a(self.block(slot), event[1])
            else:
                slot = self.slot(event[2], event[1], 0)
                self.arrive(slot)
                self.along_b(self.block(slot), event[2], event[1])

    def finish(self):
        self.serve(len(self.pending))
        for a in [0] + self.aorder:
            for b in self.border:
                for k in [0] + self.zorder:
                    self.arrive(self.slot(k, a, b))
        for sent in self.sent:
            sent.wait_send()

    @staticmethod
    def copies(grid):
        zs, ys, xs = grid
        return (zs - 1) + zs * (ys - 1) + zs * ys * (xs - 1)


def attend(qkv_ref, o_ref, start, ids, half, both):
    m = ids == ids.T
    m = jnp.concatenate([m, m], 1)
    rows = pl.ds(start, SUB)
    for t in range(half // 128):
        q2 = qkv_ref[rows, t * 128:(t + 1) * 128]
        k2 = qkv_ref[rows, half + t * 128:half + (t + 1) * 128]
        v2 = qkv_ref[rows, 2 * half + t * 128:2 * half + (t + 1) * 128]
        st = nt(k2, two_heads(q2)) * HEAD ** (-0.5)
        st = jnp.where(m, st, -1000000000.0)
        e = jnp.exp(st - jnp.max(st, 0, keepdims=True))
        p = e * (1.0 / jnp.sum(e, 0, keepdims=True))
        o_ref[rows, t * 128:(t + 1) * 128] = tn(stack_heads(p.astype(BF)), two_heads(v2)).astype(BF)


def front_kernel(
    grid,
    rows_ref, mask_ref, image_ref, g1_ref, g2_ref, temp_ref,
    iqkv_h, iout_h, iup_h, idown_h, tqkv_h, tout_h, tup_h, tdown_h, tproj_h,
    xg_ref, oqkv_h, oout_h, oup_h, dmw_ref, dh_ref, dm_ref, low_ref, gh_ref, scal_ref,
    iqkv, iout, iup, idown, tqkv, tout, tup, tdown, proj,
    own_x, small, small_abs, payload, qkv_s, o_s, image_x, part, part_in, sums, sums_in,
    wsend_qkv, wsend_out, wsend_up, wsend_proj, wland_qkv, wland_out, wland_up, wland_proj,
    dmw_send, dmw_in, cos_s, tnorm_s,
    load_sem, out_sem, x_send, x_recv, s_send, s_recv, c_send, c_recv, own_sem,
):
    zs, ys, xs = grid
    chips = zs * ys * xs
    batch, core = lax.axis_index("batch"), lax.axis_index("mp")
    place = (batch // (ys * xs), lax.rem(batch // xs, ys), lax.rem(batch, xs))
    partner = (batch, 1 - core)
    pairs, length = mask_ref.shape
    rows = pairs * length
    width = rows_ref.shape[1]
    half = width // 2
    hidden = tup.shape[1]
    hp = pairs // 2
    hr = hp * length
    total = chips * pairs
    mine = chips * hp
    patches = image_ref.shape[0] // pairs
    padded = image_x.shape[0] // pairs

    inside = total <= INSIDE

    loads = []
    for i, (h, v) in enumerate((
        (tqkv_h, tqkv), (iqkv_h, iqkv), (iout_h, iout), (tout_h, tout), (tup_h, tup), (iup_h, iup), (idown_h, idown),
        (tdown_h, tdown), (tproj_h, proj.at[0]),
    )):
        v = v if h is not tproj_h else proj.at[core]
        loads.append(pltpu.make_async_copy(h, v, load_sem.at[i]))
        loads[-1].start()

    gather = Spread(grid, place, core, lambda s: xg_ref.at[s], x_send, x_recv, own_x)
    peers = [partner]
    peers += [gather.target(d, 0, 0) for d in range(1, zs)]
    peers += [gather.target(0, d, 0) for d in range(1, ys)]
    peers += [gather.target(0, 0, d) for d in range(1, xs)]
    barrier = pltpu.get_barrier_semaphore()
    for peer in peers:
        pl.semaphore_signal(barrier, inc=1, device_id=peer, device_id_type=MESH)

    mask = mask_ref[...].astype(F32)
    lane = lax.broadcasted_iota(jnp.int32, (rows, length), 1)
    sub = lax.broadcasted_iota(jnp.int32, (rows, length), 0)
    spread_mask = jnp.broadcast_to(mask[:, None, :], (pairs, length, length)).reshape(rows, length)
    valid = jnp.sum(jnp.where(lane == lax.rem(sub, length), spread_mask, 0.0), 1, keepdims=True)
    text_x = rows_ref[...].astype(F32)
    marked = jnp.where(valid > 0, text_x, SENTINEL)
    own_x[...] = jnp.where(core == 0, marked[:hr], marked[hr:])
    pl.semaphore_wait(barrier, len(peers))
    gather.start()
    own_copy = pltpu.make_async_copy(own_x, xg_ref.at[0], own_sem)
    own_copy.start()

    g1, g2 = g1_ref[...], g2_ref[...]
    a1 = (normalize(text_x)[0] * g1).astype(BF)
    loads[0].wait()
    for k in range(3):
        qkv_s[:rows, k * half:(k + 1) * half] = nn(a1, tqkv[k]).astype(BF)
    pair_of = (lax.broadcasted_iota(jnp.int32, (rows, 128), 0) // length).astype(F32)
    attend(qkv_s, o_s, 0, jnp.where(valid > 0, pair_of, -1.0), half, None)
    loads[3].wait()
    top = padded * pairs
    part[top:, :] = nn(o_s[:rows, :], tout[...])

    def swap(source, landing, index):
        c = pltpu.make_async_remote_copy(
            src_ref=source, dst_ref=landing, send_sem=c_send.at[index], recv_sem=c_recv.at[index],
            device_id=partner, device_id_type=MESH,
        )
        c.start()
        return c

    def contrast():
        for s in range(chips):
            kz, ky, kx = s // (ys * xs), s // xs % ys, s % xs
            at = (lax.rem(place[0] + kz, zs) * ys + lax.rem(place[1] + ky, ys)) * xs + lax.rem(place[2] + kx, xs)
            small_abs[:, at] = small[:, s]
        low = small_abs[0, :, :, :width].reshape(total, width).astype(BF)
        low_ref[...] = low
        counts = small_abs[0, :, :, width:].reshape(total, 128)[:, :1]
        embed = jnp.concatenate([nn(low, proj[0]), nn(low, proj[1])], 1)
        inv = lax.rsqrt(jnp.sum(embed * embed, 1, keepdims=True) + NORM_EPS)
        tnorm_s[...] = embed * inv
        images = small_abs[1, :, :, :width].reshape(total, width)
        scale = jnp.exp(jnp.full((1, 1), temp_ref[0, 0], F32))
        cos_s[...] = lax.dot_general(
            tnorm_s[...], images, (((1,), (1,)), ((), ())), precision=HIGHEST, preferred_element_type=F32
        )
        logits = cos_s[...] * scale
        row_top = jnp.max(logits, 1, keepdims=True)
        row_lse = row_top + jnp.log(jnp.sum(jnp.exp(logits - row_top), 1, keepdims=True))
        col_top = jnp.max(logits, 0, keepdims=True)
        col_lse = col_top + jnp.log(jnp.sum(jnp.exp(logits - col_top), 0, keepdims=True))
        eye = (lax.broadcasted_iota(jnp.int32, (total, total), 0) == lax.broadcasted_iota(jnp.int32, (total, total), 1))
        eye = eye.astype(F32)
        pair_grad = (jnp.exp(logits - row_lse) + jnp.exp(logits - col_lse) - 2.0 * eye) * (0.5 / total)

        def everything(v):
            return jnp.sum(jnp.sum(v, 1, keepdims=True), 0, keepdims=True)

        loss = (everything(row_lse) + everything(col_lse) - 2.0 * everything(logits * eye)) * (0.5 / total)
        temp = scale * everything(pair_grad * cos_s[...])
        lane = lax.broadcasted_iota(jnp.int32, (8, 128), 1)
        scal_ref[...] = jnp.where(lane == 0, loss, temp)
        grad_norm = scale * lax.dot_general(
            pair_grad, images, (((1,), (0,)), ((), ())), precision=HIGHEST, preferred_element_type=F32
        )
        tnorm = tnorm_s[...]
        grad_embed = ((grad_norm - tnorm * jnp.sum(tnorm * grad_norm, 1, keepdims=True)) * inv).astype(BF)
        gh_ref[...] = jnp.where(core == 0, grad_embed[:, :half], grad_embed[:, half:])
        dh = (nt(grad_embed[:, :half], proj[0]) + nt(grad_embed[:, half:], proj[1])) / counts
        dm = dh.astype(BF)

        r = lax.broadcasted_iota(jnp.int32, (total, total), 0)
        owner = jnp.where(r < mine, core, 1 - core)
        r = lax.rem(r, mine)
        k, i = r // hp, lax.rem(r, hp)
        at = (lax.rem(place[0] + k // (ys * xs), zs) * ys + lax.rem(place[1] + lax.rem(k // xs, ys), ys)) * xs
        at = at + lax.rem(place[2] + lax.rem(k, xs), xs)
        pick = (at * pairs + owner * hp + i == lax.broadcasted_iota(jnp.int32, (total, total), 1)).astype(BF)
        dm_sorted = nn(pick, dm).astype(BF)
        dm_ref[...] = dm_sorted
        dmw = nt(dm_sorted, tdown[...])
        dmw_send[...] = dmw[mine:]
        dmw_swap = swap(dmw_send, dmw_in, 8)
        dh_high, dh_low = halves(dh)
        dh_ref[:mine, :] = nn(pick[:mine], dh_high).astype(BF)
        dh_ref[mine:, :] = nn(pick[:mine], dh_low).astype(BF)
        dmw_high, dmw_low = halves(dmw[:mine])
        dmw_ref[:mine, :hidden] = dmw_high
        dmw_ref[mine:, :hidden] = dmw_low
        return dmw_swap

    swaps = []
    text_swap = swap(part.at[pl.ds(top, rows)], part_in.at[pl.ds(top, rows)], 0)
    swaps.append(text_swap)

    r = lax.broadcasted_iota(jnp.int32, (padded * pairs, patches * pairs), 0)
    c = lax.broadcasted_iota(jnp.int32, (padded * pairs, patches * pairs), 1)
    place_of = lax.rem(r, padded) * pairs + r // padded
    reorder = jnp.where((place_of == c) & (lax.rem(r, padded) < patches), 1.0, 0.0).astype(BF)
    image_x[...] = nn(reorder, image_ref[...])
    a1 = normalize(image_x[...])[0].astype(BF)
    loads[1].wait()
    for k in range(3):
        qkv_s[:, k * half:(k + 1) * half] = nn(a1, iqkv[k]).astype(BF)
    gather.serve(1)
    for s in range(padded * pairs // SUB):
        r = lax.broadcasted_iota(jnp.int32, (SUB, 128), 0) + s * SUB
        ids = jnp.where(lax.rem(r, padded) < patches, (r // padded).astype(F32), -1.0)
        attend(qkv_s, o_s, s * SUB, ids, half, None)
        if s % 2 == 1:
            gather.serve(1)
    loads[2].wait()
    part[:top, :] = nn(o_s[...], iout[...])
    image_swap = swap(part.at[pl.ds(0, top)], part_in.at[pl.ds(0, top)], 1)
    swaps.append(image_swap)
    gather.serve(1)

    for k in range(3):
        wsend_qkv[k] = tqkv[k].astype(F32)
    wsend_out[...] = tout[...].astype(F32)
    loads[4].wait()
    wsend_up[...] = tup[...].astype(F32)
    loads[8].wait()
    wsend_proj[...] = proj[core].astype(F32)

    text_swap.wait_recv()
    h1 = text_x + (part[top:, :] + part_in[top:, :])
    a2 = (normalize(h1)[0] * g2).astype(BF)
    mean_h = jnp.sum((h1 * valid).reshape(pairs, length, width), 1)
    piece = 512
    bars = []
    for j in range(hidden // piece):
        u = nn(a2, tup[:, j * piece:(j + 1) * piece])
        g = (u * (0.5 + 0.5 * lax.erf(u * 0.5 ** 0.5))).astype(BF).astype(F32) * valid
        bars.append(jnp.sum(g.reshape(pairs, length, piece), 1))
    bar = jnp.concatenate(halves(jnp.concatenate(bars, 1)), 0)
    loads[7].wait()
    low = nn(bar, tdown[...])
    text_sum = low[:pairs] + low[pairs:]
    sums[:pairs, :] = text_sum

    image_swap.wait_recv()
    proj_swap = swap(wsend_proj, wland_proj, 2)
    qkv_swap = swap(wsend_qkv, wland_qkv, 3)
    out_swap = swap(wsend_out, wland_out, 4)
    up_swap = swap(wsend_up, wland_up, 5)
    swaps += [proj_swap, qkv_swap, out_swap, up_swap]
    image_x[...] += part[:top, :] + part_in[:top, :]
    a2 = normalize(image_x[...])[0].astype(BF)
    mean_i = jnp.sum(image_x[...].reshape(pairs, padded, width), 1)
    loads[5].wait()
    bars = []
    for j in range(hidden // piece):
        u = nn(a2, iup[:, j * piece:(j + 1) * piece])
        g = (u * (0.5 + 0.5 * lax.erf(u * 0.5 ** 0.5))).astype(BF).astype(F32)
        bars.append(jnp.sum(g.reshape(pairs, padded, piece), 1))
        gather.serve(1)
    bar = jnp.concatenate(halves(jnp.concatenate(bars, 1)), 0)
    loads[6].wait()
    low = nn(bar, idown[...])
    sums[pairs:, :] = low[:pairs] + low[pairs:]
    sums_swap = swap(sums, sums_in, 6)
    swaps.append(sums_swap)
    gather.serve(1)
    sums_swap.wait_recv()
    count = jnp.sum(mask, 1, keepdims=True)
    pooled = (mean_h + (sums[:pairs, :] + sums_in[:pairs, :])) / count
    e = (mean_i + (sums[pairs:, :] + sums_in[pairs:, :])) * (1.0 / patches)
    image_norm = e * lax.rsqrt(jnp.sum(e * e, 1, keepdims=True) + NORM_EPS)
    payload[:, :width] = jnp.where(core == 0, pooled, image_norm)
    payload[:, width:] = jnp.broadcast_to(count, (pairs, 128))
    spread = Spread(grid, place, core, lambda s: small.at[core, s], s_send, s_recv, payload)
    spread.start()
    small[core, 0] = payload[...]
    gather.serve(1)
    spread.finish()
    both_swap = swap(small.at[core], small.at[core], 7)
    swaps.append(both_swap)
    gather.serve(len(gather.pending))
    both_swap.wait_recv()

    proj_swap.wait_recv()
    proj[1 - core] = wland_proj[...].astype(BF)
    if inside:
        dmw_swap = contrast()
        swaps.append(dmw_swap)
    else:
        dmw_ref[...] = small[...]
        dm_ref[...] = proj[...]

    oqkv, oout, oup = iqkv, iout, iup
    outs = []
    qkv_swap.wait_recv()
    for k in range(3):
        oqkv[k] = wland_qkv[k].astype(BF)
    outs.append(pltpu.make_async_copy(oqkv, oqkv_h, out_sem.at[0]))
    outs[-1].start()
    out_swap.wait_recv()
    oout[...] = wland_out[...].astype(BF)
    outs.append(pltpu.make_async_copy(oout, oout_h, out_sem.at[1]))
    outs[-1].start()
    up_swap.wait_recv()
    oup[...] = wland_up[...].astype(BF)
    outs.append(pltpu.make_async_copy(oup, oup_h, out_sem.at[2]))
    outs[-1].start()
    if inside:
        dmw_swap.wait_recv()
        dmw_high, dmw_low = halves(dmw_in[...])
        dmw_ref[:mine, hidden:] = dmw_high
        dmw_ref[mine:, hidden:] = dmw_low
    gather.finish()
    own_copy.wait()
    for s in swaps:
        s.wait_send()
    for o in outs:
        o.wait()


def front(grid, rows, mask, image, g1, g2, temp, weights):
    chips = grid[0] * grid[1] * grid[2]
    pairs, length = mask.shape
    width = rows.shape[1]
    half = width // 2
    iqkv, iout, iup, idown, tqkv, tout, tup, tdown, tproj = weights
    hidden = tup.shape[1]
    total = chips * pairs
    mine = total // 2
    patches = image.shape[0] // pairs
    padded = -(-patches // 64) * 64
    top = padded * pairs
    hr = pairs // 2 * length
    vmem = pl.BlockSpec(memory_space=pltpu.VMEM)
    hbm = pl.BlockSpec(memory_space=pl.ANY)
    shape = jax.ShapeDtypeStruct
    copies = Spread.copies(grid)
    inside = total <= INSIDE
    if inside:
        ends = (
            shape((2 * mine, 2 * hidden), BF), shape((2 * mine, width), BF), shape((total, width), BF),
            shape((total, width), BF), shape((total, half), BF), shape((8, 128), F32),
        )
    else:
        mine, total = 8, 128
        ends = (shape((2, chips, pairs, width + 128), F32),) + (shape((8, 128), F32),)
        ends += (shape((2,) + tproj.shape, BF),) + (shape((8, 128), F32),) * 3
    return pl.pallas_call(
        functools.partial(front_kernel, grid),
        out_shape=(
            shape((chips, hr, width), F32),
            shape(tqkv.shape, BF), shape(tout.shape, BF), shape(tup.shape, BF),
        ) + ends,
        in_specs=[vmem] * 5 + [pl.BlockSpec(memory_space=pltpu.SMEM)] + [hbm] * 9,
        out_specs=[hbm] * 4 + [vmem] * 6,
        scratch_shapes=[
            pltpu.VMEM(iqkv.shape, BF), pltpu.VMEM(iout.shape, BF), pltpu.VMEM(iup.shape, BF), pltpu.VMEM(idown.shape, BF),
            pltpu.VMEM(tqkv.shape, BF), pltpu.VMEM(tout.shape, BF), pltpu.VMEM(tup.shape, BF), pltpu.VMEM(tdown.shape, BF),
            pltpu.VMEM((2,) + tproj.shape, BF),
            pltpu.VMEM((hr, width), F32),
            pltpu.VMEM((2, chips, pairs, width + 128), F32),
            pltpu.VMEM((2, chips if inside else 1, pairs, width + 128), F32),
            pltpu.VMEM((pairs, width + 128), F32),
            pltpu.VMEM((top, 3 * half), BF),
            pltpu.VMEM((top, half), BF),
            pltpu.VMEM((top, width), F32),
            pltpu.VMEM((top + pairs * length, width), F32),
            pltpu.VMEM((top + pairs * length, width), F32),
            pltpu.VMEM((2 * pairs, width), F32),
            pltpu.VMEM((2 * pairs, width), F32),
            pltpu.VMEM(tqkv.shape, F32), pltpu.VMEM(tout.shape, F32), pltpu.VMEM(tup.shape, F32), pltpu.VMEM(tproj.shape, F32),
            pltpu.VMEM(tqkv.shape, F32), pltpu.VMEM(tout.shape, F32), pltpu.VMEM(tup.shape, F32), pltpu.VMEM(tproj.shape, F32),
            pltpu.VMEM((mine, hidden), F32), pltpu.VMEM((mine, hidden), F32),
            pltpu.VMEM((total, total), F32), pltpu.VMEM((total, width), F32),
            pltpu.SemaphoreType.DMA((9,)), pltpu.SemaphoreType.DMA((3,)),
            pltpu.SemaphoreType.DMA((copies,)), pltpu.SemaphoreType.DMA((chips,)),
            pltpu.SemaphoreType.DMA((copies,)), pltpu.SemaphoreType.DMA((chips,)),
            pltpu.SemaphoreType.DMA((9,)), pltpu.SemaphoreType.DMA((9,)), pltpu.SemaphoreType.DMA,
        ],
        compiler_params=pltpu.CompilerParams(collective_id=0, has_side_effects=True, vmem_limit_bytes=60 * MIB),
        name="front",
    )(rows, mask, image, g1, g2, temp, *weights)


def contrast_outside(grid, small, proj, log_temp, text_down):
    core = lax.axis_index("mp")
    here = lax.axis_index("batch")
    chips, pairs, width = small.shape[1], small.shape[2], small.shape[3] - 128
    half = width // 2
    zs, ys, xs = grid
    slots = jnp.arange(chips, dtype=jnp.int32)
    z, y, x = here // (ys * xs), here // xs % ys, here % xs
    offset = (z + slots // (ys * xs)) % zs * (ys * xs) + (y + slots // xs % ys) % ys * xs + (x + slots % xs) % xs
    slot_of = jnp.argsort(offset)
    ordered = small[:, slot_of].reshape(2, chips * pairs, width + 128)
    low = ordered[0, :, :width].astype(BF)
    counts = ordered[0, :, width:width + 1]
    images = ordered[1, :, :width]
    total = chips * pairs
    embed = jnp.concatenate([nn(low, proj[0]), nn(low, proj[1])], 1)
    inv = lax.rsqrt(jnp.sum(embed * embed, 1, keepdims=True) + NORM_EPS)
    text_norm = embed * inv
    scale = jnp.exp(log_temp)
    cosine = jnp.dot(text_norm, images.T, precision=HIGHEST, preferred_element_type=F32)
    logits = scale * cosine
    text_lse = jax.nn.logsumexp(logits, 1, keepdims=True)
    image_lse = jax.nn.logsumexp(logits, 0, keepdims=True)
    eye = jnp.eye(total, dtype=F32)
    pair_grad = (jnp.exp(logits - text_lse) + jnp.exp(logits - image_lse) - 2.0 * eye) / (2.0 * total)
    loss = (jnp.sum(text_lse) + jnp.sum(image_lse) - 2.0 * jnp.sum(logits * eye)) / (2.0 * total)
    temp = scale * jnp.sum(pair_grad * cosine)
    grad_norm = scale * jnp.dot(pair_grad, images, precision=HIGHEST, preferred_element_type=F32)
    grad_embed = ((grad_norm - text_norm * jnp.sum(text_norm * grad_norm, 1, keepdims=True)) * inv).astype(BF)
    grad_half = lax.dynamic_slice_in_dim(grad_embed, core * half, half, 1)
    dh = (nt(grad_embed[:, :half], proj[0]) + nt(grad_embed[:, half:], proj[1])) / counts
    hp = pairs // 2

    def mine(v, c):
        w = v.reshape(chips, 2, hp, v.shape[-1])[offset]
        return lax.dynamic_index_in_dim(w, c, 1, keepdims=False).reshape(total // 2, v.shape[-1])

    def grouped(v):
        high, rest = halves(v)
        size = INSIDE // 8
        both = jnp.stack([high.reshape(-1, size, v.shape[1]), rest.reshape(-1, size, v.shape[1])], 1)
        return both.reshape(-1, v.shape[1])

    dm = jnp.concatenate([mine(dh, core), mine(dh, 1 - core)], 0).astype(BF)
    dmw = nt(dm, text_down)
    dmw_other = lax.ppermute(dmw[total // 2:], "mp", [(0, 1), (1, 0)])
    dmw = grouped(jnp.concatenate([dmw[:total // 2], dmw_other], 1))
    return dmw, grouped(mine(dh, core)), dm, low, grad_half, jnp.stack([loss, temp]).reshape(1, 2)


def per_device(
    grid, image_patches, text_rows, text_mask, image_qkv, image_out, image_up, image_down, text_gain_one, text_gain_two,
    text_qkv, text_out, text_up, text_down, text_proj, log_temp,
):
    pair_count, length, width = text_rows.shape
    core = lax.axis_index("mp")
    swap = [(0, 1), (1, 0)]
    half = width // 2
    hidden = text_up.shape[1]
    patches = jnp.transpose(image_patches, (1, 0, 2)).reshape(-1, width)
    iqkv = jnp.transpose(image_qkv, (1, 0, 2))
    tqkv = jnp.transpose(text_qkv, (1, 0, 2))
    g1, g2 = text_gain_one[None], text_gain_two[None]
    xg, oqkv, oout, oup, dmw, dh, dm, low, grad_half, scal = front(
        grid, text_rows.reshape(-1, width), text_mask, patches, g1, g2, log_temp.reshape(1, 1),
        (iqkv, image_out, image_up, image_down, tqkv, text_out, text_up, text_down, text_proj),
    )
    own = pair_count // 2 * length
    if dm.ndim == 3:
        dmw, dh, dm, low, grad_half, scal = contrast_outside(grid, dmw, dm, log_temp, text_down)
    rows_x = xg.reshape(-1, width)
    group_pairs = dm.shape[0] // 2 if dm.shape[0] <= INSIDE else INSIDE // 8

    def group(x, dmw, dh, init):
        a1, dqkv, o, dattn, a2, du, gsum, gain2, rows = text_pass(
            x, 0, g1, g2, dmw, dh, (tqkv, text_out, text_up, oqkv, oout, oup), (own, length))
        sums = (
            weight_grad(a2, 0, width, du, hidden, hidden, 512, "up_other", init[0]),
            weight_grad(a1, 0, width, dqkv, 3 * half, 3 * half, 384, "qkv_other", init[1]),
            weight_grad(o, half, half, dattn, 0, width, 256, "out_other", init[2]),
            weight_grad(a2, 0, width, du, 0, hidden, 512, "up_own", init[3]),
            weight_grad(a1, 0, width, dqkv, 0, 3 * half, 384, "qkv_own", init[4]),
            weight_grad(o, 0, half, dattn, 0, width, 256, "out_own", init[5]),
        )
        return sums, gsum, gain2, rows

    groups = dm.shape[0] // 2 // group_pairs
    if groups == 1:
        sums, gsum, gain2, rows = group(rows_x, dmw, dh, (None,) * 6)
    else:
        def one(carry, items):
            sums, gain2, rows = carry
            g, x, dmw, dh = items
            sums, gsum, gain2_new, rows_new = group(x, dmw, dh, sums)
            return (sums, gain2 + gain2_new, jnp.where(g == 0, rows_new, rows)), gsum

        zeros = tuple(
            jnp.zeros(shape, F32)
            for shape in ((width, hidden), (width, 3 * half), (half, width)) * 2
        )
        split = lambda v: v.reshape(groups, -1, v.shape[-1])
        carry = (zeros, jnp.zeros((1, width), F32), jnp.zeros((own, width), F32))
        (sums, gain2, rows), gsum = lax.scan(
            one, carry, (jnp.arange(groups), split(rows_x), split(dmw), split(dh)))
        gsum = gsum.reshape(-1, gsum.shape[-1])
    up_o, qkv_o, out_o, up_m, qkv_m, out_m = sums
    grad_up = up_m + lax.ppermute(up_o, "mp", swap)
    grad_qkv = qkv_m + lax.ppermute(qkv_o, "mp", swap)
    grad_out = out_m + lax.ppermute(out_o, "mp", swap)
    rows_other, gain2_other, gsum_other = lax.ppermute((rows, gain2, gsum[:, hidden:]), "mp", swap)
    grad_rows = jnp.where(core == 0, jnp.concatenate([rows, rows_other], 0), jnp.concatenate([rows_other, rows], 0))
    gsums = jnp.concatenate([gsum[:, :hidden], gsum_other], 0)
    gh, gl = halves(gsums)
    grad_down = tn(gh, dm) + tn(gl, dm)
    grad_proj = tn(low, grad_half)
    gain1 = lax.psum(jnp.sum(grad_qkv * jnp.concatenate([tqkv[0], tqkv[1], tqkv[2]], 1).astype(F32), 1), "mp")
    gain1 = gain1 / text_gain_one
    gain2 = (gain2 + gain2_other)[0]
    part = lambda v: lax.dynamic_slice_in_dim(v, core * half, half, 0)
    return (scal[0, 0], grad_rows.reshape(pair_count, length, width), part(gain1), part(gain2),
            grad_qkv.reshape(width, 3, half), grad_out, grad_up, grad_down, grad_proj, scal[0, 1])


def solution(mesh):
    return jax.shard_map(
        functools.partial(per_device, chip_grid(mesh)),
        mesh=mesh,
        in_specs=(
            P("batch", None, None), P("batch", None, None), P("batch", None), P(None, None, "mp"), P("mp", None),
            P(None, "mp"), P("mp", None), P(), P(), P(None, None, "mp"), P("mp", None), P(None, "mp"), P("mp", None),
            P(None, "mp"), P(),
        ),
        out_specs=(
            P(), P("batch", None, None), P("mp"), P("mp"), P(None, None, "mp"), P("mp", None), P(None, "mp"),
            P("mp", None), P(None, "mp"), P(),
        ),
        check_vma=False,
    )
```

```python
import functools
import jax
import jax.numpy as jnp
from jax import lax
from jax.experimental import pallas as pl
from jax.experimental.pallas import tpu as pltpu
from jax.sharding import PartitionSpec as P

HEAD = 64
LN_EPS = 1e-06
NORM_EPS = 1e-06
HIGHEST = lax.Precision.HIGHEST
BF = jnp.bfloat16
F32 = jnp.float32
MIB = 2**20


def cost(microseconds):
    return pl.CostEstimate(flops=int(microseconds * 1e9), bytes_accessed=0, transcendentals=0)


def nn(a, b):
    return lax.dot_general(a, b, (((1,), (0,)), ((), ())), preferred_element_type=F32)


def nt(a, b):
    return lax.dot_general(a, b, (((1,), (1,)), ((), ())), preferred_element_type=F32)


def tn(a, b):
    return lax.dot_general(a, b, (((0,), (0,)), ((), ())), preferred_element_type=F32)


def normalize(rows):
    center = rows - jnp.mean(rows, -1, keepdims=True)
    inv = lax.rsqrt(jnp.mean(center * center, -1, keepdims=True) + LN_EPS)
    return center * inv, inv


def normalize_pull(grad, xhat, inv):
    return inv * (
        grad - jnp.mean(grad, -1, keepdims=True) - xhat * jnp.mean(grad * xhat, -1, keepdims=True)
    )


def two_heads(tile):
    first = lax.broadcasted_iota(jnp.int32, tile.shape, 1) < HEAD
    zero = jnp.zeros_like(tile)
    return jnp.concatenate([jnp.where(first, tile, zero), jnp.where(first, zero, tile)], 0)


def stack_heads(pair):
    half = pair.shape[1] // 2
    return jnp.concatenate([pair[:, :half], pair[:, half:]], 0)


def halves(values):
    high = values.astype(BF)
    return high, (values - high.astype(F32)).astype(BF)


SENTINEL = 1e30
SUB = 128
INSIDE = 128


def three(form, a, b):
    (ah, al), (bh, bl) = halves(a), halves(b)
    return form(ah, bh) + (form(ah, bl) + form(al, bh))


def parts_of(v, n):
    q = jnp.floor((v + 0.5) * (1.0 / n))
    return q, v - q * n


def count_down(rows, cols=128):
    return lax.broadcasted_iota(jnp.int32, (rows, cols), 0).astype(F32)


def count_along(rows, cols):
    return lax.broadcasted_iota(jnp.int32, (rows, cols), 1).astype(F32)


def widen(v, cols):
    return jnp.concatenate([v] * -(-cols // 128), 1)[:, :cols]


def layout(rows, groups):
    bins = rows // SUB
    main = rows if bins % 4 else rows * 3 // 4
    return main, lambda g: ((0, main, g * main), (main, rows - main, groups * main + g * (rows - main)))


def pack(x, length):
    rows = x.shape[0]
    valid = x[:, :128] < 0.5 * SENTINEL
    along = jnp.where(valid, 1.0, 0.0).T[:8]
    pair = parts_of(count_down(rows), length)[0]
    pair_down = widen(pair, rows)
    pair_along, place = parts_of(count_along(8, rows), length)
    row = jnp.broadcast_to(pair_along[:1], (rows, rows))
    count = nn(along.astype(BF), (pair_down == row).astype(BF))
    upto = nn(along.astype(BF), (pair_down <= row).astype(BF))
    base = jnp.zeros((8, 1), F32)
    at = upto - count
    for b in range(1, rows // SUB):
        new = jnp.max(jnp.where(upto <= base + SUB, upto, 0.0), 1, keepdims=True)
        at = jnp.where(upto > new, upto - count - new + b * SUB, at)
        base = new
    at = jnp.where(along > 0, at + place, -1.0)
    pick = (widen(count_down(rows), rows) == jnp.broadcast_to(at[:1], (rows, rows))).astype(BF)
    packed = nn(pick, jnp.where(x < 0.5 * SENTINEL, x, 0.0).astype(BF))
    return packed, nn(pick, (pair + 1.0).astype(BF)) - 1.0, pick, jnp.max(at)


def forward_kernel(length, group, groups, x_ref, g1_ref, g2_ref, dmw_ref, dh_ref, *refs):
    qkv_h, out_h, up_h, oqkv_h, oout_h, oup_h = refs[:6]
    refs = refs[6:]
    if group:
        gsumi_ref, gaini_ref, flagi_ref = refs[:3]
        refs = refs[12:]
    a1t_h, qkv_o, p_o, do_o, a2t_h, du_h, ot_h, dattn_h, dux_h, gsum_ref, gain_ref, flag_ref = refs[:12]
    refs = refs[12:]
    tail = group == groups - 1
    if tail:
        send_ref = refs[0]
        refs = refs[1:]
    if group == 0:
        own_ref, pick_ref = refs[:2]
        refs = refs[2:]
    (x_s, id_s, qkv_s, p_s, o_s, h1_s, da2_s, a2_s, do_s, a1t_s, a2t_s, ot_s, du_s, dattn_s, wqkv_s, wout_s, wup_s,
     load_sem, early_sem, keep_sem) = refs
    rows, width = x_ref.shape
    hidden = wup_s.shape[1]
    pairs = rows // length
    before = gsum_ref.shape[0] - pairs
    half = width // 2
    tiles = half // 128
    main, where = layout(rows, groups)
    g1 = g1_ref[...].reshape(1, width)
    g2 = g2_ref[...].reshape(1, width)

    pieces = []
    for g, h in enumerate((qkv_h, oqkv_h)):
        for k in range(3):
            at = (3 * g + k) * half
            pieces.append((h.at[k], wqkv_s.at[:, at:at + half]))
    pieces += [(out_h, wout_s.at[:half]), (oout_h, wout_s.at[half:])]
    pieces += [(up_h, wup_s.at[:, :hidden // 2]), (oup_h, wup_s.at[:, hidden // 2:])]
    loads = [pltpu.make_async_copy(h, v, load_sem.at[i]) for i, (h, v) in enumerate(pieces)]
    for c in loads:
        c.start()
    early = []
    if group and tail:
        mine, other = slice(0, hidden // 2), slice(hidden // 2, hidden)
        for g in range(group):
            for i, (_, size, at) in enumerate(where(g)):
                if size:
                    cut = slice(at, at + size)
                    for j, (h, v, index) in enumerate((
                        (a2t_h, a2t_s, (slice(None), cut)), (dux_h, du_s.at[:, other], (cut,)),
                        (ot_h, ot_s, (slice(None), cut)), (dattn_h, dattn_s, (cut,)),
                    )):
                        early.append(pltpu.make_async_copy(h.at[index], v.at[index], early_sem.at[8 * g + 4 * i + j]))
        for c in early:
            c.start()

    packed, ids, pick, top = pack(x_ref[...].astype(F32), length)
    x_s[...] = packed
    id_s[...] = ids
    more = top >= main
    flag_ref[0, 0] = jnp.where(more, 1, 0)
    gsum_ref[before:, :] = jnp.zeros((pairs, hidden), F32)
    gain_ref[...] = jnp.zeros_like(gain_ref)
    if group:
        gsum_ref[:before, :] = gsumi_ref[...]
        gain_ref[...] = gaini_ref[...]
    if group == 0:
        own = own_ref.shape[0]
        pick_ref[...] = jnp.zeros_like(pick_ref)
        pick_ref[:, :own] = pick[:own, :own]

    def columns(g, kind, t):
        start = g * 3 * half + kind * half + t * 128
        return slice(start, start + 128)

    def keeps(part):
        start, size, at = where(group)[part]
        src, dst = slice(start, start + size), slice(at, at + size)
        every = slice(None)
        return [
            pltpu.make_async_copy(v.at[i], h.at[j], keep_sem.at[9 * part + k])
            for k, (v, h, i, j) in enumerate((
                (a1t_s, a1t_h, (every, src), (every, dst)),
                (qkv_s, qkv_o, (src,), (dst,)),
                (p_s, p_o, (slice(start // SUB, (start + size) // SUB),), (slice(at // SUB, (at + size) // SUB),)),
                (a2t_s, a2t_h, (every, dst), (every, dst)),
                (ot_s, ot_h, (every, dst), (every, dst)),
                (du_s, du_h, (dst, slice(0, hidden // 2)), (dst,)),
                (dattn_s, dattn_h, (dst,), (dst,)),
                (do_s, do_o, (src,), (dst,)),
                (du_s, dux_h, (dst, slice(hidden // 2, hidden)), (dst,)),
            )[:8 if tail else 9])
        ]

    def work(part):
        start, size, at = where(group)[part]
        here, there = slice(start, start + size), slice(at, at + size)
        store = keeps(part)
        x = x_s[here, :]
        a1 = (normalize(x)[0] * g1).astype(BF)
        a1t_s[:, here] = a1.T
        store[0].start()
        if part == 0:
            for c in loads[:6]:
                c.wait()
        qkv_s[here, :] = nn(a1, wqkv_s[...]).astype(BF)
        store[1].start()
        down = id_s[here, :]
        along = id_s[here, :].T[:1]

        def bin_of(s, carry):
            cut = pl.ds(pl.multiple_of(start + s * SUB, SUB), SUB)
            m = id_s[cut, :] == id_s[cut, :].T
            m = jnp.concatenate([m, m], 1)
            for g in range(2):
                for t in range(tiles):
                    q2 = qkv_s[cut, columns(g, 0, t)]
                    k2 = qkv_s[cut, columns(g, 1, t)]
                    v2 = qkv_s[cut, columns(g, 2, t)]
                    st = nt(k2, two_heads(q2)) * HEAD ** (-0.5)
                    st = jnp.where(m, st, -1000000000.0)
                    e = jnp.exp(st - jnp.max(st, 0, keepdims=True))
                    p = (e * (1.0 / jnp.sum(e, 0, keepdims=True))).astype(BF)
                    p_s[start // SUB + s, g * tiles + t] = p
                    col = g * half + t * 128
                    o_s[cut, col:col + 128] = tn(stack_heads(p), two_heads(v2)).astype(BF)
            return carry

        lax.fori_loop(0, size // SUB, bin_of, 0)
        store[2].start()
        if part == 0:
            for c in loads[6:8]:
                c.wait()
        h1 = x + nn(o_s[here, :], wout_s[...])
        h1_s[here, :] = h1
        a2_s[here, :] = (normalize(h1)[0] * g2).astype(BF)
        ot_s[:, there] = o_s[here, :].T
        a2t_s[:, there] = a2_s[here, :].T
        store[3].start()
        store[4].start()

        lanes = lax.broadcasted_iota(jnp.int32, (size, 2 * pairs), 1)
        lanes = jnp.where(lanes < pairs, lanes, lanes - pairs).astype(F32)
        spread = (jnp.broadcast_to(down[:, :1], lanes.shape) == lanes).astype(BF)
        subl = lax.broadcasted_iota(jnp.int32, (pairs, size), 0).astype(F32)
        gather = (jnp.broadcast_to(along, subl.shape) == subl).astype(BF)
        piece = 1024
        if part == 0:
            for c in loads[8:]:
                c.wait()
        def feed(j, carry):
            cols = pl.ds(pl.multiple_of(j * piece, piece), piece)
            u = nn(a2_s[here, :], wup_s[:, cols])
            cdf = 0.5 + 0.5 * lax.erf(u * 0.5 ** 0.5)
            g = (u * cdf).astype(BF)
            slope = cdf + u * (jnp.exp(-0.5 * u * u) * 0.3989422804014327)
            gsum_ref[before:, cols] += nn(gather, g)
            du = (nn(spread, dmw_ref[:, cols]) * slope).astype(BF)
            du_s[there, cols] = du
            da2_s[:size, :] += nt(du, wup_s[:, cols])
            return carry

        da2_s[:size, :] = jnp.zeros((size, width), F32)
        lax.fori_loop(0, hidden // piece, feed, 0)
        da2 = da2_s[:size, :]
        store[5].start()
        if not tail:
            store[8].start()
        xhat2, inv2 = normalize(h1_s[here, :])
        gain_ref[:1, :] += jnp.sum(da2 * xhat2, 0, keepdims=True)
        dh1 = nn(spread, dh_ref[...]) + normalize_pull(da2 * g2, xhat2, inv2)
        dattn_s[there, :] = dh1.astype(BF)
        store[6].start()
        do_s[here, :] = nt(dattn_s[there, :], wout_s[...]).astype(BF)
        store[7].start()
        if group == 0 and part == 0:
            own_ref[...] = dh1[:own_ref.shape[0]]

    work(0)
    if main < rows:
        pl.when(more)(lambda: work(1))

        @pl.when(jnp.logical_not(more))
        def _():
            start, size, at = where(group)[1]
            a1t_s[:, start:] = jnp.zeros((width, size), BF)
            a2t_s[:, at:at + size] = jnp.zeros((width, size), BF)
            ot_s[:, at:at + size] = jnp.zeros((width, size), BF)
            du_s[at:at + size, :] = jnp.zeros((size, hidden), BF)
            dattn_s[at:at + size, :] = jnp.zeros((size, width), BF)
            for c in keeps(1):
                c.start()
    if tail:
        for c in early:
            c.wait()
        whole = groups * main
        out = nn(ot_s[half:, :whole], dattn_s[:whole, :])
        send_ref[:width, :] = nn(a2t_s[:, :whole], du_s[:whole, hidden // 2:])
        send_ref[width:width + half // 2, :width] = out[:half // 2]
        send_ref[width:width + half // 2, width:] = out[half // 2:]
        if main < rows:
            any_more = more
            if group:
                any_more = jnp.logical_or(more, flagi_ref[0, 0] > 0)

            @pl.when(any_more)
            def _():
                out = nn(ot_s[half:, whole:], dattn_s[whole:, :])
                send_ref[:width, :] += nn(a2t_s[:, whole:], du_s[whole:, hidden // 2:])
                send_ref[width:width + half // 2, :width] += out[:half // 2]
                send_ref[width:width + half // 2, width:] += out[half // 2:]
            flag_ref[0, 0] = jnp.where(any_more, 1, 0)
        count = gsum_ref.shape[0]
        at = width + half // 2
        send_ref[at:, :] = jnp.zeros((send_ref.shape[0] - at, hidden // 2), F32)
        send_ref[at:at + count, :] = gsum_ref[:, hidden // 2:]
        send_ref[at + count:at + count + 8, :width] = gain_ref[...]
    for part in range(2 if main < rows else 1):
        for c in keeps(part):
            c.wait()


def text_forward(x, length, g1, g2, dmw, dh, weights, own, groups=1, group=0, before=None):
    rows, width = x.shape
    pairs = rows // length
    hidden = dmw.shape[1]
    half = width // 2
    total = rows * groups
    tail = group == groups - 1
    count = (group + 1) * pairs
    units = width // 128
    bins = rows // SUB
    whole = lambda a: pl.BlockSpec(memory_space=pltpu.VMEM)
    vmem = pl.BlockSpec(memory_space=pltpu.VMEM)
    smem = pl.BlockSpec(memory_space=pltpu.SMEM)
    hbm = pl.BlockSpec(memory_space=pl.ANY)
    shape = jax.ShapeDtypeStruct
    at_group = lambda cols: pl.BlockSpec((2 * pairs, cols), lambda i: (group, 0))
    every = lambda a: pl.BlockSpec(a.shape, lambda i: (0,) * len(a.shape))
    fixed = lambda *s: pl.BlockSpec(s, lambda i: (0,) * len(s))
    kept = () if before is None else tuple(before[9:12]) + tuple(before[:9])
    kept_specs = [] if before is None else [every(before[9]), every(before[10]), smem] + [hbm] * 9
    ends, end_specs = (), ()
    if tail:
        send = (width + half // 2 + -(-(count + 8) // 96) * 96, hidden // 2)
        ends, end_specs = (shape(send, F32),), (fixed(*send),)
    if group == 0:
        ends += (shape((own, width), F32), shape((own, 128), BF))
        end_specs += (fixed(own, width), fixed(own, 128))
    held = total
    return pl.pallas_call(
        functools.partial(forward_kernel, length, group, groups),
        grid=(1,),
        out_shape=(
            shape((width, total), BF), shape((total, 3 * width), BF), shape((total // SUB, units, SUB, 2 * SUB), BF),
            shape((total, width), BF), shape((width, total), BF), shape((total, hidden // 2), BF),
            shape((width, total), BF), shape((total, width), BF), shape((total, hidden // 2), BF),
            shape((count, hidden), F32), shape((8, width), F32),
            shape((1, 1), jnp.int32),
        ) + ends,
        in_specs=[every(x), every(g1), every(g2), at_group(hidden), at_group(width)] + [hbm] * 6 + kept_specs,
        out_specs=(hbm,) * 9 + (fixed(count, hidden), fixed(8, width), smem) + end_specs,
        scratch_shapes=[
            pltpu.VMEM((rows, width), F32),
            pltpu.VMEM((rows, 128), F32),
            pltpu.VMEM((rows, 3 * width), BF),
            pltpu.VMEM((bins, units, SUB, 2 * SUB), BF),
            pltpu.VMEM((rows, width), BF),
            pltpu.VMEM((rows, width), F32),
            pltpu.VMEM((rows, width), F32),
            pltpu.VMEM((rows, width), BF),
            pltpu.VMEM((rows, width), BF),
            pltpu.VMEM((width, rows), BF),
            pltpu.VMEM((width, held), BF),
            pltpu.VMEM((width, held), BF),
            pltpu.VMEM((held, hidden), BF),
            pltpu.VMEM((held, width), BF),
            pltpu.VMEM((width, 3 * width), BF),
            pltpu.VMEM((width, width), BF),
            pltpu.VMEM((width, hidden), BF),
            pltpu.SemaphoreType.DMA((10,)),
            pltpu.SemaphoreType.DMA((8 * groups,)),
            pltpu.SemaphoreType.DMA((18,)),
        ],
        input_output_aliases={} if before is None else {14 + i: i for i in range(9)},
        cost_estimate=cost(22),
        compiler_params=pltpu.CompilerParams(vmem_limit_bytes=58 * MIB),
        name="text_forward",
    )(x, g1, g2, dmw, dh, *weights, *kept)


def backward_kernel(
    whole, more_ref, x_ref, dh1_ref, pick_ref, g1_ref, qkv_h, p_h, do_h, a1t_h, wqkv_h, woqkv_h,
    own_ref, send_ref, small_ref, qkv_s, p_s, do_s, a1t_s, dqkv_s, wqkv_s, load_sem, row_sem,
):
    bins = p_s.shape[0]
    main = whole // SUB
    width = do_s.shape[1]
    half = width // 2
    tiles = half // 128

    def rows_of(b):
        return pl.ds(pl.multiple_of(b * SUB, SUB), SUB)

    def bin_loads(b):
        at = rows_of(b)
        return [
            pltpu.make_async_copy(qkv_h.at[at], qkv_s.at[at], row_sem.at[3 * b]),
            pltpu.make_async_copy(p_h.at[b], p_s.at[b], row_sem.at[3 * b + 1]),
            pltpu.make_async_copy(do_h.at[at], do_s.at[at], row_sem.at[3 * b + 2]),
        ]

    for b in range(main):
        for c in bin_loads(b):
            c.start()
    pieces = [(a1t_h, a1t_s)]
    for g, h in enumerate((wqkv_h, woqkv_h)):
        for k in range(3):
            at = (3 * g + k) * half
            pieces.append((h.at[k], wqkv_s.at[:, at:at + half]))
    loads = [pltpu.make_async_copy(h, v, load_sem.at[i]) for i, (h, v) in enumerate(pieces)]
    for c in loads:
        c.start()

    def columns(g, kind, t):
        start = g * 3 * half + kind * half + t * 128
        return slice(start, start + 128)

    def work(b):
        for c in bin_loads(b):
            c.wait()
        at = rows_of(b)
        for g in range(2):
            for t in range(tiles):
                q2 = qkv_s[at, columns(g, 0, t)]
                k2 = qkv_s[at, columns(g, 1, t)]
                v2 = qkv_s[at, columns(g, 2, t)]
                col = g * half + t * 128
                do2 = two_heads(do_s[at, col:col + 128])
                dp = nt(v2, do2)
                p_low = p_s[b, g * tiles + t]
                p = p_low.astype(F32)
                ds = (p * (dp - jnp.sum(dp * p, 0, keepdims=True))).astype(BF)
                dqkv_s[at, columns(g, 2, t)] = nn(p_low, do2).astype(BF)
                dqkv_s[at, columns(g, 1, t)] = (nn(ds, two_heads(q2)) * HEAD ** (-0.5)).astype(BF)
                dqkv_s[at, columns(g, 0, t)] = (
                    tn(stack_heads(ds), two_heads(k2)) * HEAD ** (-0.5)
                ).astype(BF)

    def step(b, carry):
        work(b)
        return carry

    lax.fori_loop(0, main, step, 0)
    for c in loads:
        c.wait()
    own = x_ref.shape[0]
    pick = pick_ref[:, :own].astype(F32)

    def unpack(v):
        return lax.dot_general(pick, v, (((0,), (0,)), ((), ())), precision=HIGHEST, preferred_element_type=F32)

    da1 = unpack(nt(dqkv_s[:own, :], wqkv_s[...]))
    x = x_ref[...].astype(F32)
    xhat, inv = normalize(jnp.where(x < 0.5 * SENTINEL, x, 0.0))
    small_ref[:own, :] = unpack(dh1_ref[...]) + normalize_pull(da1 * g1_ref[...].reshape(1, width), xhat, inv)

    def gradients(k, rows, add):
        gain = jnp.zeros((width, 128), F32)
        for g in (1, 0):
            at = (3 * g + k) * half
            grad = nn(a1t_s[:, rows], dqkv_s[rows, at:at + half])
            into = send_ref if g else own_ref
            cut = slice(k * width, (k + 1) * width)
            into[cut, :] = into[cut, :] + grad if add else grad
            for j in range(half // 128):
                piece = slice(j * 128, (j + 1) * 128)
                gain += grad[:, piece] * wqkv_s[:, at + j * 128:at + (j + 1) * 128].astype(F32)
        return jnp.sum(gain.T, 0, keepdims=True) / g1_ref[...].reshape(1, width)

    small_ref[own:, :] = jnp.zeros((small_ref.shape[0] - own, width), F32)
    small_ref[own:own + 1, :] = sum(gradients(k, slice(0, whole), False) for k in range(3))
    if main < bins:
        @pl.when(more_ref[0, 0] > 0)
        def _():
            for b in range(main, bins):
                for c in bin_loads(b):
                    c.start()
            lax.fori_loop(main, bins, step, 0)
            small_ref[own:own + 1, :] += sum(gradients(k, slice(whole, bins * SUB), True) for k in range(3))
    at = 3 * width
    send_ref[at:, :] = jnp.zeros((send_ref.shape[0] - at, half), F32)
    count = small_ref.shape[0]
    send_ref[at:at + count, :] = small_ref[:, :half]
    send_ref[at + count:at + 2 * count, :] = small_ref[:, half:]


def text_backward(whole, more, x, dh1, pick, g1, qkv, p, do, a1t, wqkv, oqkv):
    total, width = do.shape
    half = width // 2
    own = dh1.shape[0]
    count = own + 8
    every = lambda a: pl.BlockSpec(a.shape, lambda i: (0,) * len(a.shape))
    fixed = lambda *s: pl.BlockSpec(s, lambda i: (0,) * len(s))
    hbm = pl.BlockSpec(memory_space=pl.ANY)
    smem = pl.BlockSpec(memory_space=pltpu.SMEM)
    shape = jax.ShapeDtypeStruct
    bins, units = p.shape[:2]
    return pl.pallas_call(
        functools.partial(backward_kernel, whole),
        grid=(1,),
        out_shape=(
            shape((3 * width, half), F32), shape((3 * width + 2 * count, half), F32), shape((count, width), F32),
        ),
        in_specs=[smem, fixed(own, width), every(dh1), every(pick), every(g1)] + [hbm] * 6,
        out_specs=(fixed(3 * width, half), fixed(3 * width + 2 * count, half), fixed(count, width)),
        scratch_shapes=[
            pltpu.VMEM((total, 3 * width), BF),
            pltpu.VMEM((bins, units, SUB, 2 * SUB), BF),
            pltpu.VMEM((total, width), BF),
            pltpu.VMEM((width, total), BF),
            pltpu.VMEM((total, 3 * width), BF),
            pltpu.VMEM((width, 3 * width), BF),
            pltpu.SemaphoreType.DMA((7,)),
            pltpu.SemaphoreType.DMA((3 * bins,)),
        ],
        cost_estimate=cost(20),
        compiler_params=pltpu.CompilerParams(vmem_limit_bytes=58 * MIB),
        name="text_backward",
    )(more, x, dh1, pick, g1, qkv, p, do, a1t, wqkv, oqkv)


def feed_kernel(
    a2t_ref, du_ref, upi_ref, ot_ref, dattn_ref, outa_ref, outb_ref, gsum_ref, gsumi_ref, dm_ref, low_ref, gh_ref,
    up_ref, out_ref, down_ref, proj_ref,
):
    up_ref[...] = upi_ref[...] + nn(a2t_ref[...], du_ref[...])
    quarter = outa_ref.shape[0]
    out = nn(ot_ref[...], dattn_ref[...])
    out_ref[:quarter, :] = out[:quarter] + outa_ref[...]
    out_ref[quarter:, :] = out[quarter:] + outb_ref[...]
    mine = gsum_ref.shape[0]
    high, rest = halves(jnp.concatenate([gsum_ref[...], gsumi_ref[:mine]], 0))
    down_ref[...] = tn(high, dm_ref[...]) + tn(rest, dm_ref[...])
    proj_ref[...] = tn(low_ref[...], gh_ref[...])


def feed_grads(a2t, du, ot, dattn, got, gsum, dm, low, gh):
    width, total = a2t.shape
    hidden = du.shape[1]
    half = width // 2
    quarter = half // 2
    mine = gsum.shape[0]
    steps = 6
    tile = hidden // steps
    slim = width // steps
    rest = got.shape[0] - width - quarter
    whole = lambda a: pl.BlockSpec(a.shape, lambda i: (0,) * len(a.shape), pipeline_mode=pl.Buffered(1))
    shape = jax.ShapeDtypeStruct
    columns = lambda rows, cols, row=0, col=0: pl.BlockSpec((rows, cols), lambda i: (row, col + i))
    return pl.pallas_call(
        feed_kernel,
        grid=(steps,),
        out_shape=(
            shape((width, hidden), F32), shape((half, width), F32), shape((hidden, width), F32), shape((width, half), F32),
        ),
        in_specs=[
            whole(a2t), columns(total, tile), columns(width, tile),
            pl.BlockSpec((half, total), lambda i: (0, 0), pipeline_mode=pl.Buffered(1)), columns(total, slim),
            columns(quarter, slim, width // quarter), columns(quarter, slim, width // quarter, steps),
            columns(mine, tile), columns(rest, tile, (width + quarter) // rest), whole(dm), columns(low.shape[0], slim),
            whole(gh),
        ],
        out_specs=(
            columns(width, tile), columns(half, slim), pl.BlockSpec((tile, width), lambda i: (i, 0)),
            pl.BlockSpec((slim, half), lambda i: (i, 0)),
        ),
        cost_estimate=cost(9),
        compiler_params=pltpu.CompilerParams(vmem_limit_bytes=28 * MIB),
        name="feed_grads",
    )(a2t, du, got, ot, dattn, got, got, gsum, got, dm, low, gh)


def finish_kernel(own_ref, in_ref, small_ref, smalla_ref, smallb_ref, gain2_ref, gain2i_ref, qkv_ref, rows_ref, gain1o_ref, gain2o_ref):
    qkv_ref[0] = own_ref[...] + in_ref[...]
    core = lax.axis_index("mp")
    own = rows_ref.shape[0] // 2
    half = gain1o_ref.shape[0]

    @pl.when(pl.program_id(0) == 0)
    def _():
        got = jnp.concatenate([smalla_ref[...], smallb_ref[...]], 1)
        rows_ref[:own, :] = jnp.where(core == 0, small_ref[:own], got[:own])
        rows_ref[own:, :] = jnp.where(core == 0, got[:own], small_ref[:own])
        one = small_ref[own:own + 1, :] + got[own:own + 1, :]
        two = gain2_ref[:1, :] + gain2i_ref[:1, :2 * half]
        gain1o_ref[...] = jnp.where(core == 0, one[:, :half], one[:, half:]).reshape(half)
        gain2o_ref[...] = jnp.where(core == 0, two[:, :half], two[:, half:]).reshape(half)


def finish(own, got, small, gain2, other, at):
    count, width = small.shape
    rows = count - 8
    half = width // 2
    whole = lambda a: pl.BlockSpec(a.shape, lambda i: (0,) * len(a.shape), pipeline_mode=pl.Buffered(1))
    fixed = lambda *shape: pl.BlockSpec(shape, lambda i: (0,) * len(shape))
    piece = pl.BlockSpec((width, half), lambda i: (i, 0))
    start = 3 * width // count
    shape = jax.ShapeDtypeStruct
    return pl.pallas_call(
        finish_kernel,
        grid=(3,),
        out_shape=(shape((3, width, half), F32), shape((2 * rows, width), F32), shape((half,), F32), shape((half,), F32)),
        in_specs=[
            piece, piece, whole(small), pl.BlockSpec((count, half), lambda i: (start, 0)),
            pl.BlockSpec((count, half), lambda i: (start + 1, 0)), whole(gain2),
            pl.BlockSpec((8, other.shape[1]), lambda i: (at // 8, 0)),
        ],
        out_specs=(pl.BlockSpec((1, width, half), lambda i: (i, 0, 0)), fixed(2 * rows, width), fixed(half), fixed(half)),
        cost_estimate=cost(4),
        compiler_params=pltpu.CompilerParams(vmem_limit_bytes=24 * MIB),
        name="finish",
    )(own, got, small, got, got, gain2, other)


MESH = pl.DeviceIdType.MESH


def chip_grid(mesh):
    chips = mesh.devices.reshape(-1, mesh.shape["mp"])[:, 0]
    places = [getattr(d, "coords", None) for d in chips]
    if all(p is not None and len(p) == 3 for p in places):
        grid = tuple(len({p[i] for p in places}) for i in (2, 1, 0))
        if grid[0] * grid[1] * grid[2] == len(chips):
            return grid
    side = 1
    while (2 * side) ** 3 <= len(chips):
        side *= 2
    return (len(chips) // (side * side), side, side)


class Spread:
    def __init__(self, grid, place, core, block, send, recv, first):
        self.grid, self.place, self.core = grid, place, core
        self.block, self.send, self.recv = block, send, recv
        self.first = first
        self.sent = []
        zs, ys, xs = grid
        self.turn = ys == xs
        self.aorder = list(range(1, ys))
        zevents = [("z", d, None) for d in range(1, zs)]
        aevents = [[("a", d, a) for d in range(zs)] for a in self.aorder]
        self.pending = []
        for i in range(zs + len(aevents)):
            self.pending += zevents[i:i + 1]
            for j, events in enumerate(aevents):
                self.pending += events[i - j:i - j + 1] if i >= j else []

    def slot(self, kz, ka):
        return kz * self.grid[1] + ka

    def target(self, dz, da):
        zs, ys, xs = self.grid
        z, y, x = self.place
        dy, dx = (da * (1 - self.core), da * self.core) if self.turn else (da, 0)
        batch = (lax.rem(z + dz, zs) * ys + lax.rem(y + dy, ys)) * xs + lax.rem(x + dx, xs)
        return (batch, self.core)

    def copy(self, source, landing, to, when=None):
        index = len(self.sent)

        def make():
            return pltpu.make_async_remote_copy(
                src_ref=self.first if source is None else self.block(self.slot(*source)),
                dst_ref=self.block(self.slot(*landing)), send_sem=self.send.at[index],
                recv_sem=self.recv.at[self.slot(*landing)], device_id=self.target(*to), device_id_type=MESH,
            )

        if when is None:
            make().start()
        else:
            pl.when(when)(lambda: make().start())
        self.sent.append((make, when))

    def forward(self, source, kz, when=None):
        for d in self.aorder:
            self.copy(source, (kz, self.grid[1] - d), (0, d), when)

    def start(self):
        zs = self.grid[0]
        z = self.place[0]
        if zs > 1:
            self.copy(None, (zs - 1, 0), (1, 0), z < zs - 1)
            self.copy(None, (1, 0), (zs - 1, 0), z > 0)
        self.forward(None, 0)

    def arrive(self, slot):
        pltpu.make_async_remote_copy(
            src_ref=self.block(slot), dst_ref=self.block(slot), send_sem=self.send.at[0],
            recv_sem=self.recv.at[slot], device_id=self.target(1, 0), device_id_type=MESH,
        ).wait_recv()

    def sides(self, d):
        zs = self.grid[0]
        z = self.place[0]
        return [(d, z + d < zs, True), (zs - d, z - d >= 0, False)]

    def serve(self, count=1):
        zs = self.grid[0]
        z = self.place[0]
        for _ in range(min(count, len(self.pending))):
            kind, d, a = self.pending.pop(0)
            if kind == "a" and d == 0:
                self.arrive(self.slot(0, a))
                continue
            for kz, there, above in self.sides(d):
                slot = self.slot(kz, 0 if kind == "z" else a)
                pl.when(there)(lambda slot=slot: self.arrive(slot))
                if kind == "z":
                    if d + 1 < zs and above:
                        self.copy((kz, 0), (kz + 1, 0), (zs - 1, 0), there & (z > 0))
                    elif d + 1 < zs:
                        self.copy((kz, 0), (kz - 1, 0), (1, 0), there & (z < zs - 1))
                    self.forward((kz, 0), kz, there)

    def finish(self):
        self.serve(len(self.pending))
        for make, when in self.sent:
            if when is None:
                make().wait_send()
            else:
                pl.when(when)(lambda make=make: make().wait_send())

    @staticmethod
    def copies(grid):
        zs, ys, _ = grid
        return 4 * zs + 2 * zs * (ys - 1)


class Hops:
    def __init__(self, grid, place, core, block, send, recv, first):
        self.grid, self.place, self.core = grid, place, core
        self.block, self.send, self.recv = block, send, recv
        self.first = first
        self.sent = []
        zs, ys, xs = grid
        self.turn = ys == xs
        near = []
        for d in range(1, zs // 2 + 1):
            near += [d] if 2 * d == zs else [d, zs - d]
        self.zorder = near
        self.aorder = list(range(1, ys))
        self.border = list(range(1, xs))
        self.pending = [("z", k) for k in near]
        self.pending += [("a", a, k) for a in self.aorder for k in [0] + near]

    def slot(self, kz, ka, kb):
        zs, ys, xs = self.grid
        plain = (kz * ys + ka) * xs + kb
        if not self.turn:
            return plain
        other = (kz * ys + kb) * xs + ka
        return plain if plain == other else plain + self.core * (other - plain)

    def target(self, dz, da, db):
        zs, ys, xs = self.grid
        z, y, x = self.place
        if self.turn and da != db:
            dy = da + self.core * (db - da)
            dx = db + self.core * (da - db)
        else:
            dy, dx = da, db
        batch = (lax.rem(z + dz, zs) * ys + lax.rem(y + dy, ys)) * xs + lax.rem(x + dx, xs)
        return (batch, self.core)

    def copy(self, source, landing, to):
        index = len(self.sent)
        sent = pltpu.make_async_remote_copy(
            src_ref=source, dst_ref=self.block(landing), send_sem=self.send.at[index],
            recv_sem=self.recv.at[landing], device_id=to, device_id_type=MESH,
        )
        sent.start()
        self.sent.append(sent)

    def along_a(self, source, kz):
        ys = self.grid[1]
        for d in self.aorder:
            self.copy(source, self.slot(kz, ys - d, 0), self.target(0, d, 0))

    def along_b(self, source, kz, ka):
        xs = self.grid[2]
        for d in self.border:
            self.copy(source, self.slot(kz, ka, xs - d), self.target(0, 0, d))

    def start(self):
        zs = self.grid[0]
        self.along_b(self.first, 0, 0)
        self.along_a(self.first, 0)
        for d in self.zorder:
            self.copy(self.first, self.slot(zs - d, 0, 0), self.target(d, 0, 0))

    def arrive(self, slot):
        pltpu.make_async_remote_copy(
            src_ref=self.block(slot), dst_ref=self.block(slot), send_sem=self.send.at[0],
            recv_sem=self.recv.at[slot], device_id=self.target(1, 0, 0), device_id_type=MESH,
        ).wait_recv()

    def serve(self, count=1):
        for _ in range(min(count, len(self.pending))):
            event = self.pending.pop(0)
            if event[0] == "z":
                slot = self.slot(event[1], 0, 0)
                self.arrive(slot)
                self.along_b(self.block(slot), event[1], 0)
                self.along_a(self.block(slot), event[1])
            else:
                slot = self.slot(event[2], event[1], 0)
                self.arrive(slot)
                self.along_b(self.block(slot), event[2], event[1])

    def finish(self):
        self.serve(len(self.pending))
        for a in [0] + self.aorder:
            for b in self.border:
                for k in [0] + self.zorder:
                    self.arrive(self.slot(k, a, b))
        for sent in self.sent:
            sent.wait_send()

    @staticmethod
    def copies(grid):
        zs, ys, xs = grid
        return (zs - 1) + zs * (ys - 1) + zs * ys * (xs - 1)


def attend(qkv_ref, o_ref, start, ids, half):
    m = ids == ids.T
    m = jnp.concatenate([m, m], 1)
    rows = pl.ds(start, SUB)
    for t in range(half // 128):
        q2 = qkv_ref[rows, t * 128:(t + 1) * 128]
        k2 = qkv_ref[rows, half + t * 128:half + (t + 1) * 128]
        v2 = qkv_ref[rows, 2 * half + t * 128:2 * half + (t + 1) * 128]
        st = nt(k2, two_heads(q2)) * HEAD ** (-0.5)
        st = jnp.where(m, st, -1000000000.0)
        e = jnp.exp(st - jnp.max(st, 0, keepdims=True))
        p = e * (1.0 / jnp.sum(e, 0, keepdims=True))
        o_ref[rows, t * 128:(t + 1) * 128] = tn(stack_heads(p.astype(BF)), two_heads(v2)).astype(BF)


def front_kernel(
    grid,
    rows_ref, mask_ref, image_ref, g1_ref, g2_ref, temp_ref,
    iqkv_h, iout_h, iup_h, idown_h, tqkv_h, tout_h, tup_h, tdown_h, tproj_h,
    xg_ref, oqkv_h, oout_h, oup_h, dmw_ref, dh_ref, dm_ref, low_ref, gh_ref, loss_ref, temp_ref2,
    iqkv, iout, iup, idown, tqkv, tout, tup, tdown, proj,
    own_x, small, small_abs, payload, qkv_s, o_s, image_x, part, part_in, sums, sums_in,
    wsend_qkv, wsend_out, wsend_up, wsend_proj, wland_qkv, wland_out, wland_up, wland_proj,
    dmw_send, dmw_in, cos_s, tnorm_s, xg,
    load_sem, out_sem, x_send, x_recv, s_send, s_recv, c_send, c_recv, own_sem,
):
    zs, ys, xs = grid
    chips = zs * ys * xs
    planes = zs * ys
    batch, core = lax.axis_index("batch"), lax.axis_index("mp")
    place = (batch // (ys * xs), lax.rem(batch // xs, ys), lax.rem(batch, xs))
    partner = (batch, 1 - core)
    pairs, length = mask_ref.shape
    rows = pairs * length
    width = rows_ref.shape[1]
    half = width // 2
    hidden = tup.shape[1]
    hp = pairs // 2
    hr = hp * length
    total = chips * pairs
    mine = chips * hp
    patches = image_ref.shape[0] // pairs
    padded = image_x.shape[0] // pairs

    inside = total <= INSIDE

    loads = {}
    for i, (name, h, v) in enumerate((
        ("iqkv", iqkv_h, iqkv), ("tqkv", tqkv_h, tqkv), ("iout", iout_h, iout), ("tout", tout_h, tout),
        ("tup", tup_h, tup), ("iup", iup_h, iup), ("idown", idown_h, idown), ("tdown", tdown_h, tdown),
        ("proj", tproj_h, proj.at[core]),
    )):
        loads[name] = pltpu.make_async_copy(h, v, load_sem.at[i])
        if i < 3:
            loads[name].start()

    xg = xg if inside else xg_ref
    gather = Spread(grid, place, core, lambda s: xg.at[s], x_send, x_recv, own_x)
    peers = [partner]
    spread = Hops(grid, place, core, lambda s: small.at[core, s], s_send, s_recv, payload)
    peers += [spread.target(d, 0, 0) for d in range(1, zs)]
    peers += [spread.target(0, d, 0) for d in range(1, ys)]
    peers += [spread.target(0, 0, d) for d in range(1, xs)]
    barrier = pltpu.get_barrier_semaphore()
    for peer in peers:
        pl.semaphore_signal(barrier, inc=1, device_id=peer, device_id_type=MESH)

    mask = mask_ref[...].astype(F32)
    lane = count_along(rows, length)
    sub = parts_of(count_down(rows, length), length)[1]
    spread_mask = jnp.broadcast_to(mask[:, None, :], (pairs, length, length)).reshape(rows, length)
    valid = jnp.sum(jnp.where(lane == sub, spread_mask, 0.0), 1, keepdims=True)
    text_x = rows_ref[...].astype(F32)
    marked = jnp.where(valid > 0, text_x, SENTINEL)
    own_x[...] = jnp.where(core == 0, marked[:hr], marked[hr:])
    top = padded * pairs
    image_of, patch_of = parts_of(count_down(top), padded)
    image_ids = jnp.where(patch_of < patches, image_of, -1.0)
    place_of = jnp.where(patch_of < patches, patch_of * pairs + image_of, -1.0)
    reorder = (widen(place_of, patches * pairs) == count_along(top, patches * pairs)).astype(BF)
    image_x[...] = nn(reorder, image_ref[...])
    image_a1 = normalize(image_x[...])[0].astype(BF)
    pl.semaphore_wait(barrier, len(peers))
    gather.start()

    swaps = []

    def swap(source, landing, index):
        c = pltpu.make_async_remote_copy(
            src_ref=source, dst_ref=landing, send_sem=c_send.at[index], recv_sem=c_recv.at[index],
            device_id=partner, device_id_type=MESH,
        )
        c.start()
        swaps.append(c)
        return c

    def put(ref, cols, high, rest):
        size = mine // 2
        for g in range(2):
            ref[2 * g * size:(2 * g + 1) * size, cols] = high[g * size:(g + 1) * size]
            ref[(2 * g + 1) * size:(2 * g + 2) * size, cols] = rest[g * size:(g + 1) * size]

    def contrast():
        for s in range(chips):
            kz, ky, kx = s // (ys * xs), s // xs % ys, s % xs
            at = (lax.rem(place[0] + kz, zs) * ys + lax.rem(place[1] + ky, ys)) * xs + lax.rem(place[2] + kx, xs)
            small_abs[:, at] = small[:, s]
        low = small_abs[0, :, :, :width].reshape(total, width).astype(BF)
        low_ref[...] = low
        counts = small_abs[0, :, :, width:].reshape(total, 128)[:, :1]
        embed = jnp.concatenate([nn(low, proj[0]), nn(low, proj[1])], 1)
        inv = lax.rsqrt(jnp.sum(embed * embed, 1, keepdims=True) + NORM_EPS)
        tnorm_s[...] = embed * inv
        images = small_abs[1, :, :, :width].reshape(total, width)
        scale = jnp.exp(jnp.full((1, 1), temp_ref[0, 0], F32))
        cos_s[...] = three(nt, tnorm_s[...], images)
        logits = cos_s[...] * scale
        row_top = jnp.max(logits, 1, keepdims=True)
        row_lse = row_top + jnp.log(jnp.sum(jnp.exp(logits - row_top), 1, keepdims=True))
        col_top = jnp.max(logits, 0, keepdims=True)
        col_lse = col_top + jnp.log(jnp.sum(jnp.exp(logits - col_top), 0, keepdims=True))
        eye = (lax.broadcasted_iota(jnp.int32, (total, total), 0) == lax.broadcasted_iota(jnp.int32, (total, total), 1))
        eye = eye.astype(F32)
        pair_grad = (jnp.exp(logits - row_lse) + jnp.exp(logits - col_lse) - 2.0 * eye) * (0.5 / total)

        def everything(v):
            return jnp.sum(jnp.sum(v, 1, keepdims=True), 0, keepdims=True)

        loss = (everything(row_lse) + everything(col_lse) - 2.0 * everything(logits * eye)) * (0.5 / total)
        temp = scale * everything(pair_grad * cos_s[...])
        loss_ref[...] = loss
        temp_ref2[...] = temp
        grad_norm = scale * three(nn, pair_grad, images)
        tnorm = tnorm_s[...]
        grad_embed = ((grad_norm - tnorm * jnp.sum(tnorm * grad_norm, 1, keepdims=True)) * inv).astype(BF)
        gh_ref[...] = jnp.where(core == 0, grad_embed[:, :half], grad_embed[:, half:])
        dh = (nt(grad_embed[:, :half], proj[0]) + nt(grad_embed[:, half:], proj[1])) / counts
        dm = dh.astype(BF)

        r = count_along(8, total)
        here = core.astype(F32)
        owner = jnp.where(r < mine, here, 1.0 - here)
        k, i = parts_of(parts_of(r, mine)[1], hp)
        kb, rest = parts_of(k, planes)
        kz, ka = parts_of(rest, ys)
        ky, kx = (jnp.where(owner == 0, ka, kb), jnp.where(owner == 0, kb, ka)) if ys == xs else (ka, kb)
        z, y, x = (parts_of(v + p.astype(F32), n)[1] for v, p, n in zip((kz, ky, kx), place, grid))
        at = ((z * ys + y) * xs + x) * pairs + owner * hp + i
        pick = (jnp.broadcast_to(at[:1], (total, total)).T == count_along(total, total)).astype(BF)
        dm_sorted = nn(pick, dm).astype(BF)
        dm_ref[...] = dm_sorted
        dmw = nt(dm_sorted, tdown[...])
        dmw_send[...] = dmw[mine:]
        dmw_swap = swap(dmw_send, dmw_in, 8)
        dh_high, dh_low = halves(dh)
        put(dh_ref, slice(None), nn(pick[:mine], dh_high).astype(BF), nn(pick[:mine], dh_low).astype(BF))
        put(dmw_ref, slice(0, hidden), *halves(dmw[:mine]))
        return dmw_swap

    g1, g2 = g1_ref[...].reshape(1, width), g2_ref[...].reshape(1, width)
    loads["iqkv"].wait()
    for name in list(loads)[3:]:
        loads[name].start()
    for k in range(3):
        qkv_s[:, k * half:(k + 1) * half] = nn(image_a1, iqkv[k]).astype(BF)
    loads["tqkv"].wait()
    for k in range(3):
        wsend_qkv[k] = tqkv[k].astype(F32)
    qkv_swap = swap(wsend_qkv, wland_qkv, 3)
    loads["iout"].wait()
    parts = 2
    cut = top // parts
    image_swaps = []
    for i in range(parts):
        for s in range(i * cut // SUB, (i + 1) * cut // SUB):
            attend(qkv_s, o_s, s * SUB, image_ids[s * SUB:(s + 1) * SUB], half)
        at = pl.ds(i * cut, cut)
        part[at, :] = nn(o_s[at, :], iout[...])
        image_swaps.append(swap(part.at[at], part_in.at[at], i))

    a1 = (normalize(text_x)[0] * g1).astype(BF)
    for k in range(3):
        qkv_s[:rows, k * half:(k + 1) * half] = nn(a1, tqkv[k]).astype(BF)
    attend(qkv_s, o_s, 0, jnp.where(valid > 0, parts_of(count_down(rows), length)[0], -1.0), half)
    loads["tout"].wait()
    part[top:, :] = nn(o_s[:rows, :], tout[...])
    text_swap = swap(part.at[pl.ds(top, rows)], part_in.at[pl.ds(top, rows)], 5)
    gather.serve(2)

    loads["tup"].wait()
    up_cut = wsend_up.shape[0] // 4
    up_swaps = []

    def send_up(i):
        at = pl.ds(i * up_cut, up_cut)
        wsend_up[at, :] = tup[at, :].astype(F32)
        up_swaps.append(swap(wsend_up.at[at], wland_up.at[at], 9 + i))

    send_up(0)
    send_up(1)

    piece = 512
    loads["iup"].wait()
    mean_i, bars = [], []
    for i in range(parts):
        image_swaps[i].wait_recv()
        at = pl.ds(i * cut, cut)
        h1 = image_x[at, :] + (part[at, :] + part_in[at, :])
        a2 = normalize(h1)[0].astype(BF)
        mean_i.append(jnp.sum(h1.reshape(pairs // parts, padded, width), 1))
        bar = []
        for j in range(hidden // piece):
            u = nn(a2, iup[:, j * piece:(j + 1) * piece])
            g = (u * (0.5 + 0.5 * lax.erf(u * 0.5 ** 0.5))).astype(BF).astype(F32)
            bar.append(jnp.sum(g.reshape(pairs // parts, padded, piece), 1))
        bars.append(jnp.concatenate(bar, 1))
        gather.serve(1)
    mean_i = jnp.concatenate(mean_i, 0)
    bar = jnp.concatenate(halves(jnp.concatenate(bars, 0)), 0)
    loads["idown"].wait()
    low = nn(bar, idown[...])
    sums[pairs:, :] = low[:pairs] + low[pairs:]

    text_swap.wait_recv()
    h1 = text_x + (part[top:, :] + part_in[top:, :])
    a2 = (normalize(h1)[0] * g2).astype(BF)
    mean_h = jnp.sum((h1 * valid).reshape(pairs, length, width), 1)
    bars = []
    for j in range(hidden // piece):
        u = nn(a2, tup[:, j * piece:(j + 1) * piece])
        g = (u * (0.5 + 0.5 * lax.erf(u * 0.5 ** 0.5))).astype(BF).astype(F32) * valid
        bars.append(jnp.sum(g.reshape(pairs, length, piece), 1))
    bar = jnp.concatenate(halves(jnp.concatenate(bars, 1)), 0)
    loads["tdown"].wait()
    low = nn(bar, tdown[...])
    sums[:pairs, :] = low[:pairs] + low[pairs:]
    sums_swap = swap(sums, sums_in, 6)
    sums_swap.wait_recv()

    count = jnp.sum(mask, 1, keepdims=True)
    pooled = (mean_h + (sums[:pairs, :] + sums_in[:pairs, :])) / count
    e = (mean_i + (sums[pairs:, :] + sums_in[pairs:, :])) * (1.0 / patches)
    image_norm = e * lax.rsqrt(jnp.sum(e * e, 1, keepdims=True) + NORM_EPS)
    payload[:, :width] = jnp.where(core == 0, pooled, image_norm)
    payload[:, width:] = jnp.broadcast_to(count, (pairs, 128))
    spread.start()
    small[core, 0] = payload[...]
    loads["proj"].wait()
    wsend_proj[...] = proj[core].astype(F32)
    proj_swap = swap(wsend_proj, wland_proj, 2)
    wsend_out[...] = tout[...].astype(F32)
    out_swap = swap(wsend_out, wland_out, 4)
    send_up(2)
    send_up(3)
    oqkv, oout, oup = iqkv, iout, iup
    outs = []

    def hand_over(swapped, landed, held, out, index):
        swapped.wait_recv()
        held[...] = landed[...].astype(BF)
        outs.append(pltpu.make_async_copy(held, out, out_sem.at[index]))
        outs[-1].start()

    def hand_up(i):
        at = pl.ds(i * up_cut, up_cut)
        hand_over(up_swaps[i], wland_up.at[at], oup.at[at], oup_h.at[at], 2 + i)

    hand_over(qkv_swap, wland_qkv, oqkv, oqkv_h, 1)
    gather.serve(1)
    spread.serve(zs - 1)
    gather.serve(1)
    hand_up(0)
    hand_up(1)
    spread.serve(len(spread.pending))
    gather.serve(len(gather.pending))
    proj_swap.wait_recv()
    proj[1 - core] = wland_proj[...].astype(BF)
    hand_over(out_swap, wland_out, oout, oout_h, 0)
    spread.finish()
    both_swap = swap(small.at[core], small.at[core], 7)
    hand_up(2)
    both_swap.wait_recv()
    gather.serve(len(gather.pending))
    own_copy = pltpu.make_async_copy(own_x, xg_ref.at[0], own_sem.at[0])
    own_copy.start()
    if inside:
        store = pltpu.make_async_copy(xg.at[pl.ds(1, planes - 1)], xg_ref.at[pl.ds(1, planes - 1)], own_sem.at[1])
        store.start()
    if inside:
        dmw_swap = contrast()
    else:
        dmw_ref[...] = small[...]
        dm_ref[...] = proj[...]

    hand_up(3)
    if inside:
        dmw_swap.wait_recv()
        put(dmw_ref, slice(hidden, 2 * hidden), *halves(dmw_in[...]))
    gather.finish()
    own_copy.wait()
    if inside:
        store.wait()
    for s in swaps:
        s.wait_send()
    for o in outs:
        o.wait()


def front(grid, rows, mask, image, g1, g2, temp, weights):
    chips = grid[0] * grid[1] * grid[2]
    pairs, length = mask.shape
    width = rows.shape[1]
    half = width // 2
    iqkv, iout, iup, idown, tqkv, tout, tup, tdown, tproj = weights
    hidden = tup.shape[1]
    total = chips * pairs
    mine = total // 2
    patches = image.shape[0] // pairs
    padded = -(-patches // 64) * 64
    top = padded * pairs
    hr = pairs // 2 * length
    vmem = pl.BlockSpec(memory_space=pltpu.VMEM)
    hbm = pl.BlockSpec(memory_space=pl.ANY)
    shape = jax.ShapeDtypeStruct
    copies, hops = Spread.copies(grid), Hops.copies(grid)
    inside = total <= INSIDE
    if inside:
        ends = (
            shape((2 * mine, 2 * hidden), BF), shape((2 * mine, width), BF), shape((total, width), BF),
            shape((total, width), BF), shape((total, half), BF), shape((1, 1), F32), shape((1, 1), F32),
        )
    else:
        mine, total = 8, 128
        ends = (shape((2, chips, pairs, width + 128), F32),) + (shape((8, 128), F32),)
        ends += (shape((2,) + tproj.shape, BF),) + (shape((8, 128), F32),) * 4
    return pl.pallas_call(
        functools.partial(front_kernel, grid),
        out_shape=(
            shape((grid[0] * grid[1], hr, width), F32),
            shape(tqkv.shape, BF), shape(tout.shape, BF), shape(tup.shape, BF),
        ) + ends,
        in_specs=[vmem] * 5 + [pl.BlockSpec(memory_space=pltpu.SMEM)] + [hbm] * 9,
        out_specs=[hbm] * 4 + [vmem] * 7,
        scratch_shapes=[
            pltpu.VMEM(iqkv.shape, BF), pltpu.VMEM(iout.shape, BF), pltpu.VMEM(iup.shape, BF), pltpu.VMEM(idown.shape, BF),
            pltpu.VMEM(tqkv.shape, BF), pltpu.VMEM(tout.shape, BF), pltpu.VMEM(tup.shape, BF), pltpu.VMEM(tdown.shape, BF),
            pltpu.VMEM((2,) + tproj.shape, BF),
            pltpu.VMEM((hr, width), F32),
            pltpu.VMEM((2, chips, pairs, width + 128), F32),
            pltpu.VMEM((2, chips if inside else 1, pairs, width + 128), F32),
            pltpu.VMEM((pairs, width + 128), F32),
            pltpu.VMEM((top, 3 * half), BF),
            pltpu.VMEM((top, half), BF),
            pltpu.VMEM((top, width), F32),
            pltpu.VMEM((top + pairs * length, width), F32),
            pltpu.VMEM((top + pairs * length, width), F32),
            pltpu.VMEM((2 * pairs, width), F32),
            pltpu.VMEM((2 * pairs, width), F32),
            pltpu.VMEM(tqkv.shape, F32), pltpu.VMEM(tout.shape, F32), pltpu.VMEM(tup.shape, F32), pltpu.VMEM(tproj.shape, F32),
            pltpu.VMEM(tqkv.shape, F32), pltpu.VMEM(tout.shape, F32), pltpu.VMEM(tup.shape, F32), pltpu.VMEM(tproj.shape, F32),
            pltpu.VMEM((mine, hidden), F32), pltpu.VMEM((mine, hidden), F32),
            pltpu.VMEM((total, total), F32), pltpu.VMEM((total, width), F32),
            pltpu.VMEM((grid[0] * grid[1], hr, width) if inside else (1, 8, 128), F32),
            pltpu.SemaphoreType.DMA((9,)), pltpu.SemaphoreType.DMA((6,)),
            pltpu.SemaphoreType.DMA((copies,)), pltpu.SemaphoreType.DMA((grid[0] * grid[1],)),
            pltpu.SemaphoreType.DMA((hops,)), pltpu.SemaphoreType.DMA((chips,)),
            pltpu.SemaphoreType.DMA((13,)), pltpu.SemaphoreType.DMA((13,)), pltpu.SemaphoreType.DMA((2,)),
        ],
        cost_estimate=cost(40),
        compiler_params=pltpu.CompilerParams(collective_id=0, has_side_effects=True, vmem_limit_bytes=60 * MIB),
        name="front",
    )(rows, mask, image, g1, g2, temp, *weights)


def contrast_outside(grid, small, proj, log_temp, text_down):
    core = lax.axis_index("mp")
    here = lax.axis_index("batch")
    chips, pairs, width = small.shape[1], small.shape[2], small.shape[3] - 128
    half = width // 2
    zs, ys, xs = grid
    slots = jnp.arange(chips, dtype=jnp.int32)
    z, y, x = here // (ys * xs), here // xs % ys, here % xs
    offset = (z + slots // (ys * xs)) % zs * (ys * xs) + (y + slots // xs % ys) % ys * xs + (x + slots % xs) % xs
    slot_of = jnp.argsort(offset)
    total = chips * pairs
    low = small[0, :, :, :width].astype(BF)[slot_of].reshape(total, width)
    counts = small[0, :, :, width:width + 1][slot_of].reshape(total, 1)
    images = small[1, :, :, :width][slot_of].reshape(total, width)
    embed = jnp.concatenate([nn(low, proj[0]), nn(low, proj[1])], 1)
    inv = lax.rsqrt(jnp.sum(embed * embed, 1, keepdims=True) + NORM_EPS)
    text_norm = embed * inv
    scale = jnp.exp(log_temp)
    cosine = three(nt, text_norm, images)
    logits = scale * cosine
    text_lse = jax.nn.logsumexp(logits, 1, keepdims=True)
    image_lse = jax.nn.logsumexp(logits, 0, keepdims=True)
    eye = jnp.eye(total, dtype=F32)
    pair_grad = (jnp.exp(logits - text_lse) + jnp.exp(logits - image_lse) - 2.0 * eye) / (2.0 * total)
    loss = (jnp.sum(text_lse) + jnp.sum(image_lse) - 2.0 * jnp.sum(logits * eye)) / (2.0 * total)
    temp = scale * jnp.sum(pair_grad * cosine)
    grad_norm = scale * three(nn, pair_grad, images)
    grad_embed = ((grad_norm - text_norm * jnp.sum(text_norm * grad_norm, 1, keepdims=True)) * inv).astype(BF)
    grad_half = lax.dynamic_slice_in_dim(grad_embed, core * half, half, 1)
    dh = (nt(grad_embed[:, :half], proj[0]) + nt(grad_embed[:, half:], proj[1])) / counts
    hp = pairs // 2
    ka, kb = slots % ys, slots // (zs * ys)
    kz = slots // ys % zs

    def mine(v, c):
        ky, kx = (jnp.where(c == 0, ka, kb), jnp.where(c == 0, kb, ka)) if ys == xs else (ka, kb)
        chip = ((z + kz) % zs * ys + (y + ky) % ys) * xs + (x + kx) % xs
        w = v.reshape(chips, 2, hp, v.shape[-1])[chip]
        return lax.dynamic_index_in_dim(w, c, 1, keepdims=False).reshape(total // 2, v.shape[-1])

    def grouped(v):
        high, rest = halves(v)
        size = INSIDE // 8
        both = jnp.stack([high.reshape(-1, size, v.shape[1]), rest.reshape(-1, size, v.shape[1])], 1)
        return both.reshape(-1, v.shape[1])

    dm = jnp.concatenate([mine(dh, core), mine(dh, 1 - core)], 0).astype(BF)
    dmw = nt(dm, text_down)
    dmw_other = lax.ppermute(dmw[total // 2:], "mp", [(0, 1), (1, 0)])
    dmw = grouped(jnp.concatenate([dmw[:total // 2], dmw_other], 1))
    return dmw, grouped(mine(dh, core)), dm, low, grad_half, loss, temp


def last_axis(grid):
    zs, ys, xs = grid
    plans = []
    for d in range(1, xs):
        pairs = []
        for z in range(zs):
            for y in range(ys):
                for x in range(xs):
                    for core in range(2):
                        py, px = (y, (x + d) % xs) if core == 0 or ys != xs else ((y + d) % ys, x)
                        pairs.append((((z * ys + py) * xs + px) * 2 + core, ((z * ys + y) * xs + x) * 2 + core))
        plans.append(pairs)
    return plans


def per_device(
    grid, image_patches, text_rows, text_mask, image_qkv, image_out, image_up, image_down, text_gain_one, text_gain_two,
    text_qkv, text_out, text_up, text_down, text_proj, log_temp,
):
    pair_count, length, width = text_rows.shape
    half = width // 2
    hidden = text_up.shape[1]

    def swap(v):
        return lax.ppermute(v, "mp", [(0, 1), (1, 0)])

    patches = jnp.transpose(image_patches, (1, 0, 2)).reshape(-1, width)
    iqkv = jnp.transpose(image_qkv, (1, 0, 2))
    tqkv = jnp.transpose(text_qkv, (1, 0, 2))
    g1, g2 = text_gain_one, text_gain_two
    xg, oqkv, oout, oup, dmw, dh, dm, low, grad_half, loss, temp = front(
        grid, text_rows.reshape(-1, width), text_mask, patches, g1, g2, log_temp.reshape(1, 1),
        (iqkv, image_out, image_up, image_down, tqkv, text_out, text_up, text_down, text_proj),
    )
    own = pair_count // 2 * length
    if dm.ndim == 3:
        dmw, dh, dm, low, grad_half, loss, temp = contrast_outside(grid, dmw, dm, log_temp, text_down)
    weights = (tqkv, text_out, text_up, oqkv, oout, oup)
    total = dm.shape[0] // 2
    near = xg.reshape(-1, width)
    plans = last_axis(grid)
    if dm.shape[0] <= INSIDE:
        far = [lax.ppermute(near, ("batch", "mp"), pairs) for pairs in plans]
        before = None
        groups = [near] + far
        for g, x in enumerate(groups):
            before = text_forward(x, length, g1, g2, dmw, dh, weights, own, len(groups), g, before)
            if g == 0:
                dh1, pick = before[-2:]
        a1t, qkv, p, do, a2t, du, ot, dattn, _, gsum, gain2, more, send = before[:13]
        got = swap(send)
        whole = layout(near.shape[0], len(groups))[0] * len(groups)
        qkv_m, qkv_o, small = text_backward(whole, more, near, dh1, pick, g1, qkv, p, do, a1t, tqkv, oqkv)
        qkv_in = swap(qkv_o)
        grad_up, grad_out, grad_down, grad_proj = feed_grads(a2t, du, ot, dattn, got, gsum, dm, low, grad_half)
        qkv_in, grad_up, grad_out, grad_down, grad_proj = lax.optimization_barrier(
            (qkv_in, grad_up, grad_out, grad_down, grad_proj))
        other, at = got, width + half // 2 + gsum.shape[0]
    else:
        size = INSIDE // 8
        groups = total // size

        def one(carry, items):
            sums, first = carry
            g, x, dmw, dh = items
            a1t, qkv, p, do, a2t, du, ot, dattn, _, gsum, gain2, more, send, dh1, pick = text_forward(
                x, length, g1, g2, dmw, dh, weights, own)
            qkv_m, qkv_o, small = text_backward(x.shape[0], more, x, dh1, pick, g1, qkv, p, do, a1t, tqkv, oqkv)
            new = (send, gain2, qkv_m, qkv_o, small[own:], nn(a2t, du), nn(ot[:half], dattn))
            return (tuple(x + y for x, y in zip(sums, new)), jnp.where(g == 0, small[:own], first)), gsum

        zero = lambda *shape: jnp.zeros(shape, F32)
        at = width + half // 2 + size
        sums = (zero(width + half // 2 + 96, hidden), zero(8, width), zero(3 * width, half),
                zero(3 * width + 2 * own + 16, half), zero(8, width), zero(width, hidden), zero(half, width))
        split = lambda v: v.reshape(groups, -1, v.shape[-1])
        planes = [near] + [lax.ppermute(near, ("batch", "mp"), pairs) for pairs in plans]
        planes = [jnp.where(x > 0.5 * SENTINEL, SENTINEL, x).astype(BF) for x in planes]
        (sums, first), gsum = lax.scan(
            one, (sums, zero(own, width)),
            (jnp.arange(groups), split(jnp.concatenate(planes, 0)), split(dmw), split(dh)))
        gsum = gsum.reshape(-1, gsum.shape[-1])
        send, gain2, qkv_m, qkv_o, gain1, up_m, out_m = sums
        small = jnp.concatenate([first, gain1], 0)
        qkv_o = jnp.concatenate([qkv_o[:3 * width], small[:, :half], small[:, half:]], 0)
        qkv_in, got = swap(qkv_o), swap(send)
        grad_up = up_m + got[:width]
        folded = got[width:width + half // 2]
        grad_out = out_m + jnp.concatenate([folded[:, :width], folded[:, width:]], 0)
        high, rest = halves(jnp.concatenate([gsum[:, :hidden], swap(gsum[:, hidden:])], 0))
        grad_down = tn(high, dm) + tn(rest, dm)
        grad_proj = tn(low, grad_half)
        other = got
    grad_qkv, grad_rows, gain1, gain2 = finish(qkv_m, qkv_in, small, gain2, other, at)
    return (loss.reshape(()), grad_rows.reshape(pair_count, length, width), gain1, gain2,
            jnp.transpose(grad_qkv, (1, 0, 2)), grad_out, grad_up, grad_down, grad_proj, temp.reshape(()))


def solution(mesh):
    return jax.shard_map(
        functools.partial(per_device, chip_grid(mesh)),
        mesh=mesh,
        in_specs=(
            P("batch", None, None), P("batch", None, None), P("batch", None), P(None, None, "mp"), P("mp", None),
            P(None, "mp"), P("mp", None), P(), P(), P(None, None, "mp"), P("mp", None), P(None, "mp"), P("mp", None),
            P(None, "mp"), P(),
        ),
        out_specs=(
            P(), P("batch", None, None), P("mp"), P("mp"), P(None, None, "mp"), P("mp", None), P(None, "mp"),
            P("mp", None), P(None, "mp"), P(),
        ),
        check_vma=False,
    )
```

```python
import functools
import jax
import jax.numpy as jnp
from jax import lax
from jax.experimental import pallas as pl
from jax.experimental.pallas import tpu as pltpu
from jax.sharding import PartitionSpec as P

HEAD = 64
LN_EPS = 1e-06
NORM_EPS = 1e-06
HIGHEST = lax.Precision.HIGHEST
BF = jnp.bfloat16
F32 = jnp.float32
MIB = 2**20


def cost(microseconds):
    return pl.CostEstimate(flops=int(microseconds * 1e9), bytes_accessed=0, transcendentals=0)


def nn(a, b):
    return lax.dot_general(a, b, (((1,), (0,)), ((), ())), preferred_element_type=F32)


def nt(a, b):
    return lax.dot_general(a, b, (((1,), (1,)), ((), ())), preferred_element_type=F32)


def tn(a, b):
    return lax.dot_general(a, b, (((0,), (0,)), ((), ())), preferred_element_type=F32)


def normalize(rows):
    center = rows - jnp.mean(rows, -1, keepdims=True)
    inv = lax.rsqrt(jnp.mean(center * center, -1, keepdims=True) + LN_EPS)
    return center * inv, inv


def normalize_pull(grad, xhat, inv):
    return inv * (
        grad - jnp.mean(grad, -1, keepdims=True) - xhat * jnp.mean(grad * xhat, -1, keepdims=True)
    )


def two_heads(tile):
    first = lax.broadcasted_iota(jnp.int32, tile.shape, 1) < HEAD
    zero = jnp.zeros_like(tile)
    return jnp.concatenate([jnp.where(first, tile, zero), jnp.where(first, zero, tile)], 0)


def stack_heads(pair):
    half = pair.shape[1] // 2
    return jnp.concatenate([pair[:, :half], pair[:, half:]], 0)


def halves(values):
    high = values.astype(BF)
    return high, (values - high.astype(F32)).astype(BF)


SENTINEL = 1e30
SUB = 128
INSIDE = 128


def three(form, a, b):
    (ah, al), (bh, bl) = halves(a), halves(b)
    return form(ah, bh) + (form(ah, bl) + form(al, bh))


def parts_of(v, n):
    q = jnp.floor((v + 0.5) * (1.0 / n))
    return q, v - q * n


def count_down(rows, cols=128):
    return lax.broadcasted_iota(jnp.int32, (rows, cols), 0).astype(F32)


def count_along(rows, cols):
    return lax.broadcasted_iota(jnp.int32, (rows, cols), 1).astype(F32)


def widen(v, cols):
    return jnp.concatenate([v] * -(-cols // 128), 1)[:, :cols]


def layout(rows, groups):
    bins = rows // SUB
    main = rows if bins % 4 else rows * 3 // 4
    return main, lambda g: ((0, main, g * main), (main, rows - main, groups * main + g * (rows - main)))


def pack(x, length):
    rows = x.shape[0]
    valid = x[:, :128] < 0.5 * SENTINEL
    along = jnp.where(valid, 1.0, 0.0).T[:8]
    pair = parts_of(count_down(rows), length)[0]
    pair_down = widen(pair, rows)
    pair_along, place = parts_of(count_along(8, rows), length)
    row = jnp.broadcast_to(pair_along[:1], (rows, rows))
    count = nn(along.astype(BF), (pair_down == row).astype(BF))
    upto = nn(along.astype(BF), (pair_down <= row).astype(BF))
    base = jnp.zeros((8, 1), F32)
    at = upto - count
    for b in range(1, rows // SUB):
        new = jnp.max(jnp.where(upto <= base + SUB, upto, 0.0), 1, keepdims=True)
        at = jnp.where(upto > new, upto - count - new + b * SUB, at)
        base = new
    at = jnp.where(along > 0, at + place, -1.0)
    pick = (widen(count_down(rows), rows) == jnp.broadcast_to(at[:1], (rows, rows))).astype(BF)
    packed = nn(pick, jnp.where(x < 0.5 * SENTINEL, x, 0.0).astype(BF))
    return packed, nn(pick, (pair + 1.0).astype(BF)) - 1.0, pick, jnp.max(at)


def forward_kernel(length, group, groups, x_ref, g1_ref, g2_ref, dmw_ref, dh_ref, *refs):
    qkv_h, out_h, up_h, oqkv_h, oout_h, oup_h = refs[:6]
    refs = refs[6:]
    if group:
        gsumi_ref, gaini_ref, flagi_ref = refs[:3]
        refs = refs[12:]
    a1t_h, qkv_o, p_o, do_o, a2t_h, du_h, ot_h, dattn_h, dux_h, gsum_ref, gain_ref, flag_ref = refs[:12]
    refs = refs[12:]
    tail = group == groups - 1
    if tail:
        send_ref = refs[0]
        refs = refs[1:]
    if group == 0:
        own_ref, pick_ref = refs[:2]
        refs = refs[2:]
    (x_s, id_s, qkv_s, p_s, o_s, h1_s, da2_s, a2_s, do_s, a1t_s, a2t_s, ot_s, du_s, dattn_s, wqkv_s, wout_s, wup_s,
     load_sem, early_sem, keep_sem) = refs
    rows, width = x_ref.shape
    hidden = wup_s.shape[1]
    pairs = rows // length
    before = gsum_ref.shape[0] - pairs
    half = width // 2
    tiles = half // 128
    main, where = layout(rows, groups)
    g1 = g1_ref[...].reshape(1, width)
    g2 = g2_ref[...].reshape(1, width)

    pieces = []
    for g, h in enumerate((qkv_h, oqkv_h)):
        for k in range(3):
            at = (3 * g + k) * half
            pieces.append((h.at[k], wqkv_s.at[:, at:at + half]))
    pieces += [(out_h, wout_s.at[:half]), (oout_h, wout_s.at[half:])]
    pieces += [(up_h, wup_s.at[:, :hidden // 2]), (oup_h, wup_s.at[:, hidden // 2:])]
    loads = [pltpu.make_async_copy(h, v, load_sem.at[i]) for i, (h, v) in enumerate(pieces)]
    for c in loads:
        c.start()
    early = []
    if group and tail:
        mine, other = slice(0, hidden // 2), slice(hidden // 2, hidden)
        for g in range(group):
            for i, (_, size, at) in enumerate(where(g)):
                if size:
                    cut = slice(at, at + size)
                    for j, (h, v, index) in enumerate((
                        (a2t_h, a2t_s, (slice(None), cut)), (dux_h, du_s.at[:, other], (cut,)),
                        (ot_h, ot_s, (slice(None), cut)), (dattn_h, dattn_s, (cut,)),
                    )):
                        early.append(pltpu.make_async_copy(h.at[index], v.at[index], early_sem.at[8 * g + 4 * i + j]))
        for c in early:
            c.start()

    packed, ids, pick, top = pack(x_ref[...].astype(F32), length)
    x_s[...] = packed
    id_s[...] = ids
    more = top >= main
    flag_ref[0, 0] = jnp.where(more, 1, 0)
    gsum_ref[before:, :] = jnp.zeros((pairs, hidden), F32)
    gain_ref[...] = jnp.zeros_like(gain_ref)
    if group:
        gsum_ref[:before, :] = gsumi_ref[...]
        gain_ref[...] = gaini_ref[...]
    if group == 0:
        own = own_ref.shape[0]
        pick_ref[...] = jnp.zeros_like(pick_ref)
        pick_ref[:, :own] = pick[:own, :own]

    def columns(g, kind, t):
        start = g * 3 * half + kind * half + t * 128
        return slice(start, start + 128)

    def keeps(part):
        start, size, at = where(group)[part]
        src, dst = slice(start, start + size), slice(at, at + size)
        every = slice(None)
        return [
            pltpu.make_async_copy(v.at[i], h.at[j], keep_sem.at[9 * part + k])
            for k, (v, h, i, j) in enumerate((
                (a1t_s, a1t_h, (every, src), (every, dst)),
                (qkv_s, qkv_o, (src,), (dst,)),
                (p_s, p_o, (slice(start // SUB, (start + size) // SUB),), (slice(at // SUB, (at + size) // SUB),)),
                (a2t_s, a2t_h, (every, dst), (every, dst)),
                (ot_s, ot_h, (every, dst), (every, dst)),
                (du_s, du_h, (dst, slice(0, hidden // 2)), (dst,)),
                (dattn_s, dattn_h, (dst,), (dst,)),
                (do_s, do_o, (src,), (dst,)),
                (du_s, dux_h, (dst, slice(hidden // 2, hidden)), (dst,)),
            )[:8 if tail else 9])
        ]

    def work(part):
        start, size, at = where(group)[part]
        here, there = slice(start, start + size), slice(at, at + size)
        store = keeps(part)
        x = x_s[here, :]
        a1 = (normalize(x)[0] * g1).astype(BF)
        a1t_s[:, here] = a1.T
        store[0].start()
        if part == 0:
            for c in loads[:6]:
                c.wait()
        qkv_s[here, :] = nn(a1, wqkv_s[...]).astype(BF)
        store[1].start()
        down = id_s[here, :]
        along = id_s[here, :].T[:1]

        def bin_of(s, carry):
            cut = pl.ds(pl.multiple_of(start + s * SUB, SUB), SUB)
            m = id_s[cut, :] == id_s[cut, :].T
            m = jnp.concatenate([m, m], 1)
            for g in range(2):
                for t in range(tiles):
                    q2 = qkv_s[cut, columns(g, 0, t)]
                    k2 = qkv_s[cut, columns(g, 1, t)]
                    v2 = qkv_s[cut, columns(g, 2, t)]
                    st = nt(k2, two_heads(q2)) * HEAD ** (-0.5)
                    st = jnp.where(m, st, -1000000000.0)
                    e = jnp.exp(st - jnp.max(st, 0, keepdims=True))
                    p = (e * (1.0 / jnp.sum(e, 0, keepdims=True))).astype(BF)
                    p_s[start // SUB + s, g * tiles + t] = p
                    col = g * half + t * 128
                    o_s[cut, col:col + 128] = tn(stack_heads(p), two_heads(v2)).astype(BF)
            return carry

        lax.fori_loop(0, size // SUB, bin_of, 0)
        store[2].start()
        if part == 0:
            for c in loads[6:8]:
                c.wait()
        h1 = x + nn(o_s[here, :], wout_s[...])
        h1_s[here, :] = h1
        a2_s[here, :] = (normalize(h1)[0] * g2).astype(BF)
        ot_s[:, there] = o_s[here, :].T
        a2t_s[:, there] = a2_s[here, :].T
        store[3].start()
        store[4].start()

        lanes = lax.broadcasted_iota(jnp.int32, (size, 2 * pairs), 1)
        lanes = jnp.where(lanes < pairs, lanes, lanes - pairs).astype(F32)
        spread = (jnp.broadcast_to(down[:, :1], lanes.shape) == lanes).astype(BF)
        subl = lax.broadcasted_iota(jnp.int32, (pairs, size), 0).astype(F32)
        gather = (jnp.broadcast_to(along, subl.shape) == subl).astype(BF)
        piece = 1024
        if part == 0:
            for c in loads[8:]:
                c.wait()
        def feed(j, carry):
            cols = pl.ds(pl.multiple_of(j * piece, piece), piece)
            u = nn(a2_s[here, :], wup_s[:, cols])
            cdf = 0.5 + 0.5 * lax.erf(u * 0.5 ** 0.5)
            g = (u * cdf).astype(BF)
            slope = cdf + u * (jnp.exp(-0.5 * u * u) * 0.3989422804014327)
            gsum_ref[before:, cols] += nn(gather, g)
            du = (nn(spread, dmw_ref[:, cols]) * slope).astype(BF)
            du_s[there, cols] = du
            da2_s[:size, :] += nt(du, wup_s[:, cols])
            return carry

        da2_s[:size, :] = jnp.zeros((size, width), F32)
        lax.fori_loop(0, hidden // piece, feed, 0)
        da2 = da2_s[:size, :]
        store[5].start()
        if not tail:
            store[8].start()
        xhat2, inv2 = normalize(h1_s[here, :])
        gain_ref[:1, :] += jnp.sum(da2 * xhat2, 0, keepdims=True)
        dh1 = nn(spread, dh_ref[...]) + normalize_pull(da2 * g2, xhat2, inv2)
        dattn_s[there, :] = dh1.astype(BF)
        store[6].start()
        do_s[here, :] = nt(dattn_s[there, :], wout_s[...]).astype(BF)
        store[7].start()
        if group == 0 and part == 0:
            own_ref[...] = dh1[:own_ref.shape[0]]

    work(0)
    if main < rows:
        pl.when(more)(lambda: work(1))

        @pl.when(jnp.logical_not(more))
        def _():
            start, size, at = where(group)[1]
            a1t_s[:, start:] = jnp.zeros((width, size), BF)
            a2t_s[:, at:at + size] = jnp.zeros((width, size), BF)
            ot_s[:, at:at + size] = jnp.zeros((width, size), BF)
            du_s[at:at + size, :] = jnp.zeros((size, hidden), BF)
            dattn_s[at:at + size, :] = jnp.zeros((size, width), BF)
            for c in keeps(1):
                c.start()
    if tail:
        for c in early:
            c.wait()
        whole = groups * main
        out = nn(ot_s[half:, :whole], dattn_s[:whole, :])
        send_ref[:width, :] = nn(a2t_s[:, :whole], du_s[:whole, hidden // 2:])
        send_ref[width:width + half // 2, :width] = out[:half // 2]
        send_ref[width:width + half // 2, width:] = out[half // 2:]
        if main < rows:
            any_more = more
            if group:
                any_more = jnp.logical_or(more, flagi_ref[0, 0] > 0)

            @pl.when(any_more)
            def _():
                out = nn(ot_s[half:, whole:], dattn_s[whole:, :])
                send_ref[:width, :] += nn(a2t_s[:, whole:], du_s[whole:, hidden // 2:])
                send_ref[width:width + half // 2, :width] += out[:half // 2]
                send_ref[width:width + half // 2, width:] += out[half // 2:]
            flag_ref[0, 0] = jnp.where(any_more, 1, 0)
        count = gsum_ref.shape[0]
        at = width + half // 2
        send_ref[at:, :] = jnp.zeros((send_ref.shape[0] - at, hidden // 2), F32)
        send_ref[at:at + count, :] = gsum_ref[:, hidden // 2:]
        send_ref[at + count:at + count + 8, :width] = gain_ref[...]
    for part in range(2 if main < rows else 1):
        for c in keeps(part):
            c.wait()


def text_forward(x, length, g1, g2, dmw, dh, weights, own, groups=1, group=0, before=None):
    rows, width = x.shape
    pairs = rows // length
    hidden = dmw.shape[1]
    half = width // 2
    total = rows * groups
    tail = group == groups - 1
    count = (group + 1) * pairs
    units = width // 128
    bins = rows // SUB
    whole = lambda a: pl.BlockSpec(memory_space=pltpu.VMEM)
    vmem = pl.BlockSpec(memory_space=pltpu.VMEM)
    smem = pl.BlockSpec(memory_space=pltpu.SMEM)
    hbm = pl.BlockSpec(memory_space=pl.ANY)
    shape = jax.ShapeDtypeStruct
    at_group = lambda cols: pl.BlockSpec((2 * pairs, cols), lambda i: (group, 0))
    every = lambda a: pl.BlockSpec(a.shape, lambda i: (0,) * len(a.shape))
    fixed = lambda *s: pl.BlockSpec(s, lambda i: (0,) * len(s))
    kept = () if before is None else tuple(before[9:12]) + tuple(before[:9])
    kept_specs = [] if before is None else [every(before[9]), every(before[10]), smem] + [hbm] * 9
    ends, end_specs = (), ()
    if tail:
        send = (width + half // 2 + -(-(count + 8) // 96) * 96, hidden // 2)
        ends, end_specs = (shape(send, F32),), (fixed(*send),)
    if group == 0:
        ends += (shape((own, width), F32), shape((own, 128), BF))
        end_specs += (fixed(own, width), fixed(own, 128))
    held = total
    return pl.pallas_call(
        functools.partial(forward_kernel, length, group, groups),
        grid=(1,),
        out_shape=(
            shape((width, total), BF), shape((total, 3 * width), BF), shape((total // SUB, units, SUB, 2 * SUB), BF),
            shape((total, width), BF), shape((width, total), BF), shape((total, hidden // 2), BF),
            shape((width, total), BF), shape((total, width), BF), shape((total, hidden // 2), BF),
            shape((count, hidden), F32), shape((8, width), F32),
            shape((1, 1), jnp.int32),
        ) + ends,
        in_specs=[every(x), every(g1), every(g2), at_group(hidden), at_group(width)] + [hbm] * 6 + kept_specs,
        out_specs=(hbm,) * 9 + (fixed(count, hidden), fixed(8, width), smem) + end_specs,
        scratch_shapes=[
            pltpu.VMEM((rows, width), F32),
            pltpu.VMEM((rows, 128), F32),
            pltpu.VMEM((rows, 3 * width), BF),
            pltpu.VMEM((bins, units, SUB, 2 * SUB), BF),
            pltpu.VMEM((rows, width), BF),
            pltpu.VMEM((rows, width), F32),
            pltpu.VMEM((rows, width), F32),
            pltpu.VMEM((rows, width), BF),
            pltpu.VMEM((rows, width), BF),
            pltpu.VMEM((width, rows), BF),
            pltpu.VMEM((width, held), BF),
            pltpu.VMEM((width, held), BF),
            pltpu.VMEM((held, hidden), BF),
            pltpu.VMEM((held, width), BF),
            pltpu.VMEM((width, 3 * width), BF),
            pltpu.VMEM((width, width), BF),
            pltpu.VMEM((width, hidden), BF),
            pltpu.SemaphoreType.DMA((10,)),
            pltpu.SemaphoreType.DMA((8 * groups,)),
            pltpu.SemaphoreType.DMA((18,)),
        ],
        input_output_aliases={} if before is None else {14 + i: i for i in range(9)},
        cost_estimate=cost(22),
        compiler_params=pltpu.CompilerParams(vmem_limit_bytes=58 * MIB),
        name="text_forward",
    )(x, g1, g2, dmw, dh, *weights, *kept)


def backward_kernel(
    whole, more_ref, x_ref, dh1_ref, pick_ref, g1_ref, qkv_h, p_h, do_h, a1t_h, wqkv_h, woqkv_h,
    own_ref, send_ref, small_ref, qkv_s, p_s, do_s, a1t_s, dqkv_s, wqkv_s, load_sem, row_sem,
):
    bins = p_s.shape[0]
    main = whole // SUB
    width = do_s.shape[1]
    half = width // 2
    tiles = half // 128

    def rows_of(b):
        return pl.ds(pl.multiple_of(b * SUB, SUB), SUB)

    def bin_loads(b):
        at = rows_of(b)
        return [
            pltpu.make_async_copy(qkv_h.at[at], qkv_s.at[at], row_sem.at[3 * b]),
            pltpu.make_async_copy(p_h.at[b], p_s.at[b], row_sem.at[3 * b + 1]),
            pltpu.make_async_copy(do_h.at[at], do_s.at[at], row_sem.at[3 * b + 2]),
        ]

    for b in range(main):
        for c in bin_loads(b):
            c.start()
    pieces = [(a1t_h, a1t_s)]
    for g, h in enumerate((wqkv_h, woqkv_h)):
        for k in range(3):
            at = (3 * g + k) * half
            pieces.append((h.at[k], wqkv_s.at[:, at:at + half]))
    loads = [pltpu.make_async_copy(h, v, load_sem.at[i]) for i, (h, v) in enumerate(pieces)]
    for c in loads:
        c.start()

    def columns(g, kind, t):
        start = g * 3 * half + kind * half + t * 128
        return slice(start, start + 128)

    def work(b):
        for c in bin_loads(b):
            c.wait()
        at = rows_of(b)
        for g in range(2):
            for t in range(tiles):
                q2 = qkv_s[at, columns(g, 0, t)]
                k2 = qkv_s[at, columns(g, 1, t)]
                v2 = qkv_s[at, columns(g, 2, t)]
                col = g * half + t * 128
                do2 = two_heads(do_s[at, col:col + 128])
                dp = nt(v2, do2)
                p_low = p_s[b, g * tiles + t]
                p = p_low.astype(F32)
                ds = (p * (dp - jnp.sum(dp * p, 0, keepdims=True))).astype(BF)
                dqkv_s[at, columns(g, 2, t)] = nn(p_low, do2).astype(BF)
                dqkv_s[at, columns(g, 1, t)] = (nn(ds, two_heads(q2)) * HEAD ** (-0.5)).astype(BF)
                dqkv_s[at, columns(g, 0, t)] = (
                    tn(stack_heads(ds), two_heads(k2)) * HEAD ** (-0.5)
                ).astype(BF)

    def step(b, carry):
        work(b)
        return carry

    lax.fori_loop(0, main, step, 0)
    for c in loads:
        c.wait()
    own = x_ref.shape[0]
    pick = pick_ref[:, :own].astype(F32)

    def unpack(v):
        return lax.dot_general(pick, v, (((0,), (0,)), ((), ())), precision=HIGHEST, preferred_element_type=F32)

    da1 = unpack(nt(dqkv_s[:own, :], wqkv_s[...]))
    x = x_ref[...].astype(F32)
    xhat, inv = normalize(jnp.where(x < 0.5 * SENTINEL, x, 0.0))
    small_ref[:own, :] = unpack(dh1_ref[...]) + normalize_pull(da1 * g1_ref[...].reshape(1, width), xhat, inv)

    def gradients(k, rows, add):
        gain = jnp.zeros((width, 128), F32)
        for g in (1, 0):
            at = (3 * g + k) * half
            grad = nn(a1t_s[:, rows], dqkv_s[rows, at:at + half])
            into = send_ref if g else own_ref
            cut = slice(k * width, (k + 1) * width)
            into[cut, :] = into[cut, :] + grad if add else grad
            for j in range(half // 128):
                piece = slice(j * 128, (j + 1) * 128)
                gain += grad[:, piece] * wqkv_s[:, at + j * 128:at + (j + 1) * 128].astype(F32)
        return jnp.sum(gain.T, 0, keepdims=True) / g1_ref[...].reshape(1, width)

    small_ref[own:, :] = jnp.zeros((small_ref.shape[0] - own, width), F32)
    small_ref[own:own + 1, :] = sum(gradients(k, slice(0, whole), False) for k in range(3))
    if main < bins:
        @pl.when(more_ref[0, 0] > 0)
        def _():
            for b in range(main, bins):
                for c in bin_loads(b):
                    c.start()
            lax.fori_loop(main, bins, step, 0)
            small_ref[own:own + 1, :] += sum(gradients(k, slice(whole, bins * SUB), True) for k in range(3))
    at = 3 * width
    send_ref[at:, :] = jnp.zeros((send_ref.shape[0] - at, half), F32)
    count = small_ref.shape[0]
    send_ref[at:at + count, :] = small_ref[:, :half]
    send_ref[at + count:at + 2 * count, :] = small_ref[:, half:]


def text_backward(whole, more, x, dh1, pick, g1, qkv, p, do, a1t, wqkv, oqkv):
    total, width = do.shape
    half = width // 2
    own = dh1.shape[0]
    count = own + 8
    every = lambda a: pl.BlockSpec(a.shape, lambda i: (0,) * len(a.shape))
    fixed = lambda *s: pl.BlockSpec(s, lambda i: (0,) * len(s))
    hbm = pl.BlockSpec(memory_space=pl.ANY)
    smem = pl.BlockSpec(memory_space=pltpu.SMEM)
    shape = jax.ShapeDtypeStruct
    bins, units = p.shape[:2]
    return pl.pallas_call(
        functools.partial(backward_kernel, whole),
        grid=(1,),
        out_shape=(
            shape((3 * width, half), F32), shape((3 * width + 2 * count, half), F32), shape((count, width), F32),
        ),
        in_specs=[smem, fixed(own, width), every(dh1), every(pick), every(g1)] + [hbm] * 6,
        out_specs=(fixed(3 * width, half), fixed(3 * width + 2 * count, half), fixed(count, width)),
        scratch_shapes=[
            pltpu.VMEM((total, 3 * width), BF),
            pltpu.VMEM((bins, units, SUB, 2 * SUB), BF),
            pltpu.VMEM((total, width), BF),
            pltpu.VMEM((width, total), BF),
            pltpu.VMEM((total, 3 * width), BF),
            pltpu.VMEM((width, 3 * width), BF),
            pltpu.SemaphoreType.DMA((7,)),
            pltpu.SemaphoreType.DMA((3 * bins,)),
        ],
        cost_estimate=cost(20),
        compiler_params=pltpu.CompilerParams(vmem_limit_bytes=58 * MIB),
        name="text_backward",
    )(more, x, dh1, pick, g1, qkv, p, do, a1t, wqkv, oqkv)


def feed_kernel(
    a2t_ref, du_ref, upi_ref, ot_ref, dattn_ref, outa_ref, outb_ref, gsum_ref, gsumi_ref, dm_ref, low_ref, gh_ref,
    up_ref, out_ref, down_ref, proj_ref,
):
    up_ref[...] = upi_ref[...] + nn(a2t_ref[...], du_ref[...])
    quarter = outa_ref.shape[0]
    out = nn(ot_ref[...], dattn_ref[...])
    out_ref[:quarter, :] = out[:quarter] + outa_ref[...]
    out_ref[quarter:, :] = out[quarter:] + outb_ref[...]
    mine = gsum_ref.shape[0]
    high, rest = halves(jnp.concatenate([gsum_ref[...], gsumi_ref[:mine]], 0))
    down_ref[...] = tn(high, dm_ref[...]) + tn(rest, dm_ref[...])
    proj_ref[...] = tn(low_ref[...], gh_ref[...])


def feed_grads(a2t, du, ot, dattn, got, gsum, dm, low, gh):
    width, total = a2t.shape
    hidden = du.shape[1]
    half = width // 2
    quarter = half // 2
    mine = gsum.shape[0]
    steps = 6
    tile = hidden // steps
    slim = width // steps
    rest = got.shape[0] - width - quarter
    whole = lambda a: pl.BlockSpec(a.shape, lambda i: (0,) * len(a.shape), pipeline_mode=pl.Buffered(1))
    shape = jax.ShapeDtypeStruct
    columns = lambda rows, cols, row=0, col=0: pl.BlockSpec((rows, cols), lambda i: (row, col + i))
    return pl.pallas_call(
        feed_kernel,
        grid=(steps,),
        out_shape=(
            shape((width, hidden), F32), shape((half, width), F32), shape((hidden, width), F32), shape((width, half), F32),
        ),
        in_specs=[
            whole(a2t), columns(total, tile), columns(width, tile),
            pl.BlockSpec((half, total), lambda i: (0, 0), pipeline_mode=pl.Buffered(1)), columns(total, slim),
            columns(quarter, slim, width // quarter), columns(quarter, slim, width // quarter, steps),
            columns(mine, tile), columns(rest, tile, (width + quarter) // rest), whole(dm), columns(low.shape[0], slim),
            whole(gh),
        ],
        out_specs=(
            columns(width, tile), columns(half, slim), pl.BlockSpec((tile, width), lambda i: (i, 0)),
            pl.BlockSpec((slim, half), lambda i: (i, 0)),
        ),
        cost_estimate=cost(9),
        compiler_params=pltpu.CompilerParams(vmem_limit_bytes=28 * MIB),
        name="feed_grads",
    )(a2t, du, got, ot, dattn, got, got, gsum, got, dm, low, gh)


def finish_kernel(
    own_ref, in_ref, small_ref, smalla_ref, smallb_ref, gain2_ref, gain2i_ref, loss_ref, temp_ref,
    qkv_ref, rows_ref, gain1o_ref, gain2o_ref, losso_ref, tempo_ref,
):
    qkv_ref[0] = own_ref[...] + in_ref[...]
    core = lax.axis_index("mp")
    own = rows_ref.shape[0] // 2
    half = gain1o_ref.shape[0]

    @pl.when(pl.program_id(0) == 0)
    def _():
        got = jnp.concatenate([smalla_ref[...], smallb_ref[...]], 1)
        rows_ref[:own, :] = jnp.where(core == 0, small_ref[:own], got[:own])
        rows_ref[own:, :] = jnp.where(core == 0, got[:own], small_ref[:own])
        losso_ref[...] = loss_ref[...]
        tempo_ref[...] = temp_ref[...]
        one = small_ref[own:own + 1, :] + got[own:own + 1, :]
        two = gain2_ref[:1, :] + gain2i_ref[:1, :2 * half]
        gain1o_ref[...] = jnp.where(core == 0, one[:, :half], one[:, half:]).reshape(half)
        gain2o_ref[...] = jnp.where(core == 0, two[:, :half], two[:, half:]).reshape(half)


def finish(own, got, small, gain2, other, at, loss, temp):
    count, width = small.shape
    rows = count - 8
    half = width // 2
    whole = lambda a: pl.BlockSpec(a.shape, lambda i: (0,) * len(a.shape), pipeline_mode=pl.Buffered(1))
    fixed = lambda *shape: pl.BlockSpec(shape, lambda i: (0,) * len(shape))
    piece = pl.BlockSpec((width, half), lambda i: (i, 0))
    start = 3 * width // count
    shape = jax.ShapeDtypeStruct
    return pl.pallas_call(
        finish_kernel,
        grid=(3,),
        out_shape=(shape((3, width, half), F32), shape((2 * rows, width), F32), shape((half,), F32), shape((half,), F32)) + (shape((1, 1), F32),) * 2,
        in_specs=[
            piece, piece, whole(small), pl.BlockSpec((count, half), lambda i: (start, 0)),
            pl.BlockSpec((count, half), lambda i: (start + 1, 0)), whole(gain2),
            pl.BlockSpec((8, other.shape[1]), lambda i: (at // 8, 0)), whole(loss), whole(temp),
        ],
        out_specs=(pl.BlockSpec((1, width, half), lambda i: (i, 0, 0)), fixed(2 * rows, width), fixed(half), fixed(half), fixed(1, 1), fixed(1, 1)),
        cost_estimate=cost(4),
        compiler_params=pltpu.CompilerParams(vmem_limit_bytes=24 * MIB),
        name="finish",
    )(own, got, small, got, got, gain2, other, loss, temp)


MESH = pl.DeviceIdType.MESH


def chip_grid(mesh):
    chips = mesh.devices.reshape(-1, mesh.shape["mp"])[:, 0]
    places = [getattr(d, "coords", None) for d in chips]
    if all(p is not None and len(p) == 3 for p in places):
        grid = tuple(len({p[i] for p in places}) for i in (2, 1, 0))
        if grid[0] * grid[1] * grid[2] == len(chips):
            return grid
    side = 1
    while (2 * side) ** 3 <= len(chips):
        side *= 2
    return (len(chips) // (side * side), side, side)


class Spread:
    def __init__(self, grid, place, core, block, send, recv, first):
        self.grid, self.place, self.core = grid, place, core
        self.block, self.send, self.recv = block, send, recv
        self.first = first
        self.sent = []
        zs, ys, xs = grid
        self.turn = ys == xs
        self.aorder = list(range(1, ys))
        zevents = [("z", d, None) for d in range(1, zs)]
        aevents = [[("a", d, a) for d in range(zs)] for a in self.aorder]
        self.pending = []
        for i in range(zs + len(aevents)):
            self.pending += zevents[i:i + 1]
            for j, events in enumerate(aevents):
                self.pending += events[i - j:i - j + 1] if i >= j else []

    def slot(self, kz, ka):
        return kz * self.grid[1] + ka

    def target(self, dz, da):
        zs, ys, xs = self.grid
        z, y, x = self.place
        dy, dx = (da * (1 - self.core), da * self.core) if self.turn else (da, 0)
        batch = (lax.rem(z + dz, zs) * ys + lax.rem(y + dy, ys)) * xs + lax.rem(x + dx, xs)
        return (batch, self.core)

    def copy(self, source, landing, to, when=None):
        index = len(self.sent)

        def make():
            return pltpu.make_async_remote_copy(
                src_ref=self.first if source is None else self.block(self.slot(*source)),
                dst_ref=self.block(self.slot(*landing)), send_sem=self.send.at[index],
                recv_sem=self.recv.at[self.slot(*landing)], device_id=self.target(*to), device_id_type=MESH,
            )

        if when is None:
            make().start()
        else:
            pl.when(when)(lambda: make().start())
        self.sent.append((make, when))

    def forward(self, source, kz, when=None):
        for d in self.aorder:
            self.copy(source, (kz, self.grid[1] - d), (0, d), when)

    def start(self):
        zs = self.grid[0]
        z = self.place[0]
        if zs > 1:
            self.copy(None, (zs - 1, 0), (1, 0), z < zs - 1)
            self.copy(None, (1, 0), (zs - 1, 0), z > 0)
        self.forward(None, 0)

    def arrive(self, slot):
        pltpu.make_async_remote_copy(
            src_ref=self.block(slot), dst_ref=self.block(slot), send_sem=self.send.at[0],
            recv_sem=self.recv.at[slot], device_id=self.target(1, 0), device_id_type=MESH,
        ).wait_recv()

    def sides(self, d):
        zs = self.grid[0]
        z = self.place[0]
        return [(d, z + d < zs, True), (zs - d, z - d >= 0, False)]

    def serve(self, count=1):
        zs = self.grid[0]
        z = self.place[0]
        for _ in range(min(count, len(self.pending))):
            kind, d, a = self.pending.pop(0)
            if kind == "a" and d == 0:
                self.arrive(self.slot(0, a))
                continue
            for kz, there, above in self.sides(d):
                slot = self.slot(kz, 0 if kind == "z" else a)
                pl.when(there)(lambda slot=slot: self.arrive(slot))
                if kind == "z":
                    if d + 1 < zs and above:
                        self.copy((kz, 0), (kz + 1, 0), (zs - 1, 0), there & (z > 0))
                    elif d + 1 < zs:
                        self.copy((kz, 0), (kz - 1, 0), (1, 0), there & (z < zs - 1))
                    self.forward((kz, 0), kz, there)

    def finish(self):
        self.serve(len(self.pending))
        for make, when in self.sent:
            if when is None:
                make().wait_send()
            else:
                pl.when(when)(lambda make=make: make().wait_send())

    @staticmethod
    def copies(grid):
        zs, ys, _ = grid
        return 4 * zs + 2 * zs * (ys - 1)


class Hops:
    def __init__(self, grid, place, core, block, send, recv, first):
        self.grid, self.place, self.core = grid, place, core
        self.block, self.send, self.recv = block, send, recv
        self.first = first
        self.sent = []
        zs, ys, xs = grid
        self.turn = ys == xs
        near = []
        for d in range(1, zs // 2 + 1):
            near += [d] if 2 * d == zs else [d, zs - d]
        self.zorder = near
        self.aorder = list(range(1, ys))
        self.border = list(range(1, xs))
        self.pending = [("z", k) for k in near]
        self.pending += [("a", a, k) for a in self.aorder for k in [0] + near]

    def slot(self, kz, ka, kb):
        zs, ys, xs = self.grid
        plain = (kz * ys + ka) * xs + kb
        if not self.turn:
            return plain
        other = (kz * ys + kb) * xs + ka
        return plain if plain == other else plain + self.core * (other - plain)

    def target(self, dz, da, db):
        zs, ys, xs = self.grid
        z, y, x = self.place
        if self.turn and da != db:
            dy = da + self.core * (db - da)
            dx = db + self.core * (da - db)
        else:
            dy, dx = da, db
        batch = (lax.rem(z + dz, zs) * ys + lax.rem(y + dy, ys)) * xs + lax.rem(x + dx, xs)
        return (batch, self.core)

    def copy(self, source, landing, to):
        index = len(self.sent)
        sent = pltpu.make_async_remote_copy(
            src_ref=source, dst_ref=self.block(landing), send_sem=self.send.at[index],
            recv_sem=self.recv.at[landing], device_id=to, device_id_type=MESH,
        )
        sent.start()
        self.sent.append(sent)

    def along_a(self, source, kz):
        ys = self.grid[1]
        for d in self.aorder:
            self.copy(source, self.slot(kz, ys - d, 0), self.target(0, d, 0))

    def along_b(self, source, kz, ka):
        xs = self.grid[2]
        for d in self.border:
            self.copy(source, self.slot(kz, ka, xs - d), self.target(0, 0, d))

    def start(self):
        zs = self.grid[0]
        self.along_b(self.first, 0, 0)
        self.along_a(self.first, 0)
        for d in self.zorder:
            self.copy(self.first, self.slot(zs - d, 0, 0), self.target(d, 0, 0))

    def arrive(self, slot):
        pltpu.make_async_remote_copy(
            src_ref=self.block(slot), dst_ref=self.block(slot), send_sem=self.send.at[0],
            recv_sem=self.recv.at[slot], device_id=self.target(1, 0, 0), device_id_type=MESH,
        ).wait_recv()

    def serve(self, count=1):
        for _ in range(min(count, len(self.pending))):
            event = self.pending.pop(0)
            if event[0] == "z":
                slot = self.slot(event[1], 0, 0)
                self.arrive(slot)
                self.along_b(self.block(slot), event[1], 0)
                self.along_a(self.block(slot), event[1])
            else:
                slot = self.slot(event[2], event[1], 0)
                self.arrive(slot)
                self.along_b(self.block(slot), event[2], event[1])

    def finish(self):
        self.serve(len(self.pending))
        for a in [0] + self.aorder:
            for b in self.border:
                for k in [0] + self.zorder:
                    self.arrive(self.slot(k, a, b))
        for sent in self.sent:
            sent.wait_send()

    @staticmethod
    def copies(grid):
        zs, ys, xs = grid
        return (zs - 1) + zs * (ys - 1) + zs * ys * (xs - 1)


def attend(qkv_ref, o_ref, start, ids, half):
    m = ids == ids.T
    m = jnp.concatenate([m, m], 1)
    rows = pl.ds(start, SUB)
    for t in range(half // 128):
        q2 = qkv_ref[rows, t * 128:(t + 1) * 128]
        k2 = qkv_ref[rows, half + t * 128:half + (t + 1) * 128]
        v2 = qkv_ref[rows, 2 * half + t * 128:2 * half + (t + 1) * 128]
        st = nt(k2, two_heads(q2)) * HEAD ** (-0.5)
        st = jnp.where(m, st, -1000000000.0)
        e = jnp.exp(st - jnp.max(st, 0, keepdims=True))
        p = e * (1.0 / jnp.sum(e, 0, keepdims=True))
        o_ref[rows, t * 128:(t + 1) * 128] = tn(stack_heads(p.astype(BF)), two_heads(v2)).astype(BF)


def front_kernel(
    grid,
    rows_ref, mask_ref, image_ref, g1_ref, g2_ref, temp_ref,
    iqkv_h, iout_h, iup_h, idown_h, tqkv_h, tout_h, tup_h, tdown_h, tproj_h,
    xg_ref, oqkv_h, oout_h, oup_h, dmw_ref, dh_ref, dm_ref, low_ref, gh_ref, loss_ref, temp_ref2,
    iqkv, iout, iup, idown, tqkv, tout, tup, tdown, proj,
    own_x, small, small_abs, payload, qkv_s, o_s, image_x, part, part_in, sums, sums_in,
    wsend_qkv, wsend_out, wsend_up, wsend_proj, wland_qkv, wland_out, wland_up, wland_proj,
    dmw_send, dmw_in, cos_s, tnorm_s, xg,
    load_sem, out_sem, x_send, x_recv, s_send, s_recv, c_send, c_recv, own_sem,
):
    zs, ys, xs = grid
    chips = zs * ys * xs
    planes = zs * ys
    batch, core = lax.axis_index("batch"), lax.axis_index("mp")
    place = (batch // (ys * xs), lax.rem(batch // xs, ys), lax.rem(batch, xs))
    partner = (batch, 1 - core)
    pairs, length = mask_ref.shape
    rows = pairs * length
    width = rows_ref.shape[1]
    half = width // 2
    hidden = tup.shape[1]
    hp = pairs // 2
    hr = hp * length
    total = chips * pairs
    mine = chips * hp
    patches = image_ref.shape[0] // pairs
    padded = image_x.shape[0] // pairs

    inside = total <= INSIDE

    loads = {}
    for i, (name, h, v) in enumerate((
        ("iqkv", iqkv_h, iqkv), ("tqkv", tqkv_h, tqkv), ("iout", iout_h, iout), ("tout", tout_h, tout),
        ("tup", tup_h, tup), ("iup", iup_h, iup), ("idown", idown_h, idown), ("tdown", tdown_h, tdown),
        ("proj", tproj_h, proj.at[core]),
    )):
        loads[name] = pltpu.make_async_copy(h, v, load_sem.at[i])
        if i < 3:
            loads[name].start()

    xg = xg if inside else xg_ref
    gather = Spread(grid, place, core, lambda s: xg.at[s], x_send, x_recv, own_x)
    peers = [partner]
    spread = Hops(grid, place, core, lambda s: small.at[core, s], s_send, s_recv, payload)
    peers += [spread.target(d, 0, 0) for d in range(1, zs)]
    peers += [spread.target(0, d, 0) for d in range(1, ys)]
    peers += [spread.target(0, 0, d) for d in range(1, xs)]
    barrier = pltpu.get_barrier_semaphore()
    for peer in peers:
        pl.semaphore_signal(barrier, inc=1, device_id=peer, device_id_type=MESH)

    mask = mask_ref[...].astype(F32)
    lane = count_along(rows, length)
    sub = parts_of(count_down(rows, length), length)[1]
    spread_mask = jnp.broadcast_to(mask[:, None, :], (pairs, length, length)).reshape(rows, length)
    valid = jnp.sum(jnp.where(lane == sub, spread_mask, 0.0), 1, keepdims=True)
    text_x = rows_ref[...].astype(F32)
    marked = jnp.where(valid > 0, text_x, SENTINEL)
    own_x[...] = jnp.where(core == 0, marked[:hr], marked[hr:])
    top = padded * pairs
    image_of, patch_of = parts_of(count_down(top), padded)
    image_ids = jnp.where(patch_of < patches, image_of, -1.0)
    place_of = jnp.where(patch_of < patches, patch_of * pairs + image_of, -1.0)
    reorder = (widen(place_of, patches * pairs) == count_along(top, patches * pairs)).astype(BF)
    image_x[...] = nn(reorder, image_ref[...])
    image_a1 = normalize(image_x[...])[0].astype(BF)
    pl.semaphore_wait(barrier, len(peers))
    gather.start()

    swaps = []

    def swap(source, landing, index):
        c = pltpu.make_async_remote_copy(
            src_ref=source, dst_ref=landing, send_sem=c_send.at[index], recv_sem=c_recv.at[index],
            device_id=partner, device_id_type=MESH,
        )
        c.start()
        swaps.append(c)
        return c

    def put(ref, cols, high, rest):
        size = mine // 2
        for g in range(2):
            ref[2 * g * size:(2 * g + 1) * size, cols] = high[g * size:(g + 1) * size]
            ref[(2 * g + 1) * size:(2 * g + 2) * size, cols] = rest[g * size:(g + 1) * size]

    def contrast():
        for s in range(chips):
            kz, ky, kx = s // (ys * xs), s // xs % ys, s % xs
            at = (lax.rem(place[0] + kz, zs) * ys + lax.rem(place[1] + ky, ys)) * xs + lax.rem(place[2] + kx, xs)
            small_abs[:, at] = small[:, s]
        low = small_abs[0, :, :, :width].reshape(total, width).astype(BF)
        low_ref[...] = low
        counts = small_abs[0, :, :, width:].reshape(total, 128)[:, :1]
        embed = jnp.concatenate([nn(low, proj[0]), nn(low, proj[1])], 1)
        inv = lax.rsqrt(jnp.sum(embed * embed, 1, keepdims=True) + NORM_EPS)
        tnorm_s[...] = embed * inv
        images = small_abs[1, :, :, :width].reshape(total, width)
        scale = jnp.exp(jnp.full((1, 1), temp_ref[0, 0], F32))
        cos_s[...] = three(nt, tnorm_s[...], images)
        logits = cos_s[...] * scale
        row_top = jnp.max(logits, 1, keepdims=True)
        row_lse = row_top + jnp.log(jnp.sum(jnp.exp(logits - row_top), 1, keepdims=True))
        col_top = jnp.max(logits, 0, keepdims=True)
        col_lse = col_top + jnp.log(jnp.sum(jnp.exp(logits - col_top), 0, keepdims=True))
        eye = (lax.broadcasted_iota(jnp.int32, (total, total), 0) == lax.broadcasted_iota(jnp.int32, (total, total), 1))
        eye = eye.astype(F32)
        pair_grad = (jnp.exp(logits - row_lse) + jnp.exp(logits - col_lse) - 2.0 * eye) * (0.5 / total)

        def everything(v):
            return jnp.sum(jnp.sum(v, 1, keepdims=True), 0, keepdims=True)

        loss = (everything(row_lse) + everything(col_lse) - 2.0 * everything(logits * eye)) * (0.5 / total)
        temp = scale * everything(pair_grad * cos_s[...])
        loss_ref[...] = loss
        temp_ref2[...] = temp
        grad_norm = scale * three(nn, pair_grad, images)
        tnorm = tnorm_s[...]
        grad_embed = ((grad_norm - tnorm * jnp.sum(tnorm * grad_norm, 1, keepdims=True)) * inv).astype(BF)
        gh_ref[...] = jnp.where(core == 0, grad_embed[:, :half], grad_embed[:, half:])
        dh = (nt(grad_embed[:, :half], proj[0]) + nt(grad_embed[:, half:], proj[1])) / counts
        dm = dh.astype(BF)

        r = count_along(8, total)
        here = core.astype(F32)
        owner = jnp.where(r < mine, here, 1.0 - here)
        k, i = parts_of(parts_of(r, mine)[1], hp)
        kb, rest = parts_of(k, planes)
        kz, ka = parts_of(rest, ys)
        ky, kx = (jnp.where(owner == 0, ka, kb), jnp.where(owner == 0, kb, ka)) if ys == xs else (ka, kb)
        z, y, x = (parts_of(v + p.astype(F32), n)[1] for v, p, n in zip((kz, ky, kx), place, grid))
        at = ((z * ys + y) * xs + x) * pairs + owner * hp + i
        pick = (jnp.broadcast_to(at[:1], (total, total)).T == count_along(total, total)).astype(BF)
        dm_sorted = nn(pick, dm).astype(BF)
        dm_ref[...] = dm_sorted
        dmw = nt(dm_sorted, tdown[...])
        dmw_send[...] = dmw[mine:]
        dmw_swap = swap(dmw_send, dmw_in, 8)
        dh_high, dh_low = halves(dh)
        put(dh_ref, slice(None), nn(pick[:mine], dh_high).astype(BF), nn(pick[:mine], dh_low).astype(BF))
        put(dmw_ref, slice(0, hidden), *halves(dmw[:mine]))
        return dmw_swap

    g1, g2 = g1_ref[...].reshape(1, width), g2_ref[...].reshape(1, width)
    loads["iqkv"].wait()
    for name in list(loads)[3:]:
        loads[name].start()
    for k in range(3):
        qkv_s[:, k * half:(k + 1) * half] = nn(image_a1, iqkv[k]).astype(BF)
    loads["tqkv"].wait()
    for k in range(3):
        wsend_qkv[k] = tqkv[k].astype(F32)
    qkv_swap = swap(wsend_qkv, wland_qkv, 3)
    loads["iout"].wait()
    parts = 2
    cut = top // parts
    image_swaps = []
    for i in range(parts):
        for s in range(i * cut // SUB, (i + 1) * cut // SUB):
            attend(qkv_s, o_s, s * SUB, image_ids[s * SUB:(s + 1) * SUB], half)
        at = pl.ds(i * cut, cut)
        part[at, :] = nn(o_s[at, :], iout[...])
        image_swaps.append(swap(part.at[at], part_in.at[at], i))

    a1 = (normalize(text_x)[0] * g1).astype(BF)
    for k in range(3):
        qkv_s[:rows, k * half:(k + 1) * half] = nn(a1, tqkv[k]).astype(BF)
    attend(qkv_s, o_s, 0, jnp.where(valid > 0, parts_of(count_down(rows), length)[0], -1.0), half)
    loads["tout"].wait()
    part[top:, :] = nn(o_s[:rows, :], tout[...])
    text_swap = swap(part.at[pl.ds(top, rows)], part_in.at[pl.ds(top, rows)], 5)
    gather.serve(2)

    loads["tup"].wait()
    up_cut = wsend_up.shape[0] // 4
    up_swaps = []

    def send_up(i):
        at = pl.ds(i * up_cut, up_cut)
        wsend_up[at, :] = tup[at, :].astype(F32)
        up_swaps.append(swap(wsend_up.at[at], wland_up.at[at], 9 + i))

    send_up(0)
    send_up(1)

    piece = 512
    loads["iup"].wait()
    mean_i, bars = [], []
    for i in range(parts):
        image_swaps[i].wait_recv()
        at = pl.ds(i * cut, cut)
        h1 = image_x[at, :] + (part[at, :] + part_in[at, :])
        a2 = normalize(h1)[0].astype(BF)
        mean_i.append(jnp.sum(h1.reshape(pairs // parts, padded, width), 1))
        bar = []
        for j in range(hidden // piece):
            u = nn(a2, iup[:, j * piece:(j + 1) * piece])
            g = (u * (0.5 + 0.5 * lax.erf(u * 0.5 ** 0.5))).astype(BF).astype(F32)
            bar.append(jnp.sum(g.reshape(pairs // parts, padded, piece), 1))
        bars.append(jnp.concatenate(bar, 1))
        gather.serve(1)
    mean_i = jnp.concatenate(mean_i, 0)
    bar = jnp.concatenate(halves(jnp.concatenate(bars, 0)), 0)
    loads["idown"].wait()
    low = nn(bar, idown[...])
    sums[pairs:, :] = low[:pairs] + low[pairs:]

    text_swap.wait_recv()
    h1 = text_x + (part[top:, :] + part_in[top:, :])
    a2 = (normalize(h1)[0] * g2).astype(BF)
    mean_h = jnp.sum((h1 * valid).reshape(pairs, length, width), 1)
    bars = []
    for j in range(hidden // piece):
        u = nn(a2, tup[:, j * piece:(j + 1) * piece])
        g = (u * (0.5 + 0.5 * lax.erf(u * 0.5 ** 0.5))).astype(BF).astype(F32) * valid
        bars.append(jnp.sum(g.reshape(pairs, length, piece), 1))
    bar = jnp.concatenate(halves(jnp.concatenate(bars, 1)), 0)
    loads["tdown"].wait()
    low = nn(bar, tdown[...])
    sums[:pairs, :] = low[:pairs] + low[pairs:]
    sums_swap = swap(sums, sums_in, 6)
    sums_swap.wait_recv()

    count = jnp.sum(mask, 1, keepdims=True)
    pooled = (mean_h + (sums[:pairs, :] + sums_in[:pairs, :])) / count
    e = (mean_i + (sums[pairs:, :] + sums_in[pairs:, :])) * (1.0 / patches)
    image_norm = e * lax.rsqrt(jnp.sum(e * e, 1, keepdims=True) + NORM_EPS)
    payload[:, :width] = jnp.where(core == 0, pooled, image_norm)
    payload[:, width:] = jnp.broadcast_to(count, (pairs, 128))
    spread.start()
    small[core, 0] = payload[...]
    loads["proj"].wait()
    wsend_proj[...] = proj[core].astype(F32)
    proj_swap = swap(wsend_proj, wland_proj, 2)
    wsend_out[...] = tout[...].astype(F32)
    out_swap = swap(wsend_out, wland_out, 4)
    send_up(2)
    send_up(3)
    oqkv, oout, oup = iqkv, iout, iup
    outs = []

    def hand_over(swapped, landed, held, out, index):
        swapped.wait_recv()
        held[...] = landed[...].astype(BF)
        outs.append(pltpu.make_async_copy(held, out, out_sem.at[index]))
        outs[-1].start()

    def hand_up(i):
        at = pl.ds(i * up_cut, up_cut)
        hand_over(up_swaps[i], wland_up.at[at], oup.at[at], oup_h.at[at], 2 + i)

    hand_over(qkv_swap, wland_qkv, oqkv, oqkv_h, 1)
    gather.serve(1)
    spread.serve(zs - 1)
    gather.serve(1)
    hand_up(0)
    hand_up(1)
    spread.serve(len(spread.pending))
    gather.serve(len(gather.pending))
    proj_swap.wait_recv()
    proj[1 - core] = wland_proj[...].astype(BF)
    hand_over(out_swap, wland_out, oout, oout_h, 0)
    spread.finish()
    both_swap = swap(small.at[core], small.at[core], 7)
    hand_up(2)
    both_swap.wait_recv()
    gather.serve(len(gather.pending))
    own_copy = pltpu.make_async_copy(own_x, xg_ref.at[0], own_sem.at[0])
    own_copy.start()
    if inside:
        store = pltpu.make_async_copy(xg.at[pl.ds(1, planes - 1)], xg_ref.at[pl.ds(1, planes - 1)], own_sem.at[1])
        store.start()
    if inside:
        dmw_swap = contrast()
    else:
        dmw_ref[...] = small[...]
        dm_ref[...] = proj[...]

    hand_up(3)
    if inside:
        dmw_swap.wait_recv()
        put(dmw_ref, slice(hidden, 2 * hidden), *halves(dmw_in[...]))
    gather.finish()
    own_copy.wait()
    if inside:
        store.wait()
    for s in swaps:
        s.wait_send()
    for o in outs:
        o.wait()


def front(grid, rows, mask, image, g1, g2, temp, weights):
    chips = grid[0] * grid[1] * grid[2]
    pairs, length = mask.shape
    width = rows.shape[1]
    half = width // 2
    iqkv, iout, iup, idown, tqkv, tout, tup, tdown, tproj = weights
    hidden = tup.shape[1]
    total = chips * pairs
    mine = total // 2
    patches = image.shape[0] // pairs
    padded = -(-patches // 64) * 64
    top = padded * pairs
    hr = pairs // 2 * length
    vmem = pl.BlockSpec(memory_space=pltpu.VMEM)
    hbm = pl.BlockSpec(memory_space=pl.ANY)
    shape = jax.ShapeDtypeStruct
    copies, hops = Spread.copies(grid), Hops.copies(grid)
    inside = total <= INSIDE
    if inside:
        ends = (
            shape((2 * mine, 2 * hidden), BF), shape((2 * mine, width), BF), shape((total, width), BF),
            shape((total, width), BF), shape((total, half), BF), shape((1, 1), F32), shape((1, 1), F32),
        )
    else:
        mine, total = 8, 128
        ends = (shape((2, chips, pairs, width + 128), F32),) + (shape((8, 128), F32),)
        ends += (shape((2,) + tproj.shape, BF),) + (shape((8, 128), F32),) * 4
    return pl.pallas_call(
        functools.partial(front_kernel, grid),
        out_shape=(
            shape((grid[0] * grid[1], hr, width), F32),
            shape(tqkv.shape, BF), shape(tout.shape, BF), shape(tup.shape, BF),
        ) + ends,
        in_specs=[vmem] * 5 + [pl.BlockSpec(memory_space=pltpu.SMEM)] + [hbm] * 9,
        out_specs=[hbm] * 4 + [vmem] * 7,
        scratch_shapes=[
            pltpu.VMEM(iqkv.shape, BF), pltpu.VMEM(iout.shape, BF), pltpu.VMEM(iup.shape, BF), pltpu.VMEM(idown.shape, BF),
            pltpu.VMEM(tqkv.shape, BF), pltpu.VMEM(tout.shape, BF), pltpu.VMEM(tup.shape, BF), pltpu.VMEM(tdown.shape, BF),
            pltpu.VMEM((2,) + tproj.shape, BF),
            pltpu.VMEM((hr, width), F32),
            pltpu.VMEM((2, chips, pairs, width + 128), F32),
            pltpu.VMEM((2, chips if inside else 1, pairs, width + 128), F32),
            pltpu.VMEM((pairs, width + 128), F32),
            pltpu.VMEM((top, 3 * half), BF),
            pltpu.VMEM((top, half), BF),
            pltpu.VMEM((top, width), F32),
            pltpu.VMEM((top + pairs * length, width), F32),
            pltpu.VMEM((top + pairs * length, width), F32),
            pltpu.VMEM((2 * pairs, width), F32),
            pltpu.VMEM((2 * pairs, width), F32),
            pltpu.VMEM(tqkv.shape, F32), pltpu.VMEM(tout.shape, F32), pltpu.VMEM(tup.shape, F32), pltpu.VMEM(tproj.shape, F32),
            pltpu.VMEM(tqkv.shape, F32), pltpu.VMEM(tout.shape, F32), pltpu.VMEM(tup.shape, F32), pltpu.VMEM(tproj.shape, F32),
            pltpu.VMEM((mine, hidden), F32), pltpu.VMEM((mine, hidden), F32),
            pltpu.VMEM((total, total), F32), pltpu.VMEM((total, width), F32),
            pltpu.VMEM((grid[0] * grid[1], hr, width) if inside else (1, 8, 128), F32),
            pltpu.SemaphoreType.DMA((9,)), pltpu.SemaphoreType.DMA((6,)),
            pltpu.SemaphoreType.DMA((copies,)), pltpu.SemaphoreType.DMA((grid[0] * grid[1],)),
            pltpu.SemaphoreType.DMA((hops,)), pltpu.SemaphoreType.DMA((chips,)),
            pltpu.SemaphoreType.DMA((13,)), pltpu.SemaphoreType.DMA((13,)), pltpu.SemaphoreType.DMA((2,)),
        ],
        cost_estimate=cost(40),
        compiler_params=pltpu.CompilerParams(collective_id=0, has_side_effects=True, vmem_limit_bytes=60 * MIB),
        name="front",
    )(rows, mask, image, g1, g2, temp, *weights)


def contrast_outside(grid, small, proj, log_temp, text_down):
    core = lax.axis_index("mp")
    here = lax.axis_index("batch")
    chips, pairs, width = small.shape[1], small.shape[2], small.shape[3] - 128
    half = width // 2
    zs, ys, xs = grid
    slots = jnp.arange(chips, dtype=jnp.int32)
    z, y, x = here // (ys * xs), here // xs % ys, here % xs
    offset = (z + slots // (ys * xs)) % zs * (ys * xs) + (y + slots // xs % ys) % ys * xs + (x + slots % xs) % xs
    slot_of = jnp.argsort(offset)
    total = chips * pairs
    low = small[0, :, :, :width].astype(BF)[slot_of].reshape(total, width)
    counts = small[0, :, :, width:width + 1][slot_of].reshape(total, 1)
    images = small[1, :, :, :width][slot_of].reshape(total, width)
    embed = jnp.concatenate([nn(low, proj[0]), nn(low, proj[1])], 1)
    inv = lax.rsqrt(jnp.sum(embed * embed, 1, keepdims=True) + NORM_EPS)
    text_norm = embed * inv
    scale = jnp.exp(log_temp)
    cosine = three(nt, text_norm, images)
    logits = scale * cosine
    text_lse = jax.nn.logsumexp(logits, 1, keepdims=True)
    image_lse = jax.nn.logsumexp(logits, 0, keepdims=True)
    eye = jnp.eye(total, dtype=F32)
    pair_grad = (jnp.exp(logits - text_lse) + jnp.exp(logits - image_lse) - 2.0 * eye) / (2.0 * total)
    loss = (jnp.sum(text_lse) + jnp.sum(image_lse) - 2.0 * jnp.sum(logits * eye)) / (2.0 * total)
    temp = scale * jnp.sum(pair_grad * cosine)
    grad_norm = scale * three(nn, pair_grad, images)
    grad_embed = ((grad_norm - text_norm * jnp.sum(text_norm * grad_norm, 1, keepdims=True)) * inv).astype(BF)
    grad_half = lax.dynamic_slice_in_dim(grad_embed, core * half, half, 1)
    dh = (nt(grad_embed[:, :half], proj[0]) + nt(grad_embed[:, half:], proj[1])) / counts
    hp = pairs // 2
    ka, kb = slots % ys, slots // (zs * ys)
    kz = slots // ys % zs

    def mine(v, c):
        ky, kx = (jnp.where(c == 0, ka, kb), jnp.where(c == 0, kb, ka)) if ys == xs else (ka, kb)
        chip = ((z + kz) % zs * ys + (y + ky) % ys) * xs + (x + kx) % xs
        w = v.reshape(chips, 2, hp, v.shape[-1])[chip]
        return lax.dynamic_index_in_dim(w, c, 1, keepdims=False).reshape(total // 2, v.shape[-1])

    def grouped(v):
        high, rest = halves(v)
        size = INSIDE // 8
        both = jnp.stack([high.reshape(-1, size, v.shape[1]), rest.reshape(-1, size, v.shape[1])], 1)
        return both.reshape(-1, v.shape[1])

    dm = jnp.concatenate([mine(dh, core), mine(dh, 1 - core)], 0).astype(BF)
    dmw = nt(dm, text_down)
    dmw_other = lax.ppermute(dmw[total // 2:], "mp", [(0, 1), (1, 0)])
    dmw = grouped(jnp.concatenate([dmw[:total // 2], dmw_other], 1))
    return dmw, grouped(mine(dh, core)), dm, low, grad_half, loss, temp


def last_axis(grid):
    zs, ys, xs = grid
    plans = []
    for d in range(1, xs):
        pairs = []
        for z in range(zs):
            for y in range(ys):
                for x in range(xs):
                    for core in range(2):
                        py, px = (y, (x + d) % xs) if core == 0 or ys != xs else ((y + d) % ys, x)
                        pairs.append((((z * ys + py) * xs + px) * 2 + core, ((z * ys + y) * xs + x) * 2 + core))
        plans.append(pairs)
    return plans


def per_device(
    grid, image_patches, text_rows, text_mask, image_qkv, image_out, image_up, image_down, text_gain_one, text_gain_two,
    text_qkv, text_out, text_up, text_down, text_proj, log_temp,
):
    pair_count, length, width = text_rows.shape
    half = width // 2
    hidden = text_up.shape[1]

    def swap(v):
        return lax.ppermute(v, "mp", [(0, 1), (1, 0)])

    patches = jnp.transpose(image_patches, (1, 0, 2)).reshape(-1, width)
    iqkv = jnp.transpose(image_qkv, (1, 0, 2))
    tqkv = jnp.transpose(text_qkv, (1, 0, 2))
    g1, g2 = text_gain_one, text_gain_two
    xg, oqkv, oout, oup, dmw, dh, dm, low, grad_half, loss, temp = front(
        grid, text_rows.reshape(-1, width), text_mask, patches, g1, g2, log_temp.reshape(1, 1),
        (iqkv, image_out, image_up, image_down, tqkv, text_out, text_up, text_down, text_proj),
    )
    own = pair_count // 2 * length
    if dm.ndim == 3:
        dmw, dh, dm, low, grad_half, loss, temp = contrast_outside(grid, dmw, dm, log_temp, text_down)
    weights = (tqkv, text_out, text_up, oqkv, oout, oup)
    total = dm.shape[0] // 2
    near = xg.reshape(-1, width)
    plans = last_axis(grid)
    if dm.shape[0] <= INSIDE:
        far = [lax.ppermute(near, ("batch", "mp"), pairs) for pairs in plans]
        before = None
        groups = [near] + far
        for g, x in enumerate(groups):
            before = text_forward(x, length, g1, g2, dmw, dh, weights, own, len(groups), g, before)
            if g == 0:
                dh1, pick = before[-2:]
        a1t, qkv, p, do, a2t, du, ot, dattn, _, gsum, gain2, more, send = before[:13]
        got = swap(send)
        whole = layout(near.shape[0], len(groups))[0] * len(groups)
        qkv_m, qkv_o, small = text_backward(whole, more, near, dh1, pick, g1, qkv, p, do, a1t, tqkv, oqkv)
        qkv_in = swap(qkv_o)
        grad_up, grad_out, grad_down, grad_proj = feed_grads(a2t, du, ot, dattn, got, gsum, dm, low, grad_half)
        qkv_in, grad_up, grad_out, grad_down, grad_proj = lax.optimization_barrier(
            (qkv_in, grad_up, grad_out, grad_down, grad_proj))
        other, at = got, width + half // 2 + gsum.shape[0]
    else:
        size = INSIDE // 8
        groups = total // size

        def one(carry, items):
            sums, first = carry
            g, x, dmw, dh = items
            a1t, qkv, p, do, a2t, du, ot, dattn, _, gsum, gain2, more, send, dh1, pick = text_forward(
                x, length, g1, g2, dmw, dh, weights, own)
            qkv_m, qkv_o, small = text_backward(x.shape[0], more, x, dh1, pick, g1, qkv, p, do, a1t, tqkv, oqkv)
            new = (send, gain2, qkv_m, qkv_o, small[own:], nn(a2t, du), nn(ot[:half], dattn))
            return (tuple(x + y for x, y in zip(sums, new)), jnp.where(g == 0, small[:own], first)), gsum

        zero = lambda *shape: jnp.zeros(shape, F32)
        at = width + half // 2 + size
        sums = (zero(width + half // 2 + 96, hidden), zero(8, width), zero(3 * width, half),
                zero(3 * width + 2 * own + 16, half), zero(8, width), zero(width, hidden), zero(half, width))
        split = lambda v: v.reshape(groups, -1, v.shape[-1])
        planes = [near] + [lax.ppermute(near, ("batch", "mp"), pairs) for pairs in plans]
        planes = [jnp.where(x > 0.5 * SENTINEL, SENTINEL, x).astype(BF) for x in planes]
        (sums, first), gsum = lax.scan(
            one, (sums, zero(own, width)),
            (jnp.arange(groups), split(jnp.concatenate(planes, 0)), split(dmw), split(dh)))
        gsum = gsum.reshape(-1, gsum.shape[-1])
        send, gain2, qkv_m, qkv_o, gain1, up_m, out_m = sums
        small = jnp.concatenate([first, gain1], 0)
        qkv_o = jnp.concatenate([qkv_o[:3 * width], small[:, :half], small[:, half:]], 0)
        qkv_in, got = swap(qkv_o), swap(send)
        grad_up = up_m + got[:width]
        folded = got[width:width + half // 2]
        grad_out = out_m + jnp.concatenate([folded[:, :width], folded[:, width:]], 0)
        high, rest = halves(jnp.concatenate([gsum[:, :hidden], swap(gsum[:, hidden:])], 0))
        grad_down = tn(high, dm) + tn(rest, dm)
        grad_proj = tn(low, grad_half)
        other = got
    grad_qkv, grad_rows, gain1, gain2, loss, temp = finish(
        qkv_m, qkv_in, small, gain2, other, at, loss.reshape(1, 1), temp.reshape(1, 1))
    return (loss.reshape(()), grad_rows.reshape(pair_count, length, width), gain1, gain2,
            jnp.transpose(grad_qkv, (1, 0, 2)), grad_out, grad_up, grad_down, grad_proj, temp.reshape(()))


def solution(mesh):
    return jax.shard_map(
        functools.partial(per_device, chip_grid(mesh)),
        mesh=mesh,
        in_specs=(
            P("batch", None, None), P("batch", None, None), P("batch", None), P(None, None, "mp"), P("mp", None),
            P(None, "mp"), P("mp", None), P(), P(), P(None, None, "mp"), P("mp", None), P(None, "mp"), P("mp", None),
            P(None, "mp"), P(),
        ),
        out_specs=(
            P(), P("batch", None, None), P("mp"), P("mp"), P(None, None, "mp"), P("mp", None), P(None, "mp"),
            P("mp", None), P(None, "mp"), P(),
        ),
        check_vma=False,
    )
```

```python
import functools
import jax
import jax.numpy as jnp
from jax import lax
from jax.experimental import pallas as pl
from jax.experimental.pallas import tpu as pltpu
from jax.sharding import PartitionSpec as P

HEAD = 64
LN_EPS = 1e-06
NORM_EPS = 1e-06
HIGHEST = lax.Precision.HIGHEST
BF = jnp.bfloat16
F32 = jnp.float32
MIB = 2**20


def cost(microseconds):
    return pl.CostEstimate(flops=int(microseconds * 1e9), bytes_accessed=0, transcendentals=0)


def nn(a, b):
    return lax.dot_general(a, b, (((1,), (0,)), ((), ())), preferred_element_type=F32)


def nt(a, b):
    return lax.dot_general(a, b, (((1,), (1,)), ((), ())), preferred_element_type=F32)


def tn(a, b):
    return lax.dot_general(a, b, (((0,), (0,)), ((), ())), preferred_element_type=F32)


def normalize(rows):
    center = rows - jnp.mean(rows, -1, keepdims=True)
    inv = lax.rsqrt(jnp.mean(center * center, -1, keepdims=True) + LN_EPS)
    return center * inv, inv


def normalize_pull(grad, xhat, inv):
    return inv * (
        grad - jnp.mean(grad, -1, keepdims=True) - xhat * jnp.mean(grad * xhat, -1, keepdims=True)
    )


def two_heads(tile):
    first = lax.broadcasted_iota(jnp.int32, tile.shape, 1) < HEAD
    zero = jnp.zeros_like(tile)
    return jnp.concatenate([jnp.where(first, tile, zero), jnp.where(first, zero, tile)], 0)


def stack_heads(pair):
    half = pair.shape[1] // 2
    return jnp.concatenate([pair[:, :half], pair[:, half:]], 0)


def halves(values):
    high = values.astype(BF)
    return high, (values - high.astype(F32)).astype(BF)


SENTINEL = 1e30
SUB = 128
INSIDE = 128


def three(form, a, b):
    (ah, al), (bh, bl) = halves(a), halves(b)
    return form(ah, bh) + (form(ah, bl) + form(al, bh))


def parts_of(v, n):
    q = jnp.floor((v + 0.5) * (1.0 / n))
    return q, v - q * n


def count_down(rows, cols=128):
    return lax.broadcasted_iota(jnp.int32, (rows, cols), 0).astype(F32)


def count_along(rows, cols):
    return lax.broadcasted_iota(jnp.int32, (rows, cols), 1).astype(F32)


def widen(v, cols):
    return jnp.concatenate([v] * -(-cols // 128), 1)[:, :cols]


def layout(rows, groups):
    bins = rows // SUB
    main = rows if bins % 4 else rows * 3 // 4
    return main, lambda g: ((0, main, g * main), (main, rows - main, groups * main + g * (rows - main)))


def pack(x, length):
    rows = x.shape[0]
    valid = x[:, :128] < 0.5 * SENTINEL
    along = jnp.where(valid, 1.0, 0.0).T[:8]
    pair = parts_of(count_down(rows), length)[0]
    pair_down = widen(pair, rows)
    pair_along, place = parts_of(count_along(8, rows), length)
    row = jnp.broadcast_to(pair_along[:1], (rows, rows))
    count = nn(along.astype(BF), (pair_down == row).astype(BF))
    upto = nn(along.astype(BF), (pair_down <= row).astype(BF))
    base = jnp.zeros((8, 1), F32)
    at = upto - count
    for b in range(1, rows // SUB):
        new = jnp.max(jnp.where(upto <= base + SUB, upto, 0.0), 1, keepdims=True)
        at = jnp.where(upto > new, upto - count - new + b * SUB, at)
        base = new
    at = jnp.where(along > 0, at + place, -1.0)
    pick = (widen(count_down(rows), rows) == jnp.broadcast_to(at[:1], (rows, rows))).astype(BF)
    packed = nn(pick, jnp.where(x < 0.5 * SENTINEL, x, 0.0).astype(BF))
    return packed, nn(pick, (pair + 1.0).astype(BF)) - 1.0, pick, jnp.max(at)


def forward_kernel(length, group, groups, x_ref, g1_ref, g2_ref, dmw_ref, dh_ref, *refs):
    qkv_h, out_h, up_h, oqkv_h, oout_h, oup_h = refs[:6]
    refs = refs[6:]
    if group:
        gsumi_ref, gaini_ref, flagi_ref = refs[:3]
        refs = refs[12:]
    a1t_h, qkv_o, p_o, do_o, a2t_h, du_h, ot_h, dattn_h, dux_h, gsum_ref, gain_ref, flag_ref = refs[:12]
    refs = refs[12:]
    tail = group == groups - 1
    if tail:
        send_h = refs[0]
        refs = refs[1:]
    if group == 0:
        own_ref, pick_ref = refs[:2]
        refs = refs[2:]
    (x_s, id_s, qkv_s, p_s, o_s, h1_s, da2_s, a2_s, do_s, a1t_s, a2t_s, ot_s, du_s, dattn_s, wqkv_s, wout_s, wup_s,
     load_sem, early_sem, keep_sem) = refs[:20]
    if tail:
        send_ref, send_sem = refs[20:]
    rows, width = x_ref.shape
    hidden = wup_s.shape[1]
    pairs = rows // length
    before = gsum_ref.shape[0] - pairs
    half = width // 2
    tiles = half // 128
    main, where = layout(rows, groups)
    g1 = g1_ref[...].reshape(1, width)
    g2 = g2_ref[...].reshape(1, width)

    pieces = []
    for g, h in enumerate((qkv_h, oqkv_h)):
        for k in range(3):
            at = (3 * g + k) * half
            pieces.append((h.at[k], wqkv_s.at[:, at:at + half]))
    pieces += [(out_h, wout_s.at[:half]), (oout_h, wout_s.at[half:])]
    pieces += [(up_h, wup_s.at[:, :hidden // 2]), (oup_h, wup_s.at[:, hidden // 2:])]
    loads = [pltpu.make_async_copy(h, v, load_sem.at[i]) for i, (h, v) in enumerate(pieces)]
    for c in loads:
        c.start()
    early = []
    if group and tail:
        mine, other = slice(0, hidden // 2), slice(hidden // 2, hidden)
        for g in range(group):
            for i, (_, size, at) in enumerate(where(g)):
                if size:
                    cut = slice(at, at + size)
                    for j, (h, v, index) in enumerate((
                        (a2t_h, a2t_s, (slice(None), cut)), (dux_h, du_s.at[:, other], (cut,)),
                        (ot_h, ot_s, (slice(None), cut)), (dattn_h, dattn_s, (cut,)),
                    )):
                        early.append(pltpu.make_async_copy(h.at[index], v.at[index], early_sem.at[8 * g + 4 * i + j]))
        for c in early:
            c.start()

    packed, ids, pick, top = pack(x_ref[...].astype(F32), length)
    x_s[...] = packed
    id_s[...] = ids
    more = top >= main
    flag_ref[0, 0] = jnp.where(more, 1, 0)
    gsum_ref[before:, :] = jnp.zeros((pairs, hidden), F32)
    gain_ref[...] = jnp.zeros_like(gain_ref)
    if group:
        gsum_ref[:before, :] = gsumi_ref[...]
        gain_ref[...] = gaini_ref[...]
    if group == 0:
        own = own_ref.shape[0]
        pick_ref[...] = jnp.zeros_like(pick_ref)
        pick_ref[:, :own] = pick[:own, :own]

    def columns(g, kind, t):
        start = g * 3 * half + kind * half + t * 128
        return slice(start, start + 128)

    def keeps(part):
        start, size, at = where(group)[part]
        src, dst = slice(start, start + size), slice(at, at + size)
        every = slice(None)
        return [
            pltpu.make_async_copy(v.at[i], h.at[j], keep_sem.at[9 * part + k])
            for k, (v, h, i, j) in enumerate((
                (a1t_s, a1t_h, (every, src), (every, dst)),
                (qkv_s, qkv_o, (src,), (dst,)),
                (p_s, p_o, (slice(start // SUB, (start + size) // SUB),), (slice(at // SUB, (at + size) // SUB),)),
                (a2t_s, a2t_h, (every, dst), (every, dst)),
                (ot_s, ot_h, (every, dst), (every, dst)),
                (du_s, du_h, (dst, slice(0, hidden // 2)), (dst,)),
                (dattn_s, dattn_h, (dst,), (dst,)),
                (do_s, do_o, (src,), (dst,)),
                (du_s, dux_h, (dst, slice(hidden // 2, hidden)), (dst,)),
            )[:8 if tail else 9])
        ]

    def work(part):
        start, size, at = where(group)[part]
        here, there = slice(start, start + size), slice(at, at + size)
        store = keeps(part)
        x = x_s[here, :]
        a1 = (normalize(x)[0] * g1).astype(BF)
        a1t_s[:, here] = a1.T
        store[0].start()
        if part == 0:
            for c in loads[:6]:
                c.wait()
        qkv_s[here, :] = nn(a1, wqkv_s[...]).astype(BF)
        store[1].start()
        down = id_s[here, :]
        along = id_s[here, :].T[:1]

        def bin_of(s, carry):
            cut = pl.ds(pl.multiple_of(start + s * SUB, SUB), SUB)
            m = id_s[cut, :] == id_s[cut, :].T
            m = jnp.concatenate([m, m], 1)
            for g in range(2):
                for t in range(tiles):
                    q2 = qkv_s[cut, columns(g, 0, t)]
                    k2 = qkv_s[cut, columns(g, 1, t)]
                    v2 = qkv_s[cut, columns(g, 2, t)]
                    st = nt(k2, two_heads(q2)) * HEAD ** (-0.5)
                    st = jnp.where(m, st, -1000000000.0)
                    e = jnp.exp(st - jnp.max(st, 0, keepdims=True))
                    p = (e * (1.0 / jnp.sum(e, 0, keepdims=True))).astype(BF)
                    p_s[start // SUB + s, g * tiles + t] = p
                    col = g * half + t * 128
                    o_s[cut, col:col + 128] = tn(stack_heads(p), two_heads(v2)).astype(BF)
            return carry

        lax.fori_loop(0, size // SUB, bin_of, 0)
        store[2].start()
        if part == 0:
            for c in loads[6:8]:
                c.wait()
        h1 = x + nn(o_s[here, :], wout_s[...])
        h1_s[here, :] = h1
        a2_s[here, :] = (normalize(h1)[0] * g2).astype(BF)
        ot_s[:, there] = o_s[here, :].T
        a2t_s[:, there] = a2_s[here, :].T
        store[3].start()
        store[4].start()

        lanes = lax.broadcasted_iota(jnp.int32, (size, 2 * pairs), 1)
        lanes = jnp.where(lanes < pairs, lanes, lanes - pairs).astype(F32)
        spread = (jnp.broadcast_to(down[:, :1], lanes.shape) == lanes).astype(BF)
        subl = lax.broadcasted_iota(jnp.int32, (pairs, size), 0).astype(F32)
        gather = (jnp.broadcast_to(along, subl.shape) == subl).astype(BF)
        piece = 1024
        if part == 0:
            for c in loads[8:]:
                c.wait()
        def feed(j, carry):
            cols = pl.ds(pl.multiple_of(j * piece, piece), piece)
            u = nn(a2_s[here, :], wup_s[:, cols])
            cdf = 0.5 + 0.5 * lax.erf(u * 0.5 ** 0.5)
            g = (u * cdf).astype(BF)
            slope = cdf + u * (jnp.exp(-0.5 * u * u) * 0.3989422804014327)
            gsum_ref[before:, cols] += nn(gather, g)
            du = (nn(spread, dmw_ref[:, cols]) * slope).astype(BF)
            du_s[there, cols] = du
            da2_s[:size, :] += nt(du, wup_s[:, cols])
            return carry

        da2_s[:size, :] = jnp.zeros((size, width), F32)
        lax.fori_loop(0, hidden // piece, feed, 0)
        da2 = da2_s[:size, :]
        store[5].start()
        if not tail:
            store[8].start()
        xhat2, inv2 = normalize(h1_s[here, :])
        gain_ref[:1, :] += jnp.sum(da2 * xhat2, 0, keepdims=True)
        dh1 = nn(spread, dh_ref[...]) + normalize_pull(da2 * g2, xhat2, inv2)
        dattn_s[there, :] = dh1.astype(BF)
        store[6].start()
        do_s[here, :] = nt(dattn_s[there, :], wout_s[...]).astype(BF)
        store[7].start()
        if group == 0 and part == 0:
            own_ref[...] = dh1[:own_ref.shape[0]]

    work(0)
    if main < rows:
        pl.when(more)(lambda: work(1))

        @pl.when(jnp.logical_not(more))
        def _():
            start, size, at = where(group)[1]
            a1t_s[:, start:] = jnp.zeros((width, size), BF)
            a2t_s[:, at:at + size] = jnp.zeros((width, size), BF)
            ot_s[:, at:at + size] = jnp.zeros((width, size), BF)
            du_s[at:at + size, :] = jnp.zeros((size, hidden), BF)
            dattn_s[at:at + size, :] = jnp.zeros((size, width), BF)
            for c in keeps(1):
                c.start()
    if tail:
        for c in early:
            c.wait()
        whole = groups * main
        at = width + half // 2
        blocks = ((0, half), (half, half), (width, half // 2), (at, send_ref.shape[0] - at))
        leave = [
            pltpu.make_async_copy(send_ref.at[pl.ds(i, n)], send_h.at[pl.ds(i, n)], send_sem.at[k])
            for k, (i, n) in enumerate(blocks)
        ]
        for i in range(2):
            send_ref[i * half:(i + 1) * half, :] = nn(a2t_s[i * half:(i + 1) * half, :whole], du_s[:whole, hidden // 2:])
            leave[i].start()
        out = nn(ot_s[half:, :whole], dattn_s[:whole, :])
        send_ref[width:at, :width] = out[:half // 2]
        send_ref[width:at, width:] = out[half // 2:]
        leave[2].start()
        if main < rows:
            any_more = more
            if group:
                any_more = jnp.logical_or(more, flagi_ref[0, 0] > 0)

            @pl.when(any_more)
            def _():
                for c in leave[:3]:
                    c.wait()
                out = nn(ot_s[half:, whole:], dattn_s[whole:, :])
                send_ref[:width, :] += nn(a2t_s[:, whole:], du_s[whole:, hidden // 2:])
                send_ref[width:at, :width] += out[:half // 2]
                send_ref[width:at, width:] += out[half // 2:]
                for c in leave[:3]:
                    c.start()

            flag_ref[0, 0] = jnp.where(any_more, 1, 0)
        count = gsum_ref.shape[0]
        send_ref[at:, :] = jnp.zeros((send_ref.shape[0] - at, hidden // 2), F32)
        send_ref[at:at + count, :] = gsum_ref[:, hidden // 2:]
        send_ref[at + count:at + count + 8, :width] = gain_ref[...]
        leave[3].start()
        for c in leave:
            c.wait()
    for part in range(2 if main < rows else 1):
        for c in keeps(part):
            c.wait()


def text_forward(x, length, g1, g2, dmw, dh, weights, own, groups=1, group=0, before=None):
    rows, width = x.shape
    pairs = rows // length
    hidden = dmw.shape[1]
    half = width // 2
    total = rows * groups
    tail = group == groups - 1
    count = (group + 1) * pairs
    units = width // 128
    bins = rows // SUB
    whole = lambda a: pl.BlockSpec(memory_space=pltpu.VMEM)
    vmem = pl.BlockSpec(memory_space=pltpu.VMEM)
    smem = pl.BlockSpec(memory_space=pltpu.SMEM)
    hbm = pl.BlockSpec(memory_space=pl.ANY)
    shape = jax.ShapeDtypeStruct
    at_group = lambda cols: pl.BlockSpec((2 * pairs, cols), lambda i: (group, 0))
    every = lambda a: pl.BlockSpec(a.shape, lambda i: (0,) * len(a.shape))
    fixed = lambda *s: pl.BlockSpec(s, lambda i: (0,) * len(s))
    kept = () if before is None else tuple(before[9:12]) + tuple(before[:9])
    kept_specs = [] if before is None else [every(before[9]), every(before[10]), smem] + [hbm] * 9
    ends, end_specs = (), ()
    if tail:
        send = (width + half // 2 + -(-(count + 8) // 96) * 96, hidden // 2)
        ends, end_specs = (shape(send, F32),), (hbm,)
    if group == 0:
        ends += (shape((own, width), F32), shape((own, 128), BF))
        end_specs += (fixed(own, width), fixed(own, 128))
    held = total
    return pl.pallas_call(
        functools.partial(forward_kernel, length, group, groups),
        grid=(1,),
        out_shape=(
            shape((width, total), BF), shape((total, 3 * width), BF), shape((total // SUB, units, SUB, 2 * SUB), BF),
            shape((total, width), BF), shape((width, total), BF), shape((total, hidden // 2), BF),
            shape((width, total), BF), shape((total, width), BF), shape((total, hidden // 2), BF),
            shape((count, hidden), F32), shape((8, width), F32),
            shape((1, 1), jnp.int32),
        ) + ends,
        in_specs=[every(x), every(g1), every(g2), at_group(hidden), at_group(width)] + [hbm] * 6 + kept_specs,
        out_specs=(hbm,) * 9 + (fixed(count, hidden), fixed(8, width), smem) + end_specs,
        scratch_shapes=[
            pltpu.VMEM((rows, width), F32),
            pltpu.VMEM((rows, 128), F32),
            pltpu.VMEM((rows, 3 * width), BF),
            pltpu.VMEM((bins, units, SUB, 2 * SUB), BF),
            pltpu.VMEM((rows, width), BF),
            pltpu.VMEM((rows, width), F32),
            pltpu.VMEM((rows, width), F32),
            pltpu.VMEM((rows, width), BF),
            pltpu.VMEM((rows, width), BF),
            pltpu.VMEM((width, rows), BF),
            pltpu.VMEM((width, held), BF),
            pltpu.VMEM((width, held), BF),
            pltpu.VMEM((held, hidden), BF),
            pltpu.VMEM((held, width), BF),
            pltpu.VMEM((width, 3 * width), BF),
            pltpu.VMEM((width, width), BF),
            pltpu.VMEM((width, hidden), BF),
            pltpu.SemaphoreType.DMA((10,)),
            pltpu.SemaphoreType.DMA((8 * groups,)),
            pltpu.SemaphoreType.DMA((18,)),
        ] + ([pltpu.VMEM(send, F32), pltpu.SemaphoreType.DMA((4,))] if tail else []),
        input_output_aliases={} if before is None else {14 + i: i for i in range(9)},
        cost_estimate=cost(22),
        compiler_params=pltpu.CompilerParams(vmem_limit_bytes=58 * MIB),
        name="text_forward",
    )(x, g1, g2, dmw, dh, *weights, *kept)


def backward_kernel(
    whole, more_ref, x_ref, dh1_ref, pick_ref, g1_ref, qkv_h, p_h, do_h, a1t_h, wqkv_h, woqkv_h,
    own_h, send_h, small_ref, qkv_s, p_s, do_s, a1t_s, dqkv_s, wqkv_s, own_ref, send_ref, load_sem, row_sem, out_sem,
):
    bins = p_s.shape[0]
    main = whole // SUB
    width = do_s.shape[1]
    half = width // 2
    tiles = half // 128

    def rows_of(b):
        return pl.ds(pl.multiple_of(b * SUB, SUB), SUB)

    def bin_loads(b):
        at = rows_of(b)
        return [
            pltpu.make_async_copy(qkv_h.at[at], qkv_s.at[at], row_sem.at[3 * b]),
            pltpu.make_async_copy(p_h.at[b], p_s.at[b], row_sem.at[3 * b + 1]),
            pltpu.make_async_copy(do_h.at[at], do_s.at[at], row_sem.at[3 * b + 2]),
        ]

    for b in range(main):
        for c in bin_loads(b):
            c.start()
    pieces = [(a1t_h, a1t_s)]
    for g, h in enumerate((wqkv_h, woqkv_h)):
        for k in range(3):
            at = (3 * g + k) * half
            pieces.append((h.at[k], wqkv_s.at[:, at:at + half]))
    loads = [pltpu.make_async_copy(h, v, load_sem.at[i]) for i, (h, v) in enumerate(pieces)]
    for c in loads:
        c.start()

    def columns(g, kind, t):
        start = g * 3 * half + kind * half + t * 128
        return slice(start, start + 128)

    def work(b):
        for c in bin_loads(b):
            c.wait()
        at = rows_of(b)
        for g in range(2):
            for t in range(tiles):
                q2 = qkv_s[at, columns(g, 0, t)]
                k2 = qkv_s[at, columns(g, 1, t)]
                v2 = qkv_s[at, columns(g, 2, t)]
                col = g * half + t * 128
                do2 = two_heads(do_s[at, col:col + 128])
                dp = nt(v2, do2)
                p_low = p_s[b, g * tiles + t]
                p = p_low.astype(F32)
                ds = (p * (dp - jnp.sum(dp * p, 0, keepdims=True))).astype(BF)
                dqkv_s[at, columns(g, 2, t)] = nn(p_low, do2).astype(BF)
                dqkv_s[at, columns(g, 1, t)] = (nn(ds, two_heads(q2)) * HEAD ** (-0.5)).astype(BF)
                dqkv_s[at, columns(g, 0, t)] = (
                    tn(stack_heads(ds), two_heads(k2)) * HEAD ** (-0.5)
                ).astype(BF)

    def step(b, carry):
        work(b)
        return carry

    lax.fori_loop(0, main, step, 0)
    for c in loads:
        c.wait()
    own = x_ref.shape[0]
    pick = pick_ref[:, :own].astype(F32)

    def unpack(v):
        return lax.dot_general(pick, v, (((0,), (0,)), ((), ())), precision=HIGHEST, preferred_element_type=F32)

    da1 = unpack(nt(dqkv_s[:own, :], wqkv_s[...]))
    x = x_ref[...].astype(F32)
    xhat, inv = normalize(jnp.where(x < 0.5 * SENTINEL, x, 0.0))
    small_ref[:own, :] = unpack(dh1_ref[...]) + normalize_pull(da1 * g1_ref[...].reshape(1, width), xhat, inv)

    def leave(k):
        cut = pl.ds(k * width, width)
        return [
            pltpu.make_async_copy(own_ref.at[cut], own_h.at[cut], out_sem.at[2 * k]),
            pltpu.make_async_copy(send_ref.at[cut], send_h.at[cut], out_sem.at[2 * k + 1]),
        ]

    def gradients(k, rows, add):
        if add:
            for c in leave(k):
                c.wait()
        gain = jnp.zeros((width, 128), F32)
        for g in (1, 0):
            at = (3 * g + k) * half
            grad = nn(a1t_s[:, rows], dqkv_s[rows, at:at + half])
            into = send_ref if g else own_ref
            cut = slice(k * width, (k + 1) * width)
            into[cut, :] = into[cut, :] + grad if add else grad
            for j in range(half // 128):
                piece = slice(j * 128, (j + 1) * 128)
                gain += grad[:, piece] * wqkv_s[:, at + j * 128:at + (j + 1) * 128].astype(F32)
        for c in leave(k):
            c.start()
        return jnp.sum(gain.T, 0, keepdims=True) / g1_ref[...].reshape(1, width)

    small_ref[own:, :] = jnp.zeros((small_ref.shape[0] - own, width), F32)
    small_ref[own:own + 1, :] = sum(gradients(k, slice(0, whole), False) for k in range(3))
    if main < bins:
        @pl.when(more_ref[0, 0] > 0)
        def _():
            for b in range(main, bins):
                for c in bin_loads(b):
                    c.start()
            lax.fori_loop(main, bins, step, 0)
            small_ref[own:own + 1, :] += sum(gradients(k, slice(whole, bins * SUB), True) for k in range(3))
    at = 3 * width
    send_ref[at:, :] = jnp.zeros((send_ref.shape[0] - at, half), F32)
    count = small_ref.shape[0]
    send_ref[at:at + count, :] = small_ref[:, :half]
    send_ref[at + count:at + 2 * count, :] = small_ref[:, half:]
    rest = pltpu.make_async_copy(send_ref.at[pl.ds(at, 2 * count)], send_h.at[pl.ds(at, 2 * count)], out_sem.at[6])
    rest.start()
    for k in range(3):
        for c in leave(k):
            c.wait()
    rest.wait()


def text_backward(whole, more, x, dh1, pick, g1, qkv, p, do, a1t, wqkv, oqkv):
    total, width = do.shape
    half = width // 2
    own = dh1.shape[0]
    count = own + 8
    every = lambda a: pl.BlockSpec(a.shape, lambda i: (0,) * len(a.shape))
    fixed = lambda *s: pl.BlockSpec(s, lambda i: (0,) * len(s))
    hbm = pl.BlockSpec(memory_space=pl.ANY)
    smem = pl.BlockSpec(memory_space=pltpu.SMEM)
    shape = jax.ShapeDtypeStruct
    bins, units = p.shape[:2]
    return pl.pallas_call(
        functools.partial(backward_kernel, whole),
        grid=(1,),
        out_shape=(
            shape((3 * width, half), F32), shape((3 * width + 2 * count, half), F32), shape((count, width), F32),
        ),
        in_specs=[smem, fixed(own, width), every(dh1), every(pick), every(g1)] + [hbm] * 6,
        out_specs=(hbm, hbm, fixed(count, width)),
        scratch_shapes=[
            pltpu.VMEM((total, 3 * width), BF),
            pltpu.VMEM((bins, units, SUB, 2 * SUB), BF),
            pltpu.VMEM((total, width), BF),
            pltpu.VMEM((width, total), BF),
            pltpu.VMEM((total, 3 * width), BF),
            pltpu.VMEM((width, 3 * width), BF),
            pltpu.VMEM((3 * width, half), F32),
            pltpu.VMEM((3 * width + 2 * count, half), F32),
            pltpu.SemaphoreType.DMA((7,)),
            pltpu.SemaphoreType.DMA((3 * bins,)),
            pltpu.SemaphoreType.DMA((7,)),
        ],
        cost_estimate=cost(20),
        compiler_params=pltpu.CompilerParams(vmem_limit_bytes=58 * MIB),
        name="text_backward",
    )(more, x, dh1, pick, g1, qkv, p, do, a1t, wqkv, oqkv)


def feed_kernel(
    a2t_ref, du_ref, upi_ref, ot_ref, dattn_ref, outa_ref, outb_ref, gsum_ref, gsumi_ref, dm_ref, low_ref, gh_ref,
    up_ref, out_ref, down_ref, proj_ref,
):
    up_ref[...] = upi_ref[...] + nn(a2t_ref[...], du_ref[...])
    quarter = outa_ref.shape[0]
    out = nn(ot_ref[...], dattn_ref[...])
    out_ref[:quarter, :] = out[:quarter] + outa_ref[...]
    out_ref[quarter:, :] = out[quarter:] + outb_ref[...]
    mine = gsum_ref.shape[0]
    high, rest = halves(jnp.concatenate([gsum_ref[...], gsumi_ref[:mine]], 0))
    down_ref[...] = tn(high, dm_ref[...]) + tn(rest, dm_ref[...])
    proj_ref[...] = tn(low_ref[...], gh_ref[...])


def feed_grads(a2t, du, ot, dattn, got, gsum, dm, low, gh):
    width, total = a2t.shape
    hidden = du.shape[1]
    half = width // 2
    quarter = half // 2
    mine = gsum.shape[0]
    steps = 6
    tile = hidden // steps
    slim = width // steps
    rest = got.shape[0] - width - quarter
    whole = lambda a: pl.BlockSpec(a.shape, lambda i: (0,) * len(a.shape), pipeline_mode=pl.Buffered(1))
    shape = jax.ShapeDtypeStruct
    columns = lambda rows, cols, row=0, col=0: pl.BlockSpec((rows, cols), lambda i: (row, col + i))
    return pl.pallas_call(
        feed_kernel,
        grid=(steps,),
        out_shape=(
            shape((width, hidden), F32), shape((half, width), F32), shape((hidden, width), F32), shape((width, half), F32),
        ),
        in_specs=[
            whole(a2t), columns(total, tile), columns(width, tile),
            pl.BlockSpec((half, total), lambda i: (0, 0), pipeline_mode=pl.Buffered(1)), columns(total, slim),
            columns(quarter, slim, width // quarter), columns(quarter, slim, width // quarter, steps),
            columns(mine, tile), columns(rest, tile, (width + quarter) // rest), whole(dm), columns(low.shape[0], slim),
            whole(gh),
        ],
        out_specs=(
            columns(width, tile), columns(half, slim), pl.BlockSpec((tile, width), lambda i: (i, 0)),
            pl.BlockSpec((slim, half), lambda i: (i, 0)),
        ),
        cost_estimate=cost(9),
        compiler_params=pltpu.CompilerParams(vmem_limit_bytes=28 * MIB),
        name="feed_grads",
    )(a2t, du, got, ot, dattn, got, got, gsum, got, dm, low, gh)


def finish_kernel(
    own_ref, in_ref, small_ref, smalla_ref, smallb_ref, gain2_ref, gain2i_ref, loss_ref, temp_ref,
    qkv_ref, rows_ref, gain1o_ref, gain2o_ref, losso_ref, tempo_ref,
):
    qkv_ref[0] = own_ref[...] + in_ref[...]
    core = lax.axis_index("mp")
    own = rows_ref.shape[0] // 2
    half = gain1o_ref.shape[0]

    @pl.when(pl.program_id(0) == 0)
    def _():
        got = jnp.concatenate([smalla_ref[...], smallb_ref[...]], 1)
        rows_ref[:own, :] = jnp.where(core == 0, small_ref[:own], got[:own])
        rows_ref[own:, :] = jnp.where(core == 0, got[:own], small_ref[:own])
        losso_ref[...] = loss_ref[...]
        tempo_ref[...] = temp_ref[...]
        one = small_ref[own:own + 1, :] + got[own:own + 1, :]
        two = gain2_ref[:1, :] + gain2i_ref[:1, :2 * half]
        gain1o_ref[...] = jnp.where(core == 0, one[:, :half], one[:, half:]).reshape(half)
        gain2o_ref[...] = jnp.where(core == 0, two[:, :half], two[:, half:]).reshape(half)


def finish(own, got, small, gain2, other, at, loss, temp):
    count, width = small.shape
    rows = count - 8
    half = width // 2
    whole = lambda a: pl.BlockSpec(a.shape, lambda i: (0,) * len(a.shape), pipeline_mode=pl.Buffered(1))
    fixed = lambda *shape: pl.BlockSpec(shape, lambda i: (0,) * len(shape))
    piece = pl.BlockSpec((width, half), lambda i: (i, 0))
    start = 3 * width // count
    shape = jax.ShapeDtypeStruct
    return pl.pallas_call(
        finish_kernel,
        grid=(3,),
        out_shape=(shape((3, width, half), F32), shape((2 * rows, width), F32), shape((half,), F32), shape((half,), F32)) + (shape((1, 1), F32),) * 2,
        in_specs=[
            piece, piece, whole(small), pl.BlockSpec((count, half), lambda i: (start, 0)),
            pl.BlockSpec((count, half), lambda i: (start + 1, 0)), whole(gain2),
            pl.BlockSpec((8, other.shape[1]), lambda i: (at // 8, 0)), whole(loss), whole(temp),
        ],
        out_specs=(pl.BlockSpec((1, width, half), lambda i: (i, 0, 0)), fixed(2 * rows, width), fixed(half), fixed(half), fixed(1, 1), fixed(1, 1)),
        cost_estimate=cost(4),
        compiler_params=pltpu.CompilerParams(vmem_limit_bytes=24 * MIB),
        name="finish",
    )(own, got, small, got, got, gain2, other, loss, temp)


MESH = pl.DeviceIdType.MESH


def chip_grid(mesh):
    chips = mesh.devices.reshape(-1, mesh.shape["mp"])[:, 0]
    places = [getattr(d, "coords", None) for d in chips]
    if all(p is not None and len(p) == 3 for p in places):
        grid = tuple(len({p[i] for p in places}) for i in (2, 1, 0))
        if grid[0] * grid[1] * grid[2] == len(chips):
            return grid
    side = 1
    while (2 * side) ** 3 <= len(chips):
        side *= 2
    return (len(chips) // (side * side), side, side)


class Spread:
    def __init__(self, grid, place, core, block, send, recv, first):
        self.grid, self.place, self.core = grid, place, core
        self.block, self.send, self.recv = block, send, recv
        self.first = first
        self.sent = []
        zs, ys, xs = grid
        self.turn = ys == xs
        self.aorder = list(range(1, ys))
        zevents = [("z", d, None) for d in range(1, zs)]
        aevents = [[("a", d, a) for d in range(zs)] for a in self.aorder]
        self.pending = []
        for i in range(zs + len(aevents)):
            self.pending += zevents[i:i + 1]
            for j, events in enumerate(aevents):
                self.pending += events[i - j:i - j + 1] if i >= j else []

    def slot(self, kz, ka):
        return kz * self.grid[1] + ka

    def target(self, dz, da):
        zs, ys, xs = self.grid
        z, y, x = self.place
        dy, dx = (da * (1 - self.core), da * self.core) if self.turn else (da, 0)
        batch = (lax.rem(z + dz, zs) * ys + lax.rem(y + dy, ys)) * xs + lax.rem(x + dx, xs)
        return (batch, self.core)

    def copy(self, source, landing, to, when=None):
        index = len(self.sent)

        def make():
            return pltpu.make_async_remote_copy(
                src_ref=self.first if source is None else self.block(self.slot(*source)),
                dst_ref=self.block(self.slot(*landing)), send_sem=self.send.at[index],
                recv_sem=self.recv.at[self.slot(*landing)], device_id=self.target(*to), device_id_type=MESH,
            )

        if when is None:
            make().start()
        else:
            pl.when(when)(lambda: make().start())
        self.sent.append((make, when))

    def forward(self, source, kz, when=None):
        for d in self.aorder:
            self.copy(source, (kz, self.grid[1] - d), (0, d), when)

    def start(self):
        zs = self.grid[0]
        z = self.place[0]
        if zs > 1:
            self.copy(None, (zs - 1, 0), (1, 0), z < zs - 1)
            self.copy(None, (1, 0), (zs - 1, 0), z > 0)
        self.forward(None, 0)

    def arrive(self, slot):
        pltpu.make_async_remote_copy(
            src_ref=self.block(slot), dst_ref=self.block(slot), send_sem=self.send.at[0],
            recv_sem=self.recv.at[slot], device_id=self.target(1, 0), device_id_type=MESH,
        ).wait_recv()

    def sides(self, d):
        zs = self.grid[0]
        z = self.place[0]
        return [(d, z + d < zs, True), (zs - d, z - d >= 0, False)]

    def serve(self, count=1):
        zs = self.grid[0]
        z = self.place[0]
        for _ in range(min(count, len(self.pending))):
            kind, d, a = self.pending.pop(0)
            if kind == "a" and d == 0:
                self.arrive(self.slot(0, a))
                continue
            for kz, there, above in self.sides(d):
                slot = self.slot(kz, 0 if kind == "z" else a)
                pl.when(there)(lambda slot=slot: self.arrive(slot))
                if kind == "z":
                    if d + 1 < zs and above:
                        self.copy((kz, 0), (kz + 1, 0), (zs - 1, 0), there & (z > 0))
                    elif d + 1 < zs:
                        self.copy((kz, 0), (kz - 1, 0), (1, 0), there & (z < zs - 1))
                    self.forward((kz, 0), kz, there)

    def finish(self):
        self.serve(len(self.pending))
        for make, when in self.sent:
            if when is None:
                make().wait_send()
            else:
                pl.when(when)(lambda make=make: make().wait_send())

    @staticmethod
    def copies(grid):
        zs, ys, _ = grid
        return 4 * zs + 2 * zs * (ys - 1)


class Hops:
    def __init__(self, grid, place, core, block, send, recv, first):
        self.grid, self.place, self.core = grid, place, core
        self.block, self.send, self.recv = block, send, recv
        self.first = first
        self.sent = []
        zs, ys, xs = grid
        self.turn = ys == xs
        near = []
        for d in range(1, zs // 2 + 1):
            near += [d] if 2 * d == zs else [d, zs - d]
        self.zorder = near
        self.aorder = list(range(1, ys))
        self.border = list(range(1, xs))
        self.pending = [("z", k) for k in near]
        self.pending += [("a", a, k) for a in self.aorder for k in [0] + near]

    def slot(self, kz, ka, kb):
        zs, ys, xs = self.grid
        plain = (kz * ys + ka) * xs + kb
        if not self.turn:
            return plain
        other = (kz * ys + kb) * xs + ka
        return plain if plain == other else plain + self.core * (other - plain)

    def target(self, dz, da, db):
        zs, ys, xs = self.grid
        z, y, x = self.place
        if self.turn and da != db:
            dy = da + self.core * (db - da)
            dx = db + self.core * (da - db)
        else:
            dy, dx = da, db
        batch = (lax.rem(z + dz, zs) * ys + lax.rem(y + dy, ys)) * xs + lax.rem(x + dx, xs)
        return (batch, self.core)

    def copy(self, source, landing, to):
        index = len(self.sent)
        sent = pltpu.make_async_remote_copy(
            src_ref=source, dst_ref=self.block(landing), send_sem=self.send.at[index],
            recv_sem=self.recv.at[landing], device_id=to, device_id_type=MESH,
        )
        sent.start()
        self.sent.append(sent)

    def along_a(self, source, kz):
        ys = self.grid[1]
        for d in self.aorder:
            self.copy(source, self.slot(kz, ys - d, 0), self.target(0, d, 0))

    def along_b(self, source, kz, ka):
        xs = self.grid[2]
        for d in self.border:
            self.copy(source, self.slot(kz, ka, xs - d), self.target(0, 0, d))

    def start(self):
        zs = self.grid[0]
        self.along_b(self.first, 0, 0)
        self.along_a(self.first, 0)
        for d in self.zorder:
            self.copy(self.first, self.slot(zs - d, 0, 0), self.target(d, 0, 0))

    def arrive(self, slot):
        pltpu.make_async_remote_copy(
            src_ref=self.block(slot), dst_ref=self.block(slot), send_sem=self.send.at[0],
            recv_sem=self.recv.at[slot], device_id=self.target(1, 0, 0), device_id_type=MESH,
        ).wait_recv()

    def serve(self, count=1):
        for _ in range(min(count, len(self.pending))):
            event = self.pending.pop(0)
            if event[0] == "z":
                slot = self.slot(event[1], 0, 0)
                self.arrive(slot)
                self.along_b(self.block(slot), event[1], 0)
                self.along_a(self.block(slot), event[1])
            else:
                slot = self.slot(event[2], event[1], 0)
                self.arrive(slot)
                self.along_b(self.block(slot), event[2], event[1])

    def finish(self):
        self.serve(len(self.pending))
        for a in [0] + self.aorder:
            for b in self.border:
                for k in [0] + self.zorder:
                    self.arrive(self.slot(k, a, b))
        for sent in self.sent:
            sent.wait_send()

    @staticmethod
    def copies(grid):
        zs, ys, xs = grid
        return (zs - 1) + zs * (ys - 1) + zs * ys * (xs - 1)


def attend(qkv_ref, o_ref, start, ids, half):
    m = ids == ids.T
    m = jnp.concatenate([m, m], 1)
    rows = pl.ds(start, SUB)
    for t in range(half // 128):
        q2 = qkv_ref[rows, t * 128:(t + 1) * 128]
        k2 = qkv_ref[rows, half + t * 128:half + (t + 1) * 128]
        v2 = qkv_ref[rows, 2 * half + t * 128:2 * half + (t + 1) * 128]
        st = nt(k2, two_heads(q2)) * HEAD ** (-0.5)
        st = jnp.where(m, st, -1000000000.0)
        e = jnp.exp(st - jnp.max(st, 0, keepdims=True))
        p = e * (1.0 / jnp.sum(e, 0, keepdims=True))
        o_ref[rows, t * 128:(t + 1) * 128] = tn(stack_heads(p.astype(BF)), two_heads(v2)).astype(BF)


def front_kernel(
    grid,
    rows_ref, mask_ref, image_ref, g1_ref, g2_ref, temp_ref,
    iqkv_h, iout_h, iup_h, idown_h, tqkv_h, tout_h, tup_h, tdown_h, tproj_h,
    xg_ref, oqkv_h, oout_h, oup_h, dmw_ref, dh_ref, dm_ref, low_ref, gh_ref, loss_ref, temp_ref2,
    iqkv, iout, iup, idown, tqkv, tout, tup, tdown, proj,
    own_x, small, small_abs, payload, qkv_s, o_s, image_x, part, part_in, sums, sums_in,
    wsend_qkv, wsend_out, wsend_up, wsend_proj, wland_qkv, wland_out, wland_up, wland_proj,
    dmw_send, dmw_in, cos_s, tnorm_s, xg,
    load_sem, out_sem, x_send, x_recv, s_send, s_recv, c_send, c_recv, own_sem,
):
    zs, ys, xs = grid
    chips = zs * ys * xs
    planes = zs * ys
    batch, core = lax.axis_index("batch"), lax.axis_index("mp")
    place = (batch // (ys * xs), lax.rem(batch // xs, ys), lax.rem(batch, xs))
    partner = (batch, 1 - core)
    pairs, length = mask_ref.shape
    rows = pairs * length
    width = rows_ref.shape[1]
    half = width // 2
    hidden = tup.shape[1]
    hp = pairs // 2
    hr = hp * length
    total = chips * pairs
    mine = chips * hp
    patches = image_ref.shape[0] // pairs
    padded = image_x.shape[0] // pairs

    inside = total <= INSIDE

    loads = {}
    for i, (name, h, v) in enumerate((
        ("iqkv", iqkv_h, iqkv), ("tqkv", tqkv_h, tqkv), ("iout", iout_h, iout), ("tout", tout_h, tout),
        ("tup", tup_h, tup), ("iup", iup_h, iup), ("idown", idown_h, idown), ("tdown", tdown_h, tdown),
        ("proj", tproj_h, proj.at[core]),
    )):
        loads[name] = pltpu.make_async_copy(h, v, load_sem.at[i])
        if i < 3:
            loads[name].start()

    xg = xg if inside else xg_ref
    gather = Spread(grid, place, core, lambda s: xg.at[s], x_send, x_recv, own_x)
    peers = [partner]
    spread = Hops(grid, place, core, lambda s: small.at[core, s], s_send, s_recv, payload)
    peers += [spread.target(d, 0, 0) for d in range(1, zs)]
    peers += [spread.target(0, d, 0) for d in range(1, ys)]
    peers += [spread.target(0, 0, d) for d in range(1, xs)]
    barrier = pltpu.get_barrier_semaphore()
    for peer in peers:
        pl.semaphore_signal(barrier, inc=1, device_id=peer, device_id_type=MESH)

    mask = mask_ref[...].astype(F32)
    lane = count_along(rows, length)
    sub = parts_of(count_down(rows, length), length)[1]
    spread_mask = jnp.broadcast_to(mask[:, None, :], (pairs, length, length)).reshape(rows, length)
    valid = jnp.sum(jnp.where(lane == sub, spread_mask, 0.0), 1, keepdims=True)
    text_x = rows_ref[...].astype(F32)
    marked = jnp.where(valid > 0, text_x, SENTINEL)
    own_x[...] = jnp.where(core == 0, marked[:hr], marked[hr:])
    top = padded * pairs
    image_of, patch_of = parts_of(count_down(top), padded)
    image_ids = jnp.where(patch_of < patches, image_of, -1.0)
    place_of = jnp.where(patch_of < patches, patch_of * pairs + image_of, -1.0)
    reorder = (widen(place_of, patches * pairs) == count_along(top, patches * pairs)).astype(BF)
    image_x[...] = nn(reorder, image_ref[...])
    image_a1 = normalize(image_x[...])[0].astype(BF)
    pl.semaphore_wait(barrier, len(peers))
    gather.start()

    swaps = []

    def swap(source, landing, index):
        c = pltpu.make_async_remote_copy(
            src_ref=source, dst_ref=landing, send_sem=c_send.at[index], recv_sem=c_recv.at[index],
            device_id=partner, device_id_type=MESH,
        )
        c.start()
        swaps.append(c)
        return c

    def put(ref, cols, high, rest):
        size = mine // 2
        for g in range(2):
            ref[2 * g * size:(2 * g + 1) * size, cols] = high[g * size:(g + 1) * size]
            ref[(2 * g + 1) * size:(2 * g + 2) * size, cols] = rest[g * size:(g + 1) * size]

    def contrast():
        for s in range(chips):
            kz, ky, kx = s // (ys * xs), s // xs % ys, s % xs
            at = (lax.rem(place[0] + kz, zs) * ys + lax.rem(place[1] + ky, ys)) * xs + lax.rem(place[2] + kx, xs)
            small_abs[:, at] = small[:, s]
        low = small_abs[0, :, :, :width].reshape(total, width).astype(BF)
        low_ref[...] = low
        counts = small_abs[0, :, :, width:].reshape(total, 128)[:, :1]
        embed = jnp.concatenate([nn(low, proj[0]), nn(low, proj[1])], 1)
        inv = lax.rsqrt(jnp.sum(embed * embed, 1, keepdims=True) + NORM_EPS)
        tnorm_s[...] = embed * inv
        images = small_abs[1, :, :, :width].reshape(total, width)
        scale = jnp.exp(jnp.full((1, 1), temp_ref[0, 0], F32))
        cos_s[...] = three(nt, tnorm_s[...], images)
        logits = cos_s[...] * scale
        row_top = jnp.max(logits, 1, keepdims=True)
        row_lse = row_top + jnp.log(jnp.sum(jnp.exp(logits - row_top), 1, keepdims=True))
        col_top = jnp.max(logits, 0, keepdims=True)
        col_lse = col_top + jnp.log(jnp.sum(jnp.exp(logits - col_top), 0, keepdims=True))
        eye = (lax.broadcasted_iota(jnp.int32, (total, total), 0) == lax.broadcasted_iota(jnp.int32, (total, total), 1))
        eye = eye.astype(F32)
        pair_grad = (jnp.exp(logits - row_lse) + jnp.exp(logits - col_lse) - 2.0 * eye) * (0.5 / total)

        def everything(v):
            return jnp.sum(jnp.sum(v, 1, keepdims=True), 0, keepdims=True)

        loss = (everything(row_lse) + everything(col_lse) - 2.0 * everything(logits * eye)) * (0.5 / total)
        temp = scale * everything(pair_grad * cos_s[...])
        loss_ref[...] = loss
        temp_ref2[...] = temp
        grad_norm = scale * three(nn, pair_grad, images)
        tnorm = tnorm_s[...]
        grad_embed = ((grad_norm - tnorm * jnp.sum(tnorm * grad_norm, 1, keepdims=True)) * inv).astype(BF)
        gh_ref[...] = jnp.where(core == 0, grad_embed[:, :half], grad_embed[:, half:])
        dh = (nt(grad_embed[:, :half], proj[0]) + nt(grad_embed[:, half:], proj[1])) / counts
        dm = dh.astype(BF)

        r = count_along(8, total)
        here = core.astype(F32)
        owner = jnp.where(r < mine, here, 1.0 - here)
        k, i = parts_of(parts_of(r, mine)[1], hp)
        kb, rest = parts_of(k, planes)
        kz, ka = parts_of(rest, ys)
        ky, kx = (jnp.where(owner == 0, ka, kb), jnp.where(owner == 0, kb, ka)) if ys == xs else (ka, kb)
        z, y, x = (parts_of(v + p.astype(F32), n)[1] for v, p, n in zip((kz, ky, kx), place, grid))
        at = ((z * ys + y) * xs + x) * pairs + owner * hp + i
        pick = (jnp.broadcast_to(at[:1], (total, total)).T == count_along(total, total)).astype(BF)
        dm_sorted = nn(pick, dm).astype(BF)
        dm_ref[...] = dm_sorted
        dmw = nt(dm_sorted, tdown[...])
        dmw_send[...] = dmw[mine:]
        dmw_swap = swap(dmw_send, dmw_in, 8)
        dh_high, dh_low = halves(dh)
        put(dh_ref, slice(None), nn(pick[:mine], dh_high).astype(BF), nn(pick[:mine], dh_low).astype(BF))
        put(dmw_ref, slice(0, hidden), *halves(dmw[:mine]))
        return dmw_swap

    g1, g2 = g1_ref[...].reshape(1, width), g2_ref[...].reshape(1, width)
    loads["iqkv"].wait()
    for name in list(loads)[3:]:
        loads[name].start()
    for k in range(3):
        qkv_s[:, k * half:(k + 1) * half] = nn(image_a1, iqkv[k]).astype(BF)
    loads["tqkv"].wait()
    for k in range(3):
        wsend_qkv[k] = tqkv[k].astype(F32)
    qkv_swap = swap(wsend_qkv, wland_qkv, 3)
    loads["iout"].wait()
    parts = 2
    cut = top // parts
    image_swaps = []
    for i in range(parts):
        for s in range(i * cut // SUB, (i + 1) * cut // SUB):
            attend(qkv_s, o_s, s * SUB, image_ids[s * SUB:(s + 1) * SUB], half)
        at = pl.ds(i * cut, cut)
        part[at, :] = nn(o_s[at, :], iout[...])
        image_swaps.append(swap(part.at[at], part_in.at[at], i))

    a1 = (normalize(text_x)[0] * g1).astype(BF)
    for k in range(3):
        qkv_s[:rows, k * half:(k + 1) * half] = nn(a1, tqkv[k]).astype(BF)
    attend(qkv_s, o_s, 0, jnp.where(valid > 0, parts_of(count_down(rows), length)[0], -1.0), half)
    loads["tout"].wait()
    part[top:, :] = nn(o_s[:rows, :], tout[...])
    text_swap = swap(part.at[pl.ds(top, rows)], part_in.at[pl.ds(top, rows)], 5)
    gather.serve(2)

    loads["tup"].wait()
    up_cut = wsend_up.shape[0] // 4
    up_swaps = []

    def send_up(i):
        at = pl.ds(i * up_cut, up_cut)
        wsend_up[at, :] = tup[at, :].astype(F32)
        up_swaps.append(swap(wsend_up.at[at], wland_up.at[at], 9 + i))

    send_up(0)
    send_up(1)

    piece = 512
    loads["iup"].wait()
    mean_i, bars = [], []
    for i in range(parts):
        image_swaps[i].wait_recv()
        at = pl.ds(i * cut, cut)
        h1 = image_x[at, :] + (part[at, :] + part_in[at, :])
        a2 = normalize(h1)[0].astype(BF)
        mean_i.append(jnp.sum(h1.reshape(pairs // parts, padded, width), 1))
        bar = []
        for j in range(hidden // piece):
            u = nn(a2, iup[:, j * piece:(j + 1) * piece])
            g = (u * (0.5 + 0.5 * lax.erf(u * 0.5 ** 0.5))).astype(BF).astype(F32)
            bar.append(jnp.sum(g.reshape(pairs // parts, padded, piece), 1))
        bars.append(jnp.concatenate(bar, 1))
        gather.serve(1)
    mean_i = jnp.concatenate(mean_i, 0)
    bar = jnp.concatenate(halves(jnp.concatenate(bars, 0)), 0)
    loads["idown"].wait()
    low = nn(bar, idown[...])
    sums[pairs:, :] = low[:pairs] + low[pairs:]

    text_swap.wait_recv()
    h1 = text_x + (part[top:, :] + part_in[top:, :])
    a2 = (normalize(h1)[0] * g2).astype(BF)
    mean_h = jnp.sum((h1 * valid).reshape(pairs, length, width), 1)
    bars = []
    for j in range(hidden // piece):
        u = nn(a2, tup[:, j * piece:(j + 1) * piece])
        g = (u * (0.5 + 0.5 * lax.erf(u * 0.5 ** 0.5))).astype(BF).astype(F32) * valid
        bars.append(jnp.sum(g.reshape(pairs, length, piece), 1))
    bar = jnp.concatenate(halves(jnp.concatenate(bars, 1)), 0)
    loads["tdown"].wait()
    low = nn(bar, tdown[...])
    sums[:pairs, :] = low[:pairs] + low[pairs:]
    sums_swap = swap(sums, sums_in, 6)
    sums_swap.wait_recv()

    count = jnp.sum(mask, 1, keepdims=True)
    pooled = (mean_h + (sums[:pairs, :] + sums_in[:pairs, :])) / count
    e = (mean_i + (sums[pairs:, :] + sums_in[pairs:, :])) * (1.0 / patches)
    image_norm = e * lax.rsqrt(jnp.sum(e * e, 1, keepdims=True) + NORM_EPS)
    payload[:, :width] = jnp.where(core == 0, pooled, image_norm)
    payload[:, width:] = jnp.broadcast_to(count, (pairs, 128))
    spread.start()
    small[core, 0] = payload[...]
    loads["proj"].wait()
    wsend_proj[...] = proj[core].astype(F32)
    proj_swap = swap(wsend_proj, wland_proj, 2)
    wsend_out[...] = tout[...].astype(F32)
    out_swap = swap(wsend_out, wland_out, 4)
    send_up(2)
    send_up(3)
    oqkv, oout, oup = iqkv, iout, iup
    outs = []

    def hand_over(swapped, landed, held, out, index):
        swapped.wait_recv()
        held[...] = landed[...].astype(BF)
        outs.append(pltpu.make_async_copy(held, out, out_sem.at[index]))
        outs[-1].start()

    def hand_up(i):
        at = pl.ds(i * up_cut, up_cut)
        hand_over(up_swaps[i], wland_up.at[at], oup.at[at], oup_h.at[at], 2 + i)

    hand_over(qkv_swap, wland_qkv, oqkv, oqkv_h, 1)
    gather.serve(1)
    spread.serve(zs - 1)
    gather.serve(1)
    hand_up(0)
    hand_up(1)
    spread.serve(len(spread.pending))
    gather.serve(len(gather.pending))
    proj_swap.wait_recv()
    proj[1 - core] = wland_proj[...].astype(BF)
    hand_over(out_swap, wland_out, oout, oout_h, 0)
    spread.finish()
    both_swap = swap(small.at[core], small.at[core], 7)
    hand_up(2)
    both_swap.wait_recv()
    gather.serve(len(gather.pending))
    own_copy = pltpu.make_async_copy(own_x, xg_ref.at[0], own_sem.at[0])
    own_copy.start()
    if inside:
        store = pltpu.make_async_copy(xg.at[pl.ds(1, planes - 1)], xg_ref.at[pl.ds(1, planes - 1)], own_sem.at[1])
        store.start()
    if inside:
        dmw_swap = contrast()
    else:
        dmw_ref[...] = small[...]
        dm_ref[...] = proj[...]

    hand_up(3)
    if inside:
        dmw_swap.wait_recv()
        put(dmw_ref, slice(hidden, 2 * hidden), *halves(dmw_in[...]))
    gather.finish()
    own_copy.wait()
    if inside:
        store.wait()
    for s in swaps:
        s.wait_send()
    for o in outs:
        o.wait()


def front(grid, rows, mask, image, g1, g2, temp, weights):
    chips = grid[0] * grid[1] * grid[2]
    pairs, length = mask.shape
    width = rows.shape[1]
    half = width // 2
    iqkv, iout, iup, idown, tqkv, tout, tup, tdown, tproj = weights
    hidden = tup.shape[1]
    total = chips * pairs
    mine = total // 2
    patches = image.shape[0] // pairs
    padded = -(-patches // 64) * 64
    top = padded * pairs
    hr = pairs // 2 * length
    vmem = pl.BlockSpec(memory_space=pltpu.VMEM)
    hbm = pl.BlockSpec(memory_space=pl.ANY)
    shape = jax.ShapeDtypeStruct
    copies, hops = Spread.copies(grid), Hops.copies(grid)
    inside = total <= INSIDE
    if inside:
        ends = (
            shape((2 * mine, 2 * hidden), BF), shape((2 * mine, width), BF), shape((total, width), BF),
            shape((total, width), BF), shape((total, half), BF), shape((1, 1), F32), shape((1, 1), F32),
        )
    else:
        mine, total = 8, 128
        ends = (shape((2, chips, pairs, width + 128), F32),) + (shape((8, 128), F32),)
        ends += (shape((2,) + tproj.shape, BF),) + (shape((8, 128), F32),) * 4
    return pl.pallas_call(
        functools.partial(front_kernel, grid),
        out_shape=(
            shape((grid[0] * grid[1], hr, width), F32),
            shape(tqkv.shape, BF), shape(tout.shape, BF), shape(tup.shape, BF),
        ) + ends,
        in_specs=[vmem] * 5 + [pl.BlockSpec(memory_space=pltpu.SMEM)] + [hbm] * 9,
        out_specs=[hbm] * 4 + [vmem] * 7,
        scratch_shapes=[
            pltpu.VMEM(iqkv.shape, BF), pltpu.VMEM(iout.shape, BF), pltpu.VMEM(iup.shape, BF), pltpu.VMEM(idown.shape, BF),
            pltpu.VMEM(tqkv.shape, BF), pltpu.VMEM(tout.shape, BF), pltpu.VMEM(tup.shape, BF), pltpu.VMEM(tdown.shape, BF),
            pltpu.VMEM((2,) + tproj.shape, BF),
            pltpu.VMEM((hr, width), F32),
            pltpu.VMEM((2, chips, pairs, width + 128), F32),
            pltpu.VMEM((2, chips if inside else 1, pairs, width + 128), F32),
            pltpu.VMEM((pairs, width + 128), F32),
            pltpu.VMEM((top, 3 * half), BF),
            pltpu.VMEM((top, half), BF),
            pltpu.VMEM((top, width), F32),
            pltpu.VMEM((top + pairs * length, width), F32),
            pltpu.VMEM((top + pairs * length, width), F32),
            pltpu.VMEM((2 * pairs, width), F32),
            pltpu.VMEM((2 * pairs, width), F32),
            pltpu.VMEM(tqkv.shape, F32), pltpu.VMEM(tout.shape, F32), pltpu.VMEM(tup.shape, F32), pltpu.VMEM(tproj.shape, F32),
            pltpu.VMEM(tqkv.shape, F32), pltpu.VMEM(tout.shape, F32), pltpu.VMEM(tup.shape, F32), pltpu.VMEM(tproj.shape, F32),
            pltpu.VMEM((mine, hidden), F32), pltpu.VMEM((mine, hidden), F32),
            pltpu.VMEM((total, total), F32), pltpu.VMEM((total, width), F32),
            pltpu.VMEM((grid[0] * grid[1], hr, width) if inside else (1, 8, 128), F32),
            pltpu.SemaphoreType.DMA((9,)), pltpu.SemaphoreType.DMA((6,)),
            pltpu.SemaphoreType.DMA((copies,)), pltpu.SemaphoreType.DMA((grid[0] * grid[1],)),
            pltpu.SemaphoreType.DMA((hops,)), pltpu.SemaphoreType.DMA((chips,)),
            pltpu.SemaphoreType.DMA((13,)), pltpu.SemaphoreType.DMA((13,)), pltpu.SemaphoreType.DMA((2,)),
        ],
        cost_estimate=cost(40),
        compiler_params=pltpu.CompilerParams(collective_id=0, has_side_effects=True, vmem_limit_bytes=60 * MIB),
        name="front",
    )(rows, mask, image, g1, g2, temp, *weights)


def contrast_outside(grid, small, proj, log_temp, text_down):
    core = lax.axis_index("mp")
    here = lax.axis_index("batch")
    chips, pairs, width = small.shape[1], small.shape[2], small.shape[3] - 128
    half = width // 2
    zs, ys, xs = grid
    slots = jnp.arange(chips, dtype=jnp.int32)
    z, y, x = here // (ys * xs), here // xs % ys, here % xs
    offset = (z + slots // (ys * xs)) % zs * (ys * xs) + (y + slots // xs % ys) % ys * xs + (x + slots % xs) % xs
    slot_of = jnp.argsort(offset)
    total = chips * pairs
    low = small[0, :, :, :width].astype(BF)[slot_of].reshape(total, width)
    counts = small[0, :, :, width:width + 1][slot_of].reshape(total, 1)
    images = small[1, :, :, :width][slot_of].reshape(total, width)
    embed = jnp.concatenate([nn(low, proj[0]), nn(low, proj[1])], 1)
    inv = lax.rsqrt(jnp.sum(embed * embed, 1, keepdims=True) + NORM_EPS)
    text_norm = embed * inv
    scale = jnp.exp(log_temp)
    cosine = three(nt, text_norm, images)
    logits = scale * cosine
    text_lse = jax.nn.logsumexp(logits, 1, keepdims=True)
    image_lse = jax.nn.logsumexp(logits, 0, keepdims=True)
    eye = jnp.eye(total, dtype=F32)
    pair_grad = (jnp.exp(logits - text_lse) + jnp.exp(logits - image_lse) - 2.0 * eye) / (2.0 * total)
    loss = (jnp.sum(text_lse) + jnp.sum(image_lse) - 2.0 * jnp.sum(logits * eye)) / (2.0 * total)
    temp = scale * jnp.sum(pair_grad * cosine)
    grad_norm = scale * three(nn, pair_grad, images)
    grad_embed = ((grad_norm - text_norm * jnp.sum(text_norm * grad_norm, 1, keepdims=True)) * inv).astype(BF)
    grad_half = lax.dynamic_slice_in_dim(grad_embed, core * half, half, 1)
    dh = (nt(grad_embed[:, :half], proj[0]) + nt(grad_embed[:, half:], proj[1])) / counts
    hp = pairs // 2
    ka, kb = slots % ys, slots // (zs * ys)
    kz = slots // ys % zs

    def mine(v, c):
        ky, kx = (jnp.where(c == 0, ka, kb), jnp.where(c == 0, kb, ka)) if ys == xs else (ka, kb)
        chip = ((z + kz) % zs * ys + (y + ky) % ys) * xs + (x + kx) % xs
        w = v.reshape(chips, 2, hp, v.shape[-1])[chip]
        return lax.dynamic_index_in_dim(w, c, 1, keepdims=False).reshape(total // 2, v.shape[-1])

    def grouped(v):
        high, rest = halves(v)
        size = INSIDE // 8
        both = jnp.stack([high.reshape(-1, size, v.shape[1]), rest.reshape(-1, size, v.shape[1])], 1)
        return both.reshape(-1, v.shape[1])

    dm = jnp.concatenate([mine(dh, core), mine(dh, 1 - core)], 0).astype(BF)
    dmw = nt(dm, text_down)
    dmw_other = lax.ppermute(dmw[total // 2:], "mp", [(0, 1), (1, 0)])
    dmw = grouped(jnp.concatenate([dmw[:total // 2], dmw_other], 1))
    return dmw, grouped(mine(dh, core)), dm, low, grad_half, loss, temp


def last_axis(grid):
    zs, ys, xs = grid
    plans = []
    for d in range(1, xs):
        pairs = []
        for z in range(zs):
            for y in range(ys):
                for x in range(xs):
                    for core in range(2):
                        py, px = (y, (x + d) % xs) if core == 0 or ys != xs else ((y + d) % ys, x)
                        pairs.append((((z * ys + py) * xs + px) * 2 + core, ((z * ys + y) * xs + x) * 2 + core))
        plans.append(pairs)
    return plans


def per_device(
    grid, image_patches, text_rows, text_mask, image_qkv, image_out, image_up, image_down, text_gain_one, text_gain_two,
    text_qkv, text_out, text_up, text_down, text_proj, log_temp,
):
    pair_count, length, width = text_rows.shape
    half = width // 2
    hidden = text_up.shape[1]

    def swap(v):
        return lax.ppermute(v, "mp", [(0, 1), (1, 0)])

    patches = jnp.transpose(image_patches, (1, 0, 2)).reshape(-1, width)
    iqkv = jnp.transpose(image_qkv, (1, 0, 2))
    tqkv = jnp.transpose(text_qkv, (1, 0, 2))
    g1, g2 = text_gain_one, text_gain_two
    xg, oqkv, oout, oup, dmw, dh, dm, low, grad_half, loss, temp = front(
        grid, text_rows.reshape(-1, width), text_mask, patches, g1, g2, log_temp.reshape(1, 1),
        (iqkv, image_out, image_up, image_down, tqkv, text_out, text_up, text_down, text_proj),
    )
    own = pair_count // 2 * length
    if dm.ndim == 3:
        dmw, dh, dm, low, grad_half, loss, temp = contrast_outside(grid, dmw, dm, log_temp, text_down)
    weights = (tqkv, text_out, text_up, oqkv, oout, oup)
    total = dm.shape[0] // 2
    near = xg.reshape(-1, width)
    plans = last_axis(grid)
    if dm.shape[0] <= INSIDE:
        far = [lax.ppermute(near, ("batch", "mp"), pairs) for pairs in plans]
        before = None
        groups = [near] + far
        for g, x in enumerate(groups):
            before = text_forward(x, length, g1, g2, dmw, dh, weights, own, len(groups), g, before)
            if g == 0:
                dh1, pick = before[-2:]
        a1t, qkv, p, do, a2t, du, ot, dattn, _, gsum, gain2, more, send = before[:13]
        got = swap(send)
        whole = layout(near.shape[0], len(groups))[0] * len(groups)
        qkv_m, qkv_o, small = text_backward(whole, more, near, dh1, pick, g1, qkv, p, do, a1t, tqkv, oqkv)
        qkv_in = swap(qkv_o)
        grad_up, grad_out, grad_down, grad_proj = feed_grads(a2t, du, ot, dattn, got, gsum, dm, low, grad_half)
        qkv_in, grad_up, grad_out, grad_down, grad_proj = lax.optimization_barrier(
            (qkv_in, grad_up, grad_out, grad_down, grad_proj))
        other, at = got, width + half // 2 + gsum.shape[0]
    else:
        size = INSIDE // 8
        groups = total // size

        def one(carry, items):
            sums, first = carry
            g, x, dmw, dh = items
            a1t, qkv, p, do, a2t, du, ot, dattn, _, gsum, gain2, more, send, dh1, pick = text_forward(
                x, length, g1, g2, dmw, dh, weights, own)
            qkv_m, qkv_o, small = text_backward(x.shape[0], more, x, dh1, pick, g1, qkv, p, do, a1t, tqkv, oqkv)
            new = (send, gain2, qkv_m, qkv_o, small[own:], nn(a2t, du), nn(ot[:half], dattn))
            return (tuple(x + y for x, y in zip(sums, new)), jnp.where(g == 0, small[:own], first)), gsum

        zero = lambda *shape: jnp.zeros(shape, F32)
        at = width + half // 2 + size
        sums = (zero(width + half // 2 + 96, hidden), zero(8, width), zero(3 * width, half),
                zero(3 * width + 2 * own + 16, half), zero(8, width), zero(width, hidden), zero(half, width))
        split = lambda v: v.reshape(groups, -1, v.shape[-1])
        planes = [near] + [lax.ppermute(near, ("batch", "mp"), pairs) for pairs in plans]
        planes = [jnp.where(x > 0.5 * SENTINEL, SENTINEL, x).astype(BF) for x in planes]
        (sums, first), gsum = lax.scan(
            one, (sums, zero(own, width)),
            (jnp.arange(groups), split(jnp.concatenate(planes, 0)), split(dmw), split(dh)))
        gsum = gsum.reshape(-1, gsum.shape[-1])
        send, gain2, qkv_m, qkv_o, gain1, up_m, out_m = sums
        small = jnp.concatenate([first, gain1], 0)
        qkv_o = jnp.concatenate([qkv_o[:3 * width], small[:, :half], small[:, half:]], 0)
        qkv_in, got = swap(qkv_o), swap(send)
        grad_up = up_m + got[:width]
        folded = got[width:width + half // 2]
        grad_out = out_m + jnp.concatenate([folded[:, :width], folded[:, width:]], 0)
        high, rest = halves(jnp.concatenate([gsum[:, :hidden], swap(gsum[:, hidden:])], 0))
        grad_down = tn(high, dm) + tn(rest, dm)
        grad_proj = tn(low, grad_half)
        other = got
    grad_qkv, grad_rows, gain1, gain2, loss, temp = finish(
        qkv_m, qkv_in, small, gain2, other, at, loss.reshape(1, 1), temp.reshape(1, 1))
    return (loss.reshape(()), grad_rows.reshape(pair_count, length, width), gain1, gain2,
            jnp.transpose(grad_qkv, (1, 0, 2)), grad_out, grad_up, grad_down, grad_proj, temp.reshape(()))


def solution(mesh):
    return jax.shard_map(
        functools.partial(per_device, chip_grid(mesh)),
        mesh=mesh,
        in_specs=(
            P("batch", None, None), P("batch", None, None), P("batch", None), P(None, None, "mp"), P("mp", None),
            P(None, "mp"), P("mp", None), P(), P(), P(None, None, "mp"), P("mp", None), P(None, "mp"), P("mp", None),
            P(None, "mp"), P(),
        ),
        out_specs=(
            P(), P("batch", None, None), P("mp"), P("mp"), P(None, None, "mp"), P("mp", None), P(None, "mp"),
            P("mp", None), P(None, "mp"), P(),
        ),
        check_vma=False,
    )
```

```python
import functools
import jax
import jax.numpy as jnp
from jax import lax
from jax.experimental import pallas as pl
from jax.experimental.pallas import tpu as pltpu
from jax.sharding import PartitionSpec as P

HEAD = 64
LN_EPS = 1e-06
NORM_EPS = 1e-06
HIGHEST = lax.Precision.HIGHEST
BF = jnp.bfloat16
F32 = jnp.float32
MIB = 2**20


def cost(microseconds):
    return pl.CostEstimate(flops=int(microseconds * 1e9), bytes_accessed=0, transcendentals=0)


def nn(a, b):
    return lax.dot_general(a, b, (((1,), (0,)), ((), ())), preferred_element_type=F32)


def nt(a, b):
    return lax.dot_general(a, b, (((1,), (1,)), ((), ())), preferred_element_type=F32)


def tn(a, b):
    return lax.dot_general(a, b, (((0,), (0,)), ((), ())), preferred_element_type=F32)


def normalize(rows):
    center = rows - jnp.mean(rows, -1, keepdims=True)
    inv = lax.rsqrt(jnp.mean(center * center, -1, keepdims=True) + LN_EPS)
    return center * inv, inv


def normalize_pull(grad, xhat, inv):
    return inv * (
        grad - jnp.mean(grad, -1, keepdims=True) - xhat * jnp.mean(grad * xhat, -1, keepdims=True)
    )


def two_heads(tile):
    first = lax.broadcasted_iota(jnp.int32, tile.shape, 1) < HEAD
    zero = jnp.zeros_like(tile)
    return jnp.concatenate([jnp.where(first, tile, zero), jnp.where(first, zero, tile)], 0)


def stack_heads(pair):
    half = pair.shape[1] // 2
    return jnp.concatenate([pair[:, :half], pair[:, half:]], 0)


def halves(values):
    high = values.astype(BF)
    return high, (values - high.astype(F32)).astype(BF)


SENTINEL = 1e30
SUB = 128
INSIDE = 128


def three(form, a, b):
    (ah, al), (bh, bl) = halves(a), halves(b)
    return form(ah, bh) + (form(ah, bl) + form(al, bh))


def parts_of(v, n):
    q = jnp.floor((v + 0.5) * (1.0 / n))
    return q, v - q * n


def count_down(rows, cols=128):
    return lax.broadcasted_iota(jnp.int32, (rows, cols), 0).astype(F32)


def count_along(rows, cols):
    return lax.broadcasted_iota(jnp.int32, (rows, cols), 1).astype(F32)


def widen(v, cols):
    return jnp.concatenate([v] * -(-cols // 128), 1)[:, :cols]


def layout(rows, groups):
    bins = rows // SUB
    main = rows if bins % 4 else rows * 3 // 4
    return main, lambda g: ((0, main, g * main), (main, rows - main, groups * main + g * (rows - main)))


def pack(x, length):
    rows = x.shape[0]
    valid = x[:, :128] < 0.5 * SENTINEL
    along = jnp.where(valid, 1.0, 0.0).T[:8]
    pair = parts_of(count_down(rows), length)[0]
    pair_down = widen(pair, rows)
    pair_along, place = parts_of(count_along(8, rows), length)
    row = jnp.broadcast_to(pair_along[:1], (rows, rows))
    count = nn(along.astype(BF), (pair_down == row).astype(BF))
    upto = nn(along.astype(BF), (pair_down <= row).astype(BF))
    base = jnp.zeros((8, 1), F32)
    at = upto - count
    for b in range(1, rows // SUB):
        new = jnp.max(jnp.where(upto <= base + SUB, upto, 0.0), 1, keepdims=True)
        at = jnp.where(upto > new, upto - count - new + b * SUB, at)
        base = new
    at = jnp.where(along > 0, at + place, -1.0)
    pick = (widen(count_down(rows), rows) == jnp.broadcast_to(at[:1], (rows, rows))).astype(BF)
    packed = nn(pick, jnp.where(x < 0.5 * SENTINEL, x, 0.0).astype(BF))
    return packed, nn(pick, (pair + 1.0).astype(BF)) - 1.0, pick, jnp.max(at)


def forward_kernel(length, group, groups, x_ref, g1_ref, g2_ref, dmw_ref, dh_ref, *refs):
    qkv_h, out_h, up_h, oqkv_h, oout_h, oup_h = refs[:6]
    refs = refs[6:]
    if group:
        gsumi_ref, gaini_ref, flagi_ref = refs[:3]
        refs = refs[13:]
    a1t_h, qkv_o, p_o, do_o, a2t_h, du_h, ot_h, dattn_h, dux_h, otx_h, gsum_ref, gain_ref, flag_ref = refs[:13]
    refs = refs[13:]
    tail = group == groups - 1
    if tail:
        send_h = refs[0]
        refs = refs[1:]
    if group == 0:
        own_ref, pick_ref = refs[:2]
        refs = refs[2:]
    (x_s, id_s, qkv_s, p_s, o_s, h1_s, da2_s, a2_s, do_s, a1t_s, a2t_s, ot_s, du_s, dattn_s, wqkv_s, wout_s, wup_s,
     load_sem, early_sem, keep_sem) = refs[:20]
    if tail:
        send_ref, send_sem = refs[20:]
    rows, width = x_ref.shape
    hidden = wup_s.shape[1]
    pairs = rows // length
    before = gsum_ref.shape[0] - pairs
    half = width // 2
    tiles = half // 128
    main, where = layout(rows, groups)
    g1 = g1_ref[...].reshape(1, width)
    g2 = g2_ref[...].reshape(1, width)

    pieces = []
    for g, h in enumerate((qkv_h, oqkv_h)):
        for k in range(3):
            at = (3 * g + k) * half
            pieces.append((h.at[k], wqkv_s.at[:, at:at + half]))
    pieces += [(out_h, wout_s.at[:half]), (oout_h, wout_s.at[half:])]
    pieces += [(up_h, wup_s.at[:, :hidden // 2]), (oup_h, wup_s.at[:, hidden // 2:])]
    loads = [pltpu.make_async_copy(h, v, load_sem.at[i]) for i, (h, v) in enumerate(pieces)]
    for c in loads:
        c.start()
    early = []
    if group and tail:
        mine, other = slice(0, hidden // 2), slice(hidden // 2, hidden)
        for g in range(group):
            for i, (_, size, at) in enumerate(where(g)):
                if size:
                    cut = slice(at, at + size)
                    for j, (h, v, index) in enumerate((
                        (a2t_h, a2t_s, (slice(None), cut)), (dux_h, du_s.at[:, other], (cut,)),
                        (otx_h, ot_s.at[half:], (slice(None), cut)), (dattn_h, dattn_s, (cut,)),
                    )):
                        early.append(pltpu.make_async_copy(h.at[index], v.at[index], early_sem.at[8 * g + 4 * i + j]))
        for c in early:
            c.start()

    packed, ids, pick, top = pack(x_ref[...].astype(F32), length)
    x_s[...] = packed
    id_s[...] = ids
    more = top >= main
    flag_ref[0, 0] = jnp.where(more, 1, 0)
    gsum_ref[before:, :] = jnp.zeros((pairs, hidden), F32)
    gain_ref[...] = jnp.zeros_like(gain_ref)
    if group:
        gsum_ref[:before, :] = gsumi_ref[...]
        gain_ref[...] = gaini_ref[...]
    if group == 0:
        own = own_ref.shape[0]
        pick_ref[...] = jnp.zeros_like(pick_ref)
        pick_ref[:, :own] = pick[:own, :own]

    def columns(g, kind, t):
        start = g * 3 * half + kind * half + t * 128
        return slice(start, start + 128)

    def keeps(part):
        start, size, at = where(group)[part]
        src, dst = slice(start, start + size), slice(at, at + size)
        every = slice(None)
        return [
            pltpu.make_async_copy(v.at[i], h.at[j], keep_sem.at[10 * part + k])
            for k, (v, h, i, j) in enumerate((
                (a1t_s, a1t_h, (every, src), (every, dst)),
                (qkv_s, qkv_o, (src,), (dst,)),
                (p_s, p_o, (slice(start // SUB, (start + size) // SUB),), (slice(at // SUB, (at + size) // SUB),)),
                (a2t_s, a2t_h, (every, dst), (every, dst)),
                (ot_s, ot_h, (slice(0, half), dst), (every, dst)),
                (du_s, du_h, (dst, slice(0, hidden // 2)), (dst,)),
                (dattn_s, dattn_h, (dst,), (dst,)),
                (do_s, do_o, (src,), (dst,)),
                (du_s, dux_h, (dst, slice(hidden // 2, hidden)), (dst,)),
                (ot_s, otx_h, (slice(half, width), dst), (every, dst)),
            )[:8 if tail else 10])
        ]

    def work(part):
        start, size, at = where(group)[part]
        here, there = slice(start, start + size), slice(at, at + size)
        store = keeps(part)
        x = x_s[here, :]
        a1 = (normalize(x)[0] * g1).astype(BF)
        a1t_s[:, here] = a1.T
        store[0].start()
        if part == 0:
            for c in loads[:6]:
                c.wait()
        qkv_s[here, :] = nn(a1, wqkv_s[...]).astype(BF)
        store[1].start()
        down = id_s[here, :]
        along = id_s[here, :].T[:1]

        def bin_of(s, carry):
            cut = pl.ds(pl.multiple_of(start + s * SUB, SUB), SUB)
            m = id_s[cut, :] == id_s[cut, :].T
            m = jnp.concatenate([m, m], 1)
            for g in range(2):
                for t in range(tiles):
                    q2 = qkv_s[cut, columns(g, 0, t)]
                    k2 = qkv_s[cut, columns(g, 1, t)]
                    v2 = qkv_s[cut, columns(g, 2, t)]
                    st = nt(k2, two_heads(q2)) * HEAD ** (-0.5)
                    st = jnp.where(m, st, -1000000000.0)
                    e = jnp.exp(st - jnp.max(st, 0, keepdims=True))
                    p = (e * (1.0 / jnp.sum(e, 0, keepdims=True))).astype(BF)
                    p_s[start // SUB + s, g * tiles + t] = p
                    col = g * half + t * 128
                    o_s[cut, col:col + 128] = tn(stack_heads(p), two_heads(v2)).astype(BF)
            return carry

        lax.fori_loop(0, size // SUB, bin_of, 0)
        store[2].start()
        if part == 0:
            for c in loads[6:8]:
                c.wait()
        h1 = x + nn(o_s[here, :], wout_s[...])
        h1_s[here, :] = h1
        a2_s[here, :] = (normalize(h1)[0] * g2).astype(BF)
        ot_s[:, there] = o_s[here, :].T
        a2t_s[:, there] = a2_s[here, :].T
        store[3].start()
        store[4].start()

        lanes = lax.broadcasted_iota(jnp.int32, (size, 2 * pairs), 1)
        lanes = jnp.where(lanes < pairs, lanes, lanes - pairs).astype(F32)
        spread = (jnp.broadcast_to(down[:, :1], lanes.shape) == lanes).astype(BF)
        subl = lax.broadcasted_iota(jnp.int32, (pairs, size), 0).astype(F32)
        gather = (jnp.broadcast_to(along, subl.shape) == subl).astype(BF)
        piece = 1024
        if part == 0:
            for c in loads[8:]:
                c.wait()
        def feed(j, carry):
            cols = pl.ds(pl.multiple_of(j * piece, piece), piece)
            u = nn(a2_s[here, :], wup_s[:, cols])
            cdf = 0.5 + 0.5 * lax.erf(u * 0.5 ** 0.5)
            g = (u * cdf).astype(BF)
            slope = cdf + u * (jnp.exp(-0.5 * u * u) * 0.3989422804014327)
            gsum_ref[before:, cols] += nn(gather, g)
            du = (nn(spread, dmw_ref[:, cols]) * slope).astype(BF)
            du_s[there, cols] = du
            da2_s[:size, :] += nt(du, wup_s[:, cols])
            return carry

        da2_s[:size, :] = jnp.zeros((size, width), F32)
        lax.fori_loop(0, hidden // piece, feed, 0)
        da2 = da2_s[:size, :]
        store[5].start()
        if not tail:
            store[8].start()
            store[9].start()
        xhat2, inv2 = normalize(h1_s[here, :])
        gain_ref[:1, :] += jnp.sum(da2 * xhat2, 0, keepdims=True)
        dh1 = nn(spread, dh_ref[...]) + normalize_pull(da2 * g2, xhat2, inv2)
        dattn_s[there, :] = dh1.astype(BF)
        store[6].start()
        do_s[here, :] = nt(dattn_s[there, :], wout_s[...]).astype(BF)
        store[7].start()
        if group == 0 and part == 0:
            own_ref[...] = dh1[:own_ref.shape[0]]

    work(0)
    if main < rows:
        pl.when(more)(lambda: work(1))

        @pl.when(jnp.logical_not(more))
        def _():
            start, size, at = where(group)[1]
            a1t_s[:, start:] = jnp.zeros((width, size), BF)
            a2t_s[:, at:at + size] = jnp.zeros((width, size), BF)
            ot_s[:, at:at + size] = jnp.zeros((width, size), BF)
            du_s[at:at + size, :] = jnp.zeros((size, hidden), BF)
            dattn_s[at:at + size, :] = jnp.zeros((size, width), BF)
            for c in keeps(1):
                c.start()
    if tail:
        for c in early:
            c.wait()
        whole = groups * main
        at = width + half // 2
        blocks = ((0, half), (half, half), (width, half // 2), (at, send_ref.shape[0] - at))
        leave = [
            pltpu.make_async_copy(send_ref.at[pl.ds(i, n)], send_h.at[pl.ds(i, n)], send_sem.at[k])
            for k, (i, n) in enumerate(blocks)
        ]
        for i in range(2):
            send_ref[i * half:(i + 1) * half, :] = nn(a2t_s[i * half:(i + 1) * half, :whole], du_s[:whole, hidden // 2:])
            leave[i].start()
        out = nn(ot_s[half:, :whole], dattn_s[:whole, :])
        send_ref[width:at, :width] = out[:half // 2]
        send_ref[width:at, width:] = out[half // 2:]
        leave[2].start()
        if main < rows:
            any_more = more
            if group:
                any_more = jnp.logical_or(more, flagi_ref[0, 0] > 0)

            @pl.when(any_more)
            def _():
                for c in leave[:3]:
                    c.wait()
                out = nn(ot_s[half:, whole:], dattn_s[whole:, :])
                send_ref[:width, :] += nn(a2t_s[:, whole:], du_s[whole:, hidden // 2:])
                send_ref[width:at, :width] += out[:half // 2]
                send_ref[width:at, width:] += out[half // 2:]
                for c in leave[:3]:
                    c.start()

            flag_ref[0, 0] = jnp.where(any_more, 1, 0)
        count = gsum_ref.shape[0]
        send_ref[at:, :] = jnp.zeros((send_ref.shape[0] - at, hidden // 2), F32)
        send_ref[at:at + count, :] = gsum_ref[:, hidden // 2:]
        send_ref[at + count:at + count + 8, :width] = gain_ref[...]
        leave[3].start()
        for c in leave:
            c.wait()
    for part in range(2 if main < rows else 1):
        for c in keeps(part):
            c.wait()


def text_forward(x, length, g1, g2, dmw, dh, weights, own, groups=1, group=0, before=None):
    rows, width = x.shape
    pairs = rows // length
    hidden = dmw.shape[1]
    half = width // 2
    total = rows * groups
    tail = group == groups - 1
    count = (group + 1) * pairs
    units = width // 128
    bins = rows // SUB
    whole = lambda a: pl.BlockSpec(memory_space=pltpu.VMEM)
    vmem = pl.BlockSpec(memory_space=pltpu.VMEM)
    smem = pl.BlockSpec(memory_space=pltpu.SMEM)
    hbm = pl.BlockSpec(memory_space=pl.ANY)
    shape = jax.ShapeDtypeStruct
    at_group = lambda cols: pl.BlockSpec((2 * pairs, cols), lambda i: (group, 0))
    every = lambda a: pl.BlockSpec(a.shape, lambda i: (0,) * len(a.shape))
    fixed = lambda *s: pl.BlockSpec(s, lambda i: (0,) * len(s))
    kept = () if before is None else tuple(before[10:13]) + tuple(before[:10])
    kept_specs = [] if before is None else [every(before[10]), every(before[11]), smem] + [hbm] * 10
    ends, end_specs = (), ()
    if tail:
        send = (width + half // 2 + -(-(count + 8) // 96) * 96, hidden // 2)
        ends, end_specs = (shape(send, F32),), (hbm,)
    if group == 0:
        ends += (shape((own, width), F32), shape((own, 128), BF))
        end_specs += (fixed(own, width), fixed(own, 128))
    held = total
    return pl.pallas_call(
        functools.partial(forward_kernel, length, group, groups),
        grid=(1,),
        out_shape=(
            shape((width, total), BF), shape((total, 3 * width), BF), shape((total // SUB, units, SUB, 2 * SUB), BF),
            shape((total, width), BF), shape((width, total), BF), shape((total, hidden // 2), BF),
            shape((half, total), BF), shape((total, width), BF), shape((total, hidden // 2), BF),
            shape((half, total), BF), shape((count, hidden), F32), shape((8, width), F32),
            shape((1, 1), jnp.int32),
        ) + ends,
        in_specs=[every(x), every(g1), every(g2), at_group(hidden), at_group(width)] + [hbm] * 6 + kept_specs,
        out_specs=(hbm,) * 10 + (fixed(count, hidden), fixed(8, width), smem) + end_specs,
        scratch_shapes=[
            pltpu.VMEM((rows, width), F32),
            pltpu.VMEM((rows, 128), F32),
            pltpu.VMEM((rows, 3 * width), BF),
            pltpu.VMEM((bins, units, SUB, 2 * SUB), BF),
            pltpu.VMEM((rows, width), BF),
            pltpu.VMEM((rows, width), F32),
            pltpu.VMEM((rows, width), F32),
            pltpu.VMEM((rows, width), BF),
            pltpu.VMEM((rows, width), BF),
            pltpu.VMEM((width, rows), BF),
            pltpu.VMEM((width, held), BF),
            pltpu.VMEM((width, held), BF),
            pltpu.VMEM((held, hidden), BF),
            pltpu.VMEM((held, width), BF),
            pltpu.VMEM((width, 3 * width), BF),
            pltpu.VMEM((width, width), BF),
            pltpu.VMEM((width, hidden), BF),
            pltpu.SemaphoreType.DMA((10,)),
            pltpu.SemaphoreType.DMA((8 * groups,)),
            pltpu.SemaphoreType.DMA((20,)),
        ] + ([pltpu.VMEM(send, F32), pltpu.SemaphoreType.DMA((4,))] if tail else []),
        input_output_aliases={} if before is None else {14 + i: i for i in range(10)},
        cost_estimate=cost(22),
        compiler_params=pltpu.CompilerParams(vmem_limit_bytes=58 * MIB),
        name="text_forward",
    )(x, g1, g2, dmw, dh, *weights, *kept)


def backward_kernel(
    whole, more_ref, x_ref, dh1_ref, pick_ref, g1_ref, qkv_h, p_h, do_h, a1t_h, wqkv_h, woqkv_h,
    own_h, send_h, small_ref, qkv_s, p_s, do_s, a1t_s, dqkv_s, wqkv_s, own_ref, send_ref, load_sem, row_sem, out_sem,
):
    bins = p_s.shape[0]
    main = whole // SUB
    width = do_s.shape[1]
    half = width // 2
    tiles = half // 128

    def rows_of(b):
        return pl.ds(pl.multiple_of(b * SUB, SUB), SUB)

    def bin_loads(b):
        at = rows_of(b)
        return [
            pltpu.make_async_copy(qkv_h.at[at], qkv_s.at[at], row_sem.at[3 * b]),
            pltpu.make_async_copy(p_h.at[b], p_s.at[b], row_sem.at[3 * b + 1]),
            pltpu.make_async_copy(do_h.at[at], do_s.at[at], row_sem.at[3 * b + 2]),
        ]

    for b in range(main):
        for c in bin_loads(b):
            c.start()
    pieces = [(a1t_h, a1t_s)]
    for g, h in enumerate((wqkv_h, woqkv_h)):
        for k in range(3):
            at = (3 * g + k) * half
            pieces.append((h.at[k], wqkv_s.at[:, at:at + half]))
    loads = [pltpu.make_async_copy(h, v, load_sem.at[i]) for i, (h, v) in enumerate(pieces)]
    for c in loads:
        c.start()

    def columns(g, kind, t):
        start = g * 3 * half + kind * half + t * 128
        return slice(start, start + 128)

    def work(b):
        for c in bin_loads(b):
            c.wait()
        at = rows_of(b)
        for g in range(2):
            for t in range(tiles):
                q2 = qkv_s[at, columns(g, 0, t)]
                k2 = qkv_s[at, columns(g, 1, t)]
                v2 = qkv_s[at, columns(g, 2, t)]
                col = g * half + t * 128
                do2 = two_heads(do_s[at, col:col + 128])
                dp = nt(v2, do2)
                p_low = p_s[b, g * tiles + t]
                p = p_low.astype(F32)
                ds = (p * (dp - jnp.sum(dp * p, 0, keepdims=True))).astype(BF)
                dqkv_s[at, columns(g, 2, t)] = nn(p_low, do2).astype(BF)
                dqkv_s[at, columns(g, 1, t)] = (nn(ds, two_heads(q2)) * HEAD ** (-0.5)).astype(BF)
                dqkv_s[at, columns(g, 0, t)] = (
                    tn(stack_heads(ds), two_heads(k2)) * HEAD ** (-0.5)
                ).astype(BF)

    def step(b, carry):
        work(b)
        return carry

    lax.fori_loop(0, main, step, 0)
    for c in loads:
        c.wait()
    own = x_ref.shape[0]
    pick = pick_ref[:, :own].astype(F32)

    def unpack(v):
        return lax.dot_general(pick, v, (((0,), (0,)), ((), ())), precision=HIGHEST, preferred_element_type=F32)

    da1 = unpack(nt(dqkv_s[:own, :], wqkv_s[...]))
    x = x_ref[...].astype(F32)
    xhat, inv = normalize(jnp.where(x < 0.5 * SENTINEL, x, 0.0))
    small_ref[:own, :] = unpack(dh1_ref[...]) + normalize_pull(da1 * g1_ref[...].reshape(1, width), xhat, inv)

    def leave(k):
        cut = pl.ds(k * width, width)
        return [
            pltpu.make_async_copy(own_ref.at[cut], own_h.at[cut], out_sem.at[2 * k]),
            pltpu.make_async_copy(send_ref.at[cut], send_h.at[cut], out_sem.at[2 * k + 1]),
        ]

    def gradients(k, rows, add):
        if add:
            for c in leave(k):
                c.wait()
        gain = jnp.zeros((width, 128), F32)
        for g in (1, 0):
            at = (3 * g + k) * half
            grad = nn(a1t_s[:, rows], dqkv_s[rows, at:at + half])
            into = send_ref if g else own_ref
            cut = slice(k * width, (k + 1) * width)
            into[cut, :] = into[cut, :] + grad if add else grad
            for j in range(half // 128):
                piece = slice(j * 128, (j + 1) * 128)
                gain += grad[:, piece] * wqkv_s[:, at + j * 128:at + (j + 1) * 128].astype(F32)
        for c in leave(k):
            c.start()
        return jnp.sum(gain.T, 0, keepdims=True) / g1_ref[...].reshape(1, width)

    small_ref[own:, :] = jnp.zeros((small_ref.shape[0] - own, width), F32)
    small_ref[own:own + 1, :] = sum(gradients(k, slice(0, whole), False) for k in range(3))
    if main < bins:
        @pl.when(more_ref[0, 0] > 0)
        def _():
            for b in range(main, bins):
                for c in bin_loads(b):
                    c.start()
            lax.fori_loop(main, bins, step, 0)
            small_ref[own:own + 1, :] += sum(gradients(k, slice(whole, bins * SUB), True) for k in range(3))
    at = 3 * width
    send_ref[at:, :] = jnp.zeros((send_ref.shape[0] - at, half), F32)
    count = small_ref.shape[0]
    send_ref[at:at + count, :] = small_ref[:, :half]
    send_ref[at + count:at + 2 * count, :] = small_ref[:, half:]
    rest = pltpu.make_async_copy(send_ref.at[pl.ds(at, 2 * count)], send_h.at[pl.ds(at, 2 * count)], out_sem.at[6])
    rest.start()
    for k in range(3):
        for c in leave(k):
            c.wait()
    rest.wait()


def text_backward(whole, more, x, dh1, pick, g1, qkv, p, do, a1t, wqkv, oqkv):
    total, width = do.shape
    half = width // 2
    own = dh1.shape[0]
    count = own + 8
    every = lambda a: pl.BlockSpec(a.shape, lambda i: (0,) * len(a.shape))
    fixed = lambda *s: pl.BlockSpec(s, lambda i: (0,) * len(s))
    hbm = pl.BlockSpec(memory_space=pl.ANY)
    smem = pl.BlockSpec(memory_space=pltpu.SMEM)
    shape = jax.ShapeDtypeStruct
    bins, units = p.shape[:2]
    return pl.pallas_call(
        functools.partial(backward_kernel, whole),
        grid=(1,),
        out_shape=(
            shape((3 * width, half), F32), shape((3 * width + 2 * count, half), F32), shape((count, width), F32),
        ),
        in_specs=[smem, fixed(own, width), every(dh1), every(pick), every(g1)] + [hbm] * 6,
        out_specs=(hbm, hbm, fixed(count, width)),
        scratch_shapes=[
            pltpu.VMEM((total, 3 * width), BF),
            pltpu.VMEM((bins, units, SUB, 2 * SUB), BF),
            pltpu.VMEM((total, width), BF),
            pltpu.VMEM((width, total), BF),
            pltpu.VMEM((total, 3 * width), BF),
            pltpu.VMEM((width, 3 * width), BF),
            pltpu.VMEM((3 * width, half), F32),
            pltpu.VMEM((3 * width + 2 * count, half), F32),
            pltpu.SemaphoreType.DMA((7,)),
            pltpu.SemaphoreType.DMA((3 * bins,)),
            pltpu.SemaphoreType.DMA((7,)),
        ],
        cost_estimate=cost(20),
        compiler_params=pltpu.CompilerParams(vmem_limit_bytes=58 * MIB),
        name="text_backward",
    )(more, x, dh1, pick, g1, qkv, p, do, a1t, wqkv, oqkv)


def feed_kernel(
    a2t_ref, du_ref, upi_ref, ot_ref, dattn_ref, outa_ref, outb_ref, gsum_ref, gsumi_ref, dm_ref, low_ref, gh_ref,
    up_ref, out_ref, down_ref, proj_ref,
):
    up_ref[...] = upi_ref[...] + nn(a2t_ref[...], du_ref[...])
    quarter = outa_ref.shape[0]
    out = nn(ot_ref[...], dattn_ref[...])
    out_ref[:quarter, :] = out[:quarter] + outa_ref[...]
    out_ref[quarter:, :] = out[quarter:] + outb_ref[...]
    mine = gsum_ref.shape[0]
    high, rest = halves(jnp.concatenate([gsum_ref[...], gsumi_ref[:mine]], 0))
    down_ref[...] = tn(high, dm_ref[...]) + tn(rest, dm_ref[...])
    proj_ref[...] = tn(low_ref[...], gh_ref[...])


def feed_grads(a2t, du, ot, dattn, got, gsum, dm, low, gh):
    width, total = a2t.shape
    hidden = du.shape[1]
    half = width // 2
    quarter = half // 2
    mine = gsum.shape[0]
    steps = 3
    tile = hidden // steps
    slim = width // steps
    rest = got.shape[0] - width - quarter
    whole = lambda a: pl.BlockSpec(a.shape, lambda i: (0,) * len(a.shape), pipeline_mode=pl.Buffered(1))
    shape = jax.ShapeDtypeStruct
    columns = lambda rows, cols, row=0, col=0: pl.BlockSpec((rows, cols), lambda i: (row, col + i))
    return pl.pallas_call(
        feed_kernel,
        grid=(steps,),
        out_shape=(
            shape((width, hidden), F32), shape((half, width), F32), shape((hidden, width), F32), shape((width, half), F32),
        ),
        in_specs=[
            whole(a2t), columns(total, tile), columns(width, tile),
            pl.BlockSpec((half, total), lambda i: (0, 0), pipeline_mode=pl.Buffered(1)), columns(total, slim),
            columns(quarter, slim, width // quarter), columns(quarter, slim, width // quarter, steps),
            columns(mine, tile), columns(rest, tile, (width + quarter) // rest), whole(dm), columns(low.shape[0], slim),
            whole(gh),
        ],
        out_specs=(
            columns(width, tile), columns(half, slim), pl.BlockSpec((tile, width), lambda i: (i, 0)),
            pl.BlockSpec((slim, half), lambda i: (i, 0)),
        ),
        cost_estimate=cost(9),
        compiler_params=pltpu.CompilerParams(vmem_limit_bytes=28 * MIB),
        name="feed_grads",
    )(a2t, du, got, ot, dattn, got, got, gsum, got, dm, low, gh)


def finish_kernel(
    own_ref, in_ref, small_ref, smalla_ref, smallb_ref, gain2_ref, gain2i_ref, loss_ref, temp_ref,
    qkv_ref, rows_ref, gain1o_ref, gain2o_ref, losso_ref, tempo_ref,
):
    qkv_ref[0] = own_ref[...] + in_ref[...]
    core = lax.axis_index("mp")
    own = rows_ref.shape[0] // 2
    half = gain1o_ref.shape[0]

    @pl.when(pl.program_id(0) == 0)
    def _():
        got = jnp.concatenate([smalla_ref[...], smallb_ref[...]], 1)
        rows_ref[:own, :] = jnp.where(core == 0, small_ref[:own], got[:own])
        rows_ref[own:, :] = jnp.where(core == 0, got[:own], small_ref[:own])
        losso_ref[...] = loss_ref[...]
        tempo_ref[...] = temp_ref[...]
        one = small_ref[own:own + 1, :] + got[own:own + 1, :]
        two = gain2_ref[:1, :] + gain2i_ref[:1, :2 * half]
        gain1o_ref[...] = jnp.where(core == 0, one[:, :half], one[:, half:]).reshape(half)
        gain2o_ref[...] = jnp.where(core == 0, two[:, :half], two[:, half:]).reshape(half)


def finish(own, got, small, gain2, other, at, loss, temp):
    count, width = small.shape
    rows = count - 8
    half = width // 2
    whole = lambda a: pl.BlockSpec(a.shape, lambda i: (0,) * len(a.shape), pipeline_mode=pl.Buffered(1))
    fixed = lambda *shape: pl.BlockSpec(shape, lambda i: (0,) * len(shape))
    piece = pl.BlockSpec((width, half), lambda i: (i, 0))
    start = 3 * width // count
    shape = jax.ShapeDtypeStruct
    return pl.pallas_call(
        finish_kernel,
        grid=(3,),
        out_shape=(shape((3, width, half), F32), shape((2 * rows, width), F32), shape((half,), F32), shape((half,), F32)) + (shape((1, 1), F32),) * 2,
        in_specs=[
            piece, piece, whole(small), pl.BlockSpec((count, half), lambda i: (start, 0)),
            pl.BlockSpec((count, half), lambda i: (start + 1, 0)), whole(gain2),
            pl.BlockSpec((8, other.shape[1]), lambda i: (at // 8, 0)), whole(loss), whole(temp),
        ],
        out_specs=(pl.BlockSpec((1, width, half), lambda i: (i, 0, 0)), fixed(2 * rows, width), fixed(half), fixed(half), fixed(1, 1), fixed(1, 1)),
        cost_estimate=cost(4),
        compiler_params=pltpu.CompilerParams(vmem_limit_bytes=24 * MIB),
        name="finish",
    )(own, got, small, got, got, gain2, other, loss, temp)


MESH = pl.DeviceIdType.MESH


def chip_grid(mesh):
    chips = mesh.devices.reshape(-1, mesh.shape["mp"])[:, 0]
    places = [getattr(d, "coords", None) for d in chips]
    if all(p is not None and len(p) == 3 for p in places):
        grid = tuple(len({p[i] for p in places}) for i in (2, 1, 0))
        if grid[0] * grid[1] * grid[2] == len(chips):
            return grid
    side = 1
    while (2 * side) ** 3 <= len(chips):
        side *= 2
    return (len(chips) // (side * side), side, side)


class Spread:
    def __init__(self, grid, place, core, block, send, recv, first):
        self.grid, self.place, self.core = grid, place, core
        self.block, self.send, self.recv = block, send, recv
        self.first = first
        self.sent = []
        zs, ys, xs = grid
        self.turn = ys == xs
        self.aorder = list(range(1, ys))
        zevents = [("z", d, None) for d in range(1, zs)]
        aevents = [[("a", d, a) for d in range(zs)] for a in self.aorder]
        self.pending = []
        for i in range(zs + len(aevents)):
            self.pending += zevents[i:i + 1]
            for j, events in enumerate(aevents):
                self.pending += events[i - j:i - j + 1] if i >= j else []

    def slot(self, kz, ka):
        return kz * self.grid[1] + ka

    def target(self, dz, da):
        zs, ys, xs = self.grid
        z, y, x = self.place
        dy, dx = (da * (1 - self.core), da * self.core) if self.turn else (da, 0)
        batch = (lax.rem(z + dz, zs) * ys + lax.rem(y + dy, ys)) * xs + lax.rem(x + dx, xs)
        return (batch, self.core)

    def copy(self, source, landing, to, when=None):
        index = len(self.sent)

        def make():
            return pltpu.make_async_remote_copy(
                src_ref=self.first if source is None else self.block(self.slot(*source)),
                dst_ref=self.block(self.slot(*landing)), send_sem=self.send.at[index],
                recv_sem=self.recv.at[self.slot(*landing)], device_id=self.target(*to), device_id_type=MESH,
            )

        if when is None:
            make().start()
        else:
            pl.when(when)(lambda: make().start())
        self.sent.append((make, when))

    def forward(self, source, kz, when=None):
        for d in self.aorder:
            self.copy(source, (kz, self.grid[1] - d), (0, d), when)

    def start(self):
        zs = self.grid[0]
        z = self.place[0]
        if zs > 1:
            self.copy(None, (zs - 1, 0), (1, 0), z < zs - 1)
            self.copy(None, (1, 0), (zs - 1, 0), z > 0)
        self.forward(None, 0)

    def arrive(self, slot):
        pltpu.make_async_remote_copy(
            src_ref=self.block(slot), dst_ref=self.block(slot), send_sem=self.send.at[0],
            recv_sem=self.recv.at[slot], device_id=self.target(1, 0), device_id_type=MESH,
        ).wait_recv()

    def sides(self, d):
        zs = self.grid[0]
        z = self.place[0]
        return [(d, z + d < zs, True), (zs - d, z - d >= 0, False)]

    def serve(self, count=1):
        zs = self.grid[0]
        z = self.place[0]
        for _ in range(min(count, len(self.pending))):
            kind, d, a = self.pending.pop(0)
            if kind == "a" and d == 0:
                self.arrive(self.slot(0, a))
                continue
            for kz, there, above in self.sides(d):
                slot = self.slot(kz, 0 if kind == "z" else a)
                pl.when(there)(lambda slot=slot: self.arrive(slot))
                if kind == "z":
                    if d + 1 < zs and above:
                        self.copy((kz, 0), (kz + 1, 0), (zs - 1, 0), there & (z > 0))
                    elif d + 1 < zs:
                        self.copy((kz, 0), (kz - 1, 0), (1, 0), there & (z < zs - 1))
                    self.forward((kz, 0), kz, there)

    def finish(self):
        self.serve(len(self.pending))
        for make, when in self.sent:
            if when is None:
                make().wait_send()
            else:
                pl.when(when)(lambda make=make: make().wait_send())

    @staticmethod
    def copies(grid):
        zs, ys, _ = grid
        return 4 * zs + 2 * zs * (ys - 1)


class Hops:
    def __init__(self, grid, place, core, block, send, recv, first):
        self.grid, self.place, self.core = grid, place, core
        self.block, self.send, self.recv = block, send, recv
        self.first = first
        self.sent = []
        zs, ys, xs = grid
        self.turn = ys == xs
        near = []
        for d in range(1, zs // 2 + 1):
            near += [d] if 2 * d == zs else [d, zs - d]
        self.zorder = near
        self.aorder = list(range(1, ys))
        self.border = list(range(1, xs))
        self.pending = [("z", k) for k in near]
        self.pending += [("a", a, k) for a in self.aorder for k in [0] + near]

    def slot(self, kz, ka, kb):
        zs, ys, xs = self.grid
        plain = (kz * ys + ka) * xs + kb
        if not self.turn:
            return plain
        other = (kz * ys + kb) * xs + ka
        return plain if plain == other else plain + self.core * (other - plain)

    def target(self, dz, da, db):
        zs, ys, xs = self.grid
        z, y, x = self.place
        if self.turn and da != db:
            dy = da + self.core * (db - da)
            dx = db + self.core * (da - db)
        else:
            dy, dx = da, db
        batch = (lax.rem(z + dz, zs) * ys + lax.rem(y + dy, ys)) * xs + lax.rem(x + dx, xs)
        return (batch, self.core)

    def copy(self, source, landing, to):
        index = len(self.sent)
        sent = pltpu.make_async_remote_copy(
            src_ref=source, dst_ref=self.block(landing), send_sem=self.send.at[index],
            recv_sem=self.recv.at[landing], device_id=to, device_id_type=MESH,
        )
        sent.start()
        self.sent.append(sent)

    def along_a(self, source, kz):
        ys = self.grid[1]
        for d in self.aorder:
            self.copy(source, self.slot(kz, ys - d, 0), self.target(0, d, 0))

    def along_b(self, source, kz, ka):
        xs = self.grid[2]
        for d in self.border:
            self.copy(source, self.slot(kz, ka, xs - d), self.target(0, 0, d))

    def start(self):
        zs = self.grid[0]
        self.along_b(self.first, 0, 0)
        self.along_a(self.first, 0)
        for d in self.zorder:
            self.copy(self.first, self.slot(zs - d, 0, 0), self.target(d, 0, 0))

    def arrive(self, slot):
        pltpu.make_async_remote_copy(
            src_ref=self.block(slot), dst_ref=self.block(slot), send_sem=self.send.at[0],
            recv_sem=self.recv.at[slot], device_id=self.target(1, 0, 0), device_id_type=MESH,
        ).wait_recv()

    def serve(self, count=1):
        for _ in range(min(count, len(self.pending))):
            event = self.pending.pop(0)
            if event[0] == "z":
                slot = self.slot(event[1], 0, 0)
                self.arrive(slot)
                self.along_b(self.block(slot), event[1], 0)
                self.along_a(self.block(slot), event[1])
            else:
                slot = self.slot(event[2], event[1], 0)
                self.arrive(slot)
                self.along_b(self.block(slot), event[2], event[1])

    def finish(self):
        self.serve(len(self.pending))
        for a in [0] + self.aorder:
            for b in self.border:
                for k in [0] + self.zorder:
                    self.arrive(self.slot(k, a, b))
        for sent in self.sent:
            sent.wait_send()

    @staticmethod
    def copies(grid):
        zs, ys, xs = grid
        return (zs - 1) + zs * (ys - 1) + zs * ys * (xs - 1)


def attend(qkv_ref, o_ref, start, ids, half):
    m = ids == ids.T
    m = jnp.concatenate([m, m], 1)
    rows = pl.ds(start, SUB)
    for t in range(half // 128):
        q2 = qkv_ref[rows, t * 128:(t + 1) * 128]
        k2 = qkv_ref[rows, half + t * 128:half + (t + 1) * 128]
        v2 = qkv_ref[rows, 2 * half + t * 128:2 * half + (t + 1) * 128]
        st = nt(k2, two_heads(q2)) * HEAD ** (-0.5)
        st = jnp.where(m, st, -1000000000.0)
        e = jnp.exp(st - jnp.max(st, 0, keepdims=True))
        p = e * (1.0 / jnp.sum(e, 0, keepdims=True))
        o_ref[rows, t * 128:(t + 1) * 128] = tn(stack_heads(p.astype(BF)), two_heads(v2)).astype(BF)


def front_kernel(
    grid,
    rows_ref, mask_ref, image_ref, g1_ref, g2_ref, temp_ref,
    iqkv_h, iout_h, iup_h, idown_h, tqkv_h, tout_h, tup_h, tdown_h, tproj_h,
    xg_ref, oqkv_h, oout_h, oup_h, dmw_ref, dh_ref, dm_ref, low_ref, gh_ref, loss_ref, temp_ref2,
    iqkv, iout, iup, idown, tqkv, tout, tup, tdown, proj,
    own_x, small, small_abs, payload, qkv_s, o_s, image_x, part, part_in, sums, sums_in,
    wsend_qkv, wsend_out, wsend_up, wsend_proj, wland_qkv, wland_out, wland_up, wland_proj,
    dmw_send, dmw_in, cos_s, tnorm_s, xg,
    load_sem, out_sem, x_send, x_recv, s_send, s_recv, c_send, c_recv, own_sem,
):
    zs, ys, xs = grid
    chips = zs * ys * xs
    planes = zs * ys
    batch, core = lax.axis_index("batch"), lax.axis_index("mp")
    place = (batch // (ys * xs), lax.rem(batch // xs, ys), lax.rem(batch, xs))
    partner = (batch, 1 - core)
    pairs, length = mask_ref.shape
    rows = pairs * length
    width = rows_ref.shape[1]
    half = width // 2
    hidden = tup.shape[1]
    hp = pairs // 2
    hr = hp * length
    total = chips * pairs
    mine = chips * hp
    patches = image_ref.shape[0] // pairs
    padded = image_x.shape[0] // pairs

    inside = total <= INSIDE

    loads = {}
    for i, (name, h, v) in enumerate((
        ("iqkv", iqkv_h, iqkv), ("tqkv", tqkv_h, tqkv), ("iout", iout_h, iout), ("tout", tout_h, tout),
        ("tup", tup_h, tup), ("iup", iup_h, iup), ("idown", idown_h, idown), ("tdown", tdown_h, tdown),
        ("proj", tproj_h, proj.at[core]),
    )):
        loads[name] = pltpu.make_async_copy(h, v, load_sem.at[i])
        if i < 3:
            loads[name].start()

    xg = xg if inside else xg_ref
    gather = Spread(grid, place, core, lambda s: xg.at[s], x_send, x_recv, own_x)
    peers = [partner]
    spread = Hops(grid, place, core, lambda s: small.at[core, s], s_send, s_recv, payload)
    peers += [spread.target(d, 0, 0) for d in range(1, zs)]
    peers += [spread.target(0, d, 0) for d in range(1, ys)]
    peers += [spread.target(0, 0, d) for d in range(1, xs)]
    barrier = pltpu.get_barrier_semaphore()
    for peer in peers:
        pl.semaphore_signal(barrier, inc=1, device_id=peer, device_id_type=MESH)

    mask = mask_ref[...].astype(F32)
    lane = count_along(rows, length)
    sub = parts_of(count_down(rows, length), length)[1]
    spread_mask = jnp.broadcast_to(mask[:, None, :], (pairs, length, length)).reshape(rows, length)
    valid = jnp.sum(jnp.where(lane == sub, spread_mask, 0.0), 1, keepdims=True)
    text_x = rows_ref[...].astype(F32)
    marked = jnp.where(valid > 0, text_x, SENTINEL)
    own_x[...] = jnp.where(core == 0, marked[:hr], marked[hr:])
    top = padded * pairs
    image_of, patch_of = parts_of(count_down(top), padded)
    image_ids = jnp.where(patch_of < patches, image_of, -1.0)
    place_of = jnp.where(patch_of < patches, patch_of * pairs + image_of, -1.0)
    reorder = (widen(place_of, patches * pairs) == count_along(top, patches * pairs)).astype(BF)
    image_x[...] = nn(reorder, image_ref[...])
    image_a1 = normalize(image_x[...])[0].astype(BF)
    pl.semaphore_wait(barrier, len(peers))
    gather.start()

    swaps = []

    def swap(source, landing, index):
        c = pltpu.make_async_remote_copy(
            src_ref=source, dst_ref=landing, send_sem=c_send.at[index], recv_sem=c_recv.at[index],
            device_id=partner, device_id_type=MESH,
        )
        c.start()
        swaps.append(c)
        return c

    def put(ref, cols, high, rest):
        size = mine // 2
        for g in range(2):
            ref[2 * g * size:(2 * g + 1) * size, cols] = high[g * size:(g + 1) * size]
            ref[(2 * g + 1) * size:(2 * g + 2) * size, cols] = rest[g * size:(g + 1) * size]

    def contrast():
        for s in range(chips):
            kz, ky, kx = s // (ys * xs), s // xs % ys, s % xs
            at = (lax.rem(place[0] + kz, zs) * ys + lax.rem(place[1] + ky, ys)) * xs + lax.rem(place[2] + kx, xs)
            small_abs[:, at] = small[:, s]
        low = small_abs[0, :, :, :width].reshape(total, width).astype(BF)
        low_ref[...] = low
        counts = small_abs[0, :, :, width:].reshape(total, 128)[:, :1]
        embed = jnp.concatenate([nn(low, proj[0]), nn(low, proj[1])], 1)
        inv = lax.rsqrt(jnp.sum(embed * embed, 1, keepdims=True) + NORM_EPS)
        tnorm_s[...] = embed * inv
        images = small_abs[1, :, :, :width].reshape(total, width)
        scale = jnp.exp(jnp.full((1, 1), temp_ref[0, 0], F32))
        cos_s[...] = three(nt, tnorm_s[...], images)
        logits = cos_s[...] * scale
        row_top = jnp.max(logits, 1, keepdims=True)
        row_lse = row_top + jnp.log(jnp.sum(jnp.exp(logits - row_top), 1, keepdims=True))
        col_top = jnp.max(logits, 0, keepdims=True)
        col_lse = col_top + jnp.log(jnp.sum(jnp.exp(logits - col_top), 0, keepdims=True))
        eye = (lax.broadcasted_iota(jnp.int32, (total, total), 0) == lax.broadcasted_iota(jnp.int32, (total, total), 1))
        eye = eye.astype(F32)
        pair_grad = (jnp.exp(logits - row_lse) + jnp.exp(logits - col_lse) - 2.0 * eye) * (0.5 / total)

        def everything(v):
            return jnp.sum(jnp.sum(v, 1, keepdims=True), 0, keepdims=True)

        loss = (everything(row_lse) + everything(col_lse) - 2.0 * everything(logits * eye)) * (0.5 / total)
        temp = scale * everything(pair_grad * cos_s[...])
        loss_ref[...] = loss
        temp_ref2[...] = temp
        grad_norm = scale * three(nn, pair_grad, images)
        tnorm = tnorm_s[...]
        grad_embed = ((grad_norm - tnorm * jnp.sum(tnorm * grad_norm, 1, keepdims=True)) * inv).astype(BF)
        gh_ref[...] = jnp.where(core == 0, grad_embed[:, :half], grad_embed[:, half:])
        dh = (nt(grad_embed[:, :half], proj[0]) + nt(grad_embed[:, half:], proj[1])) / counts
        dm = dh.astype(BF)

        r = count_along(8, total)
        here = core.astype(F32)
        owner = jnp.where(r < mine, here, 1.0 - here)
        k, i = parts_of(parts_of(r, mine)[1], hp)
        kb, rest = parts_of(k, planes)
        kz, ka = parts_of(rest, ys)
        ky, kx = (jnp.where(owner == 0, ka, kb), jnp.where(owner == 0, kb, ka)) if ys == xs else (ka, kb)
        z, y, x = (parts_of(v + p.astype(F32), n)[1] for v, p, n in zip((kz, ky, kx), place, grid))
        at = ((z * ys + y) * xs + x) * pairs + owner * hp + i
        pick = (jnp.broadcast_to(at[:1], (total, total)).T == count_along(total, total)).astype(BF)
        dm_sorted = nn(pick, dm).astype(BF)
        dm_ref[...] = dm_sorted
        dmw = nt(dm_sorted, tdown[...])
        dmw_send[...] = dmw[mine:]
        dmw_swap = swap(dmw_send, dmw_in, 8)
        dh_high, dh_low = halves(dh)
        put(dh_ref, slice(None), nn(pick[:mine], dh_high).astype(BF), nn(pick[:mine], dh_low).astype(BF))
        put(dmw_ref, slice(0, hidden), *halves(dmw[:mine]))
        return dmw_swap

    g1, g2 = g1_ref[...].reshape(1, width), g2_ref[...].reshape(1, width)
    loads["iqkv"].wait()
    for name in list(loads)[3:]:
        loads[name].start()
    for k in range(3):
        qkv_s[:, k * half:(k + 1) * half] = nn(image_a1, iqkv[k]).astype(BF)
    loads["tqkv"].wait()
    for k in range(3):
        wsend_qkv[k] = tqkv[k].astype(F32)
    qkv_swap = swap(wsend_qkv, wland_qkv, 3)
    loads["iout"].wait()
    parts = 2
    cut = top // parts
    image_swaps = []
    for i in range(parts):
        for s in range(i * cut // SUB, (i + 1) * cut // SUB):
            attend(qkv_s, o_s, s * SUB, image_ids[s * SUB:(s + 1) * SUB], half)
        at = pl.ds(i * cut, cut)
        part[at, :] = nn(o_s[at, :], iout[...])
        image_swaps.append(swap(part.at[at], part_in.at[at], i))

    a1 = (normalize(text_x)[0] * g1).astype(BF)
    for k in range(3):
        qkv_s[:rows, k * half:(k + 1) * half] = nn(a1, tqkv[k]).astype(BF)
    attend(qkv_s, o_s, 0, jnp.where(valid > 0, parts_of(count_down(rows), length)[0], -1.0), half)
    loads["tout"].wait()
    part[top:, :] = nn(o_s[:rows, :], tout[...])
    text_swap = swap(part.at[pl.ds(top, rows)], part_in.at[pl.ds(top, rows)], 5)
    gather.serve(2)

    loads["tup"].wait()
    up_cut = wsend_up.shape[0] // 4
    up_swaps = []

    def send_up(i):
        at = pl.ds(i * up_cut, up_cut)
        wsend_up[at, :] = tup[at, :].astype(F32)
        up_swaps.append(swap(wsend_up.at[at], wland_up.at[at], 9 + i))

    send_up(0)
    send_up(1)

    piece = 512
    loads["iup"].wait()
    mean_i, bars = [], []
    for i in range(parts):
        image_swaps[i].wait_recv()
        at = pl.ds(i * cut, cut)
        h1 = image_x[at, :] + (part[at, :] + part_in[at, :])
        a2 = normalize(h1)[0].astype(BF)
        mean_i.append(jnp.sum(h1.reshape(pairs // parts, padded, width), 1))
        bar = []
        for j in range(hidden // piece):
            u = nn(a2, iup[:, j * piece:(j + 1) * piece])
            g = (u * (0.5 + 0.5 * lax.erf(u * 0.5 ** 0.5))).astype(BF).astype(F32)
            bar.append(jnp.sum(g.reshape(pairs // parts, padded, piece), 1))
        bars.append(jnp.concatenate(bar, 1))
        gather.serve(1)
    mean_i = jnp.concatenate(mean_i, 0)
    bar = jnp.concatenate(halves(jnp.concatenate(bars, 0)), 0)
    loads["idown"].wait()
    low = nn(bar, idown[...])
    sums[pairs:, :] = low[:pairs] + low[pairs:]

    text_swap.wait_recv()
    h1 = text_x + (part[top:, :] + part_in[top:, :])
    a2 = (normalize(h1)[0] * g2).astype(BF)
    mean_h = jnp.sum((h1 * valid).reshape(pairs, length, width), 1)
    bars = []
    for j in range(hidden // piece):
        u = nn(a2, tup[:, j * piece:(j + 1) * piece])
        g = (u * (0.5 + 0.5 * lax.erf(u * 0.5 ** 0.5))).astype(BF).astype(F32) * valid
        bars.append(jnp.sum(g.reshape(pairs, length, piece), 1))
    bar = jnp.concatenate(halves(jnp.concatenate(bars, 1)), 0)
    loads["tdown"].wait()
    low = nn(bar, tdown[...])
    sums[:pairs, :] = low[:pairs] + low[pairs:]
    sums_swap = swap(sums, sums_in, 6)
    sums_swap.wait_recv()

    count = jnp.sum(mask, 1, keepdims=True)
    pooled = (mean_h + (sums[:pairs, :] + sums_in[:pairs, :])) / count
    e = (mean_i + (sums[pairs:, :] + sums_in[pairs:, :])) * (1.0 / patches)
    image_norm = e * lax.rsqrt(jnp.sum(e * e, 1, keepdims=True) + NORM_EPS)
    payload[:, :width] = jnp.where(core == 0, pooled, image_norm)
    payload[:, width:] = jnp.broadcast_to(count, (pairs, 128))
    spread.start()
    small[core, 0] = payload[...]
    loads["proj"].wait()
    wsend_proj[...] = proj[core].astype(F32)
    proj_swap = swap(wsend_proj, wland_proj, 2)
    wsend_out[...] = tout[...].astype(F32)
    out_swap = swap(wsend_out, wland_out, 4)
    send_up(2)
    send_up(3)
    oqkv, oout, oup = iqkv, iout, iup
    outs = []

    def hand_over(swapped, landed, held, out, index):
        swapped.wait_recv()
        held[...] = landed[...].astype(BF)
        outs.append(pltpu.make_async_copy(held, out, out_sem.at[index]))
        outs[-1].start()

    def hand_up(i):
        at = pl.ds(i * up_cut, up_cut)
        hand_over(up_swaps[i], wland_up.at[at], oup.at[at], oup_h.at[at], 2 + i)

    hand_over(qkv_swap, wland_qkv, oqkv, oqkv_h, 1)
    gather.serve(1)
    spread.serve(zs - 1)
    gather.serve(1)
    hand_up(0)
    hand_up(1)
    spread.serve(len(spread.pending))
    gather.serve(len(gather.pending))
    proj_swap.wait_recv()
    proj[1 - core] = wland_proj[...].astype(BF)
    hand_over(out_swap, wland_out, oout, oout_h, 0)
    spread.finish()
    both_swap = swap(small.at[core], small.at[core], 7)
    hand_up(2)
    both_swap.wait_recv()
    gather.serve(len(gather.pending))
    own_copy = pltpu.make_async_copy(own_x, xg_ref.at[0], own_sem.at[0])
    own_copy.start()
    if inside:
        store = pltpu.make_async_copy(xg.at[pl.ds(1, planes - 1)], xg_ref.at[pl.ds(1, planes - 1)], own_sem.at[1])
        store.start()
    if inside:
        dmw_swap = contrast()
    else:
        dmw_ref[...] = small[...]
        dm_ref[...] = proj[...]

    hand_up(3)
    if inside:
        dmw_swap.wait_recv()
        put(dmw_ref, slice(hidden, 2 * hidden), *halves(dmw_in[...]))
    gather.finish()
    own_copy.wait()
    if inside:
        store.wait()
    for s in swaps:
        s.wait_send()
    for o in outs:
        o.wait()


def front(grid, rows, mask, image, g1, g2, temp, weights):
    chips = grid[0] * grid[1] * grid[2]
    pairs, length = mask.shape
    width = rows.shape[1]
    half = width // 2
    iqkv, iout, iup, idown, tqkv, tout, tup, tdown, tproj = weights
    hidden = tup.shape[1]
    total = chips * pairs
    mine = total // 2
    patches = image.shape[0] // pairs
    padded = -(-patches // 64) * 64
    top = padded * pairs
    hr = pairs // 2 * length
    vmem = pl.BlockSpec(memory_space=pltpu.VMEM)
    hbm = pl.BlockSpec(memory_space=pl.ANY)
    shape = jax.ShapeDtypeStruct
    copies, hops = Spread.copies(grid), Hops.copies(grid)
    inside = total <= INSIDE
    if inside:
        ends = (
            shape((2 * mine, 2 * hidden), BF), shape((2 * mine, width), BF), shape((total, width), BF),
            shape((total, width), BF), shape((total, half), BF), shape((1, 1), F32), shape((1, 1), F32),
        )
    else:
        mine, total = 8, 128
        ends = (shape((2, chips, pairs, width + 128), F32),) + (shape((8, 128), F32),)
        ends += (shape((2,) + tproj.shape, BF),) + (shape((8, 128), F32),) * 4
    return pl.pallas_call(
        functools.partial(front_kernel, grid),
        out_shape=(
            shape((grid[0] * grid[1], hr, width), F32),
            shape(tqkv.shape, BF), shape(tout.shape, BF), shape(tup.shape, BF),
        ) + ends,
        in_specs=[vmem] * 5 + [pl.BlockSpec(memory_space=pltpu.SMEM)] + [hbm] * 9,
        out_specs=[hbm] * 4 + [vmem] * 7,
        scratch_shapes=[
            pltpu.VMEM(iqkv.shape, BF), pltpu.VMEM(iout.shape, BF), pltpu.VMEM(iup.shape, BF), pltpu.VMEM(idown.shape, BF),
            pltpu.VMEM(tqkv.shape, BF), pltpu.VMEM(tout.shape, BF), pltpu.VMEM(tup.shape, BF), pltpu.VMEM(tdown.shape, BF),
            pltpu.VMEM((2,) + tproj.shape, BF),
            pltpu.VMEM((hr, width), F32),
            pltpu.VMEM((2, chips, pairs, width + 128), F32),
            pltpu.VMEM((2, chips if inside else 1, pairs, width + 128), F32),
            pltpu.VMEM((pairs, width + 128), F32),
            pltpu.VMEM((top, 3 * half), BF),
            pltpu.VMEM((top, half), BF),
            pltpu.VMEM((top, width), F32),
            pltpu.VMEM((top + pairs * length, width), F32),
            pltpu.VMEM((top + pairs * length, width), F32),
            pltpu.VMEM((2 * pairs, width), F32),
            pltpu.VMEM((2 * pairs, width), F32),
            pltpu.VMEM(tqkv.shape, F32), pltpu.VMEM(tout.shape, F32), pltpu.VMEM(tup.shape, F32), pltpu.VMEM(tproj.shape, F32),
            pltpu.VMEM(tqkv.shape, F32), pltpu.VMEM(tout.shape, F32), pltpu.VMEM(tup.shape, F32), pltpu.VMEM(tproj.shape, F32),
            pltpu.VMEM((mine, hidden), F32), pltpu.VMEM((mine, hidden), F32),
            pltpu.VMEM((total, total), F32), pltpu.VMEM((total, width), F32),
            pltpu.VMEM((grid[0] * grid[1], hr, width) if inside else (1, 8, 128), F32),
            pltpu.SemaphoreType.DMA((9,)), pltpu.SemaphoreType.DMA((6,)),
            pltpu.SemaphoreType.DMA((copies,)), pltpu.SemaphoreType.DMA((grid[0] * grid[1],)),
            pltpu.SemaphoreType.DMA((hops,)), pltpu.SemaphoreType.DMA((chips,)),
            pltpu.SemaphoreType.DMA((13,)), pltpu.SemaphoreType.DMA((13,)), pltpu.SemaphoreType.DMA((2,)),
        ],
        cost_estimate=cost(40),
        compiler_params=pltpu.CompilerParams(collective_id=0, has_side_effects=True, vmem_limit_bytes=60 * MIB),
        name="front",
    )(rows, mask, image, g1, g2, temp, *weights)


def contrast_outside(grid, small, proj, log_temp, text_down):
    core = lax.axis_index("mp")
    here = lax.axis_index("batch")
    chips, pairs, width = small.shape[1], small.shape[2], small.shape[3] - 128
    half = width // 2
    zs, ys, xs = grid
    slots = jnp.arange(chips, dtype=jnp.int32)
    z, y, x = here // (ys * xs), here // xs % ys, here % xs
    offset = (z + slots // (ys * xs)) % zs * (ys * xs) + (y + slots // xs % ys) % ys * xs + (x + slots % xs) % xs
    slot_of = jnp.argsort(offset)
    total = chips * pairs
    low = small[0, :, :, :width].astype(BF)[slot_of].reshape(total, width)
    counts = small[0, :, :, width:width + 1][slot_of].reshape(total, 1)
    images = small[1, :, :, :width][slot_of].reshape(total, width)
    embed = jnp.concatenate([nn(low, proj[0]), nn(low, proj[1])], 1)
    inv = lax.rsqrt(jnp.sum(embed * embed, 1, keepdims=True) + NORM_EPS)
    text_norm = embed * inv
    scale = jnp.exp(log_temp)
    cosine = three(nt, text_norm, images)
    logits = scale * cosine
    text_lse = jax.nn.logsumexp(logits, 1, keepdims=True)
    image_lse = jax.nn.logsumexp(logits, 0, keepdims=True)
    eye = jnp.eye(total, dtype=F32)
    pair_grad = (jnp.exp(logits - text_lse) + jnp.exp(logits - image_lse) - 2.0 * eye) / (2.0 * total)
    loss = (jnp.sum(text_lse) + jnp.sum(image_lse) - 2.0 * jnp.sum(logits * eye)) / (2.0 * total)
    temp = scale * jnp.sum(pair_grad * cosine)
    grad_norm = scale * three(nn, pair_grad, images)
    grad_embed = ((grad_norm - text_norm * jnp.sum(text_norm * grad_norm, 1, keepdims=True)) * inv).astype(BF)
    grad_half = lax.dynamic_slice_in_dim(grad_embed, core * half, half, 1)
    dh = (nt(grad_embed[:, :half], proj[0]) + nt(grad_embed[:, half:], proj[1])) / counts
    hp = pairs // 2
    ka, kb = slots % ys, slots // (zs * ys)
    kz = slots // ys % zs

    def mine(v, c):
        ky, kx = (jnp.where(c == 0, ka, kb), jnp.where(c == 0, kb, ka)) if ys == xs else (ka, kb)
        chip = ((z + kz) % zs * ys + (y + ky) % ys) * xs + (x + kx) % xs
        w = v.reshape(chips, 2, hp, v.shape[-1])[chip]
        return lax.dynamic_index_in_dim(w, c, 1, keepdims=False).reshape(total // 2, v.shape[-1])

    def grouped(v):
        high, rest = halves(v)
        size = INSIDE // 8
        both = jnp.stack([high.reshape(-1, size, v.shape[1]), rest.reshape(-1, size, v.shape[1])], 1)
        return both.reshape(-1, v.shape[1])

    dm = jnp.concatenate([mine(dh, core), mine(dh, 1 - core)], 0).astype(BF)
    dmw = nt(dm, text_down)
    dmw_other = lax.ppermute(dmw[total // 2:], "mp", [(0, 1), (1, 0)])
    dmw = grouped(jnp.concatenate([dmw[:total // 2], dmw_other], 1))
    return dmw, grouped(mine(dh, core)), dm, low, grad_half, loss, temp


def last_axis(grid):
    zs, ys, xs = grid
    plans = []
    for d in range(1, xs):
        pairs = []
        for z in range(zs):
            for y in range(ys):
                for x in range(xs):
                    for core in range(2):
                        py, px = (y, (x + d) % xs) if core == 0 or ys != xs else ((y + d) % ys, x)
                        pairs.append((((z * ys + py) * xs + px) * 2 + core, ((z * ys + y) * xs + x) * 2 + core))
        plans.append(pairs)
    return plans


def per_device(
    grid, image_patches, text_rows, text_mask, image_qkv, image_out, image_up, image_down, text_gain_one, text_gain_two,
    text_qkv, text_out, text_up, text_down, text_proj, log_temp,
):
    pair_count, length, width = text_rows.shape
    half = width // 2
    hidden = text_up.shape[1]

    def swap(v):
        return lax.ppermute(v, "mp", [(0, 1), (1, 0)])

    patches = jnp.transpose(image_patches, (1, 0, 2)).reshape(-1, width)
    iqkv = jnp.transpose(image_qkv, (1, 0, 2))
    tqkv = jnp.transpose(text_qkv, (1, 0, 2))
    g1, g2 = text_gain_one, text_gain_two
    xg, oqkv, oout, oup, dmw, dh, dm, low, grad_half, loss, temp = front(
        grid, text_rows.reshape(-1, width), text_mask, patches, g1, g2, log_temp.reshape(1, 1),
        (iqkv, image_out, image_up, image_down, tqkv, text_out, text_up, text_down, text_proj),
    )
    own = pair_count // 2 * length
    if dm.ndim == 3:
        dmw, dh, dm, low, grad_half, loss, temp = contrast_outside(grid, dmw, dm, log_temp, text_down)
    weights = (tqkv, text_out, text_up, oqkv, oout, oup)
    total = dm.shape[0] // 2
    near = xg.reshape(-1, width)
    plans = last_axis(grid)
    if dm.shape[0] <= INSIDE:
        far = [lax.ppermute(near, ("batch", "mp"), pairs) for pairs in plans]
        before = None
        groups = [near] + far
        for g, x in enumerate(groups):
            before = text_forward(x, length, g1, g2, dmw, dh, weights, own, len(groups), g, before)
            if g == 0:
                dh1, pick = before[-2:]
        a1t, qkv, p, do, a2t, du, ot, dattn, _, _, gsum, gain2, more, send = before[:14]
        got = swap(send)
        whole = layout(near.shape[0], len(groups))[0] * len(groups)
        qkv_m, qkv_o, small = text_backward(whole, more, near, dh1, pick, g1, qkv, p, do, a1t, tqkv, oqkv)
        qkv_in = swap(qkv_o)
        grad_up, grad_out, grad_down, grad_proj = feed_grads(a2t, du, ot, dattn, got, gsum, dm, low, grad_half)
        qkv_in, grad_up, grad_out, grad_down, grad_proj = lax.optimization_barrier(
            (qkv_in, grad_up, grad_out, grad_down, grad_proj))
        other, at = got, width + half // 2 + gsum.shape[0]
    else:
        size = INSIDE // 8
        groups = total // size

        def one(carry, items):
            sums, first = carry
            g, x, dmw, dh = items
            a1t, qkv, p, do, a2t, du, ot, dattn, _, _, gsum, gain2, more, send, dh1, pick = text_forward(
                x, length, g1, g2, dmw, dh, weights, own)
            qkv_m, qkv_o, small = text_backward(x.shape[0], more, x, dh1, pick, g1, qkv, p, do, a1t, tqkv, oqkv)
            new = (send, gain2, qkv_m, qkv_o, small[own:], nn(a2t, du), nn(ot, dattn))
            return (tuple(x + y for x, y in zip(sums, new)), jnp.where(g == 0, small[:own], first)), gsum

        zero = lambda *shape: jnp.zeros(shape, F32)
        at = width + half // 2 + size
        sums = (zero(width + half // 2 + 96, hidden), zero(8, width), zero(3 * width, half),
                zero(3 * width + 2 * own + 16, half), zero(8, width), zero(width, hidden), zero(half, width))
        split = lambda v: v.reshape(groups, -1, v.shape[-1])
        planes = [near] + [lax.ppermute(near, ("batch", "mp"), pairs) for pairs in plans]
        planes = [jnp.where(x > 0.5 * SENTINEL, SENTINEL, x).astype(BF) for x in planes]
        (sums, first), gsum = lax.scan(
            one, (sums, zero(own, width)),
            (jnp.arange(groups), split(jnp.concatenate(planes, 0)), split(dmw), split(dh)))
        gsum = gsum.reshape(-1, gsum.shape[-1])
        send, gain2, qkv_m, qkv_o, gain1, up_m, out_m = sums
        small = jnp.concatenate([first, gain1], 0)
        qkv_o = jnp.concatenate([qkv_o[:3 * width], small[:, :half], small[:, half:]], 0)
        qkv_in, got = swap(qkv_o), swap(send)
        grad_up = up_m + got[:width]
        folded = got[width:width + half // 2]
        grad_out = out_m + jnp.concatenate([folded[:, :width], folded[:, width:]], 0)
        high, rest = halves(jnp.concatenate([gsum[:, :hidden], swap(gsum[:, hidden:])], 0))
        grad_down = tn(high, dm) + tn(rest, dm)
        grad_proj = tn(low, grad_half)
        other = got
    grad_qkv, grad_rows, gain1, gain2, loss, temp = finish(
        qkv_m, qkv_in, small, gain2, other, at, loss.reshape(1, 1), temp.reshape(1, 1))
    return (loss.reshape(()), grad_rows.reshape(pair_count, length, width), gain1, gain2,
            jnp.transpose(grad_qkv, (1, 0, 2)), grad_out, grad_up, grad_down, grad_proj, temp.reshape(()))


def solution(mesh):
    return jax.shard_map(
        functools.partial(per_device, chip_grid(mesh)),
        mesh=mesh,
        in_specs=(
            P("batch", None, None), P("batch", None, None), P("batch", None), P(None, None, "mp"), P("mp", None),
            P(None, "mp"), P("mp", None), P(), P(), P(None, None, "mp"), P("mp", None), P(None, "mp"), P("mp", None),
            P(None, "mp"), P(),
        ),
        out_specs=(
            P(), P("batch", None, None), P("mp"), P("mp"), P(None, None, "mp"), P("mp", None), P(None, "mp"),
            P("mp", None), P(None, "mp"), P(),
        ),
        check_vma=False,
    )
```
